32 devices in a mesh: img: 8 (over z, y), band: 4 (over x, core).
Axes of the slice: x: 2, y: 2, z: 4, core: 2. Of those that a mesh axis runs over, the one named last changes fastest.
Arguments:
- tokens: bfloat16 [64, 256, 768], P('img', 'band'), may hold values from -6 to 6
- cotangent: bfloat16 [64, 256, 768], P('img', 'band'), may hold values from -6 to 6
- grid_side: int32 [64], P('img'), may hold values from 10 to 16, as said below
- visible: int32 [64, 256], P('img'), may hold values from 0 to 1, as said below
- w_qkv: bfloat16 [768, 2304], replicated, may hold values from -0.21875 to 0.21875
- q_bias: float32 [768], replicated, may hold values from -3 to 3
- v_bias: float32 [768], replicated, may hold values from -3 to 3
- w_out: bfloat16 [768, 768], replicated, may hold values from -0.625 to 0.625
- b_out: float32 [768], replicated, may hold values from -2 to 2
- ln1_gain: float32 [768], replicated, may hold values from 0.1 to 1.9
- ln1_shift: float32 [768], replicated, may hold values from -2 to 2
- ln2_gain: float32 [768], replicated, may hold values from 0.1 to 1.9
- ln2_shift: float32 [768], replicated, may hold values from -2 to 2
- w_up: bfloat16 [768, 3072], replicated, may hold values from -0.21875 to 0.21875
- b_up: float32 [3072], replicated, may hold values from -3 to 3
- w_down: bfloat16 [3072, 768], replicated, may hold values from -0.15625 to 0.15625
- b_down: float32 [768], replicated, may hold values from -2 to 2
- scale_attn: float32 [768], replicated, may hold values from 0.3 to 1
- scale_mlp: float32 [768], replicated, may hold values from 0.3 to 1
Outputs:
- output: bfloat16 [64, 256, 768], P('img', 'band')
- input_grad: bfloat16 [64, 256, 768], P('img', 'band')
- grad_w_qkv: float32 [768, 2304], P('img')
- grad_q_bias: float32 [768], P('img')
- grad_v_bias: float32 [768], P('img')
- grad_w_out: float32 [768, 768], P('img')
- grad_b_out: float32 [768], P('img')
- grad_ln1_gain: float32 [768], P('img')
- grad_ln1_shift: float32 [768], P('img')
- grad_ln2_gain: float32 [768], P('img')
- grad_ln2_shift: float32 [768], P('img')
- grad_w_up: float32 [768, 3072], P('img')
- grad_b_up: float32 [3072], P('img')
- grad_w_down: float32 [3072, 768], P('img')
- grad_b_down: float32 [768], P('img')
- grad_scale_attn: float32 [768], P('img')
- grad_scale_mlp: float32 [768], P('img')
The draws below stay inside these ranges and needn't reach their ends.
Inputs may be any that keep to these rules, and one draw needn't show every extreme that they name: `grid_side`: each grid side is 10, 14 or 16; in each aligned block of 8 images at least one has side 16. Slot 0 of every image is visible.
All inputs are finite; a program needn't handle non-finite values.
Results may differ from the reference program's by a relative error of at most 0.015.
Values may be sent and summed in bfloat16 or wider, within the bound.
No kernel may reach another device: no remote copies, remote signals or barrier semaphores. Data moves between devices by JAX's collectives and lax.ppermute only.
A program may use at most 128 MiB of HBM per device.

```python
import jax
import jax.numpy as jnp
from jax import lax

D = 768
HEADS = 12
HEAD = 64
FF = 3072
GRID = 16
IMG_DEV = 8
SLOTS = 256
IMAGES = 64
N_IMG = 8


def draw_grid_side(key, part):
    key = jax.random.fold_in(key, 11)
    first_key, second_key = jax.random.split(key)
    side_table = jnp.array([GRID * 5 // 8, GRID * 7 // 8, GRID], dtype=jnp.int32)
    picked = jax.random.randint(first_key, (IMAGES,), 0, 3)
    sides = side_table[picked]
    blocks = sides.reshape(IMAGES // IMG_DEV, IMG_DEV)
    chosen = jax.random.randint(second_key, (IMAGES // IMG_DEV,), 0, IMG_DEV)
    position = jnp.arange(IMG_DEV, dtype=jnp.int32)
    blocks = jnp.where(position[None, :] == chosen[:, None], GRID, blocks)
    return blocks.reshape(IMAGES).astype(jnp.int32)


def draw_visible(key, part):
    key = jax.random.fold_in(key, 23)
    flags = jax.random.randint(key, (IMAGES, SLOTS), 0, 2)
    return flags.at[:, 0].set(1).astype(jnp.int32)


def levels(key, extent, shards, least, largest):
    level = 1.0
    for axis_at, blocks in shards:
        draws = jax.random.uniform(jax.random.fold_in(jax.random.fold_in(key, 6), axis_at), (blocks,), jnp.float32, least / len(shards), largest / len(shards))
        level = level * jnp.repeat(jnp.exp(draws), extent[axis_at] // blocks).reshape((-1,) + (1,) * (len(extent) - 1 - axis_at))
    return level


def noise(key, shape, scale, most, pieces=(), kind=jnp.bfloat16):
    values = scale * jax.random.normal(key, shape, jnp.float32)
    if pieces:
        values = values * levels(key, shape, pieces, -0.22, 0.18)
    return jnp.clip(values, -most, most).astype(kind)


def setup_inputs(seed: int = 0) -> dict:
    splits = jax.random.split(jax.random.key(seed), 20)
    tokens = noise(splits[0], (IMAGES, SLOTS, D), 1.0, 6.0, ((0, 8), (1, 4)))
    cotangent = noise(splits[1], (IMAGES, SLOTS, D), 1.0, 6.0, ((0, 8), (1, 4)))
    grid_side = draw_grid_side(jax.random.fold_in(splits[19], 71), 0)
    visible = draw_visible(jax.random.fold_in(splits[19], 71), 0)
    w_qkv = noise(splits[4], (D, 3 * D), D ** -0.5, 0.21875)
    q_bias = noise(splits[5], (D,), 0.5, 3.0, (), jnp.float32)
    v_bias = noise(splits[6], (D,), 0.5, 3.0, (), jnp.float32)
    w_out = noise(splits[7], (D, D), (D // 8) ** -0.5, 0.625)
    b_out = noise(splits[8], (D,), 0.3, 2.0, (), jnp.float32)
    ln1_gain = jnp.clip(1.0 + 0.18 * jax.random.normal(splits[9], (D,), jnp.float32), 0.1, 1.9)
    ln1_shift = noise(splits[10], (D,), 0.3, 2.0, (), jnp.float32)
    ln2_gain = jnp.clip(1.0 + 0.18 * jax.random.normal(splits[11], (D,), jnp.float32), 0.1, 1.9)
    ln2_shift = noise(splits[12], (D,), 0.3, 2.0, (), jnp.float32)
    w_up = noise(splits[13], (D, FF), D ** -0.5, 0.21875)
    b_up = noise(splits[14], (FF,), 0.5, 3.0, (), jnp.float32)
    w_down = noise(splits[15], (FF, D), (FF // 2) ** -0.5, 0.15625)
    b_down = noise(splits[16], (D,), 0.3, 2.0, (), jnp.float32)
    scale_attn = jnp.clip(jax.random.uniform(splits[17], (D,), jnp.float32, 0.3, 1.0), 0.3, 1.0)
    scale_mlp = jnp.clip(jax.random.uniform(splits[18], (D,), jnp.float32, 0.3, 1.0), 0.3, 1.0)
    return {"tokens": tokens, "cotangent": cotangent, "grid_side": grid_side, "visible": visible, "w_qkv": w_qkv, "q_bias": q_bias, "v_bias": v_bias, "w_out": w_out, "b_out": b_out, "ln1_gain": ln1_gain, "ln1_shift": ln1_shift, "ln2_gain": ln2_gain, "ln2_shift": ln2_shift, "w_up": w_up, "b_up": b_up, "w_down": w_down, "b_down": b_down, "scale_attn": scale_attn, "scale_mlp": scale_mlp}


@jax.custom_vjp
def low(v):
    return lax.optimization_barrier(v.astype(jnp.bfloat16)).astype(jnp.float32)

@jax.custom_vjp
def low_back(v):
    return v

def low_keep(v):
    return (low(v), None)

def low_pass(kept, grad):
    return (grad,)

def back_keep(v):
    return (v, None)

def back_low(kept, grad):
    return (low(grad),)
low.defvjp(low_keep, low_pass)
low_back.defvjp(back_keep, back_low)
NEG_BIG = -1e+30
EPSILON = 1e-06
HIGHEST = lax.Precision.HIGHEST

def layer_norm(entry, gain, shift):
    center = entry - lax.optimization_barrier(jnp.mean(entry, -1, keepdims=True))
    spread = lax.optimization_barrier(jnp.mean(center * center, -1, keepdims=True))
    return center * lax.rsqrt(spread + EPSILON) * gain + shift

def gelu_exact(entry):
    return jax.nn.gelu(entry, approximate=False)

def slot_mask(sides, count, first):
    index = first + jnp.arange(count, dtype=jnp.int32)
    row_pos = index // GRID
    col_pos = index % GRID
    return (row_pos[None, :] < sides[:, None]) & (col_pos[None, :] < sides[:, None])

def block_forward(block, params, key_ok):
    w_qkv, q_bias, v_bias, w_out, b_out, ln1_gain, ln1_shift, ln2_gain, ln2_shift, w_up, b_up, w_down, b_down, scale_attn, scale_mlp = params
    count = block.shape[0]
    normed = low(layer_norm(block, ln1_gain, ln1_shift))
    projected = jnp.einsum('nsd,de->nse', normed, w_qkv, precision=HIGHEST)
    queries = low(low_back(projected[..., :D] + q_bias)).reshape(count, SLOTS, HEADS, HEAD)
    key_rows = low(low_back(projected[..., D:2 * D])).reshape(count, SLOTS, HEADS, HEAD)
    values = low(low_back(projected[..., 2 * D:] + v_bias)).reshape(count, SLOTS, HEADS, HEAD)
    scores = jnp.einsum('nqhe,nkhe->nhqk', queries, key_rows, precision=HIGHEST) * HEAD ** (-0.5)
    scores = low_back(jnp.where(key_ok[:, None, None, :], scores, NEG_BIG))
    weights = low(jax.nn.softmax(scores, axis=-1))
    attended = jnp.einsum('nhqk,nkhe->nqhe', weights, values, precision=HIGHEST).reshape(count, SLOTS, D)
    attended = low(low_back(attended))
    branch_attn = low_back(jnp.einsum('nsd,de->nse', attended, w_out, precision=HIGHEST) + b_out)
    middle = block + scale_attn * branch_attn
    normed_two = low(layer_norm(middle, ln2_gain, ln2_shift))
    hidden_pre = low_back(jnp.einsum('nsd,df->nsf', normed_two, w_up, precision=HIGHEST) + b_up)
    hidden = low(gelu_exact(hidden_pre))
    branch_mlp = low_back(jnp.einsum('nsf,fd->nsd', hidden, w_down, precision=HIGHEST) + b_down)
    return middle + scale_mlp * branch_mlp

def reference(tokens, cotangent, grid_side, visible, w_qkv, q_bias, v_bias, w_out, b_out, ln1_gain, ln1_shift, ln2_gain, ln2_shift, w_up, b_up, w_down, b_down, scale_attn, scale_mlp):
    params = tuple((weight.astype(jnp.float32) for weight in (w_qkv, q_bias, v_bias, w_out, b_out, ln1_gain, ln1_shift, ln2_gain, ln2_shift, w_up, b_up, w_down, b_down, scale_attn, scale_mlp)))
    layout = (N_IMG, IMG_DEV, SLOTS, D)

    def step(running, items):
        block, grad_out, sides, seen = items
        valid = slot_mask(sides, SLOTS, 0)
        key_ok = valid & (seen == 1)
        valid_f = valid.astype(jnp.float32)[..., None]

        def forward(entry, weights):
            return valid_f * block_forward(entry, weights, key_ok)
        result, pullback = jax.vjp(forward, block.astype(jnp.float32), params)
        grad_in, grad_params = pullback(grad_out.astype(jnp.float32))
        running = jax.tree.map(jnp.add, running, grad_params)
        return (running, (result.astype(jnp.bfloat16), grad_in.astype(jnp.bfloat16)))
    zeros = jax.tree.map(jnp.zeros_like, params)
    running, (results, grads_in) = lax.scan(step, zeros, (tokens.reshape(layout), cotangent.reshape(layout), grid_side.reshape(N_IMG, IMG_DEV), visible.reshape(N_IMG, IMG_DEV, SLOTS)))
    output = results.reshape(IMAGES, SLOTS, D)
    input_grad = grads_in.reshape(IMAGES, SLOTS, D)
    grad_w_qkv, grad_q_bias, grad_v_bias, grad_w_out, grad_b_out, grad_ln1_gain, grad_ln1_shift, grad_ln2_gain, grad_ln2_shift, grad_w_up, grad_b_up, grad_w_down, grad_b_down, grad_scale_attn, grad_scale_mlp = running
    return (output, input_grad, grad_w_qkv, grad_q_bias, grad_v_bias, grad_w_out, grad_b_out, grad_ln1_gain, grad_ln1_shift, grad_ln2_gain, grad_ln2_shift, grad_w_up, grad_b_up, grad_w_down, grad_b_down, grad_scale_attn, grad_scale_mlp)
```

```python
import jax
import jax.numpy as jnp
from jax import lax
from jax.sharding import PartitionSpec as P

HEAD = 64
GRID = 16
NEG_BIG = -1e30
EPSILON = 1e-06
F32 = jnp.float32
BF16 = jnp.bfloat16


def swap(entry, axis, mask):
    size = lax.axis_size(axis)
    return lax.ppermute(entry, axis, [(i, i ^ mask) for i in range(size)])


def norm_parts(entry):
    center = entry - jnp.mean(entry, -1, keepdims=True)
    spread = jnp.mean(center * center, -1, keepdims=True)
    inverse = lax.rsqrt(spread + EPSILON)
    return center * inverse, inverse


def norm_back(grad, gain, xhat, inverse):
    scaled = grad * gain
    inner = scaled - jnp.mean(scaled, -1, keepdims=True)
    inner = inner - xhat * jnp.mean(scaled * xhat, -1, keepdims=True)
    return inner * inverse, jnp.sum(grad * xhat, 0), jnp.sum(grad, 0)


def dot(left, right, dims):
    return lax.dot_general(left, right, (dims, ((), ())), preferred_element_type=F32)


def local_layer(x, cot, valid, key_ok, params):
    (w_qkv, q_bias, v_bias, w_out, b_out, g1, c1, g2, c2, w_up, b_up, w_down, b_down, s_attn, s_mlp) = params
    rows, width = x.shape
    images, slots = key_ok.shape
    heads = width // HEAD
    inputs = x.astype(F32)
    xhat1, inv1 = norm_parts(inputs)
    normed = (xhat1 * g1 + c1).astype(BF16)
    proj = dot(normed, w_qkv, ((1,), (0,)))
    q = (proj[:, :width] + q_bias).astype(BF16)
    k = proj[:, width : 2 * width].astype(BF16)
    v = (proj[:, 2 * width :] + v_bias).astype(BF16)

    def split(entry):
        return entry.reshape(images, slots, heads, HEAD)

    q, k, v = split(q), split(k), split(v)
    scores = jnp.einsum("nqhe,nkhe->nhqk", q, k, preferred_element_type=F32) * HEAD**-0.5
    scores = jnp.where(key_ok[:, None, None, :], scores, NEG_BIG)
    probs = jax.nn.softmax(scores, axis=-1)
    weights = probs.astype(BF16)
    attended = jnp.einsum("nhqk,nkhe->nqhe", weights, v, preferred_element_type=F32)
    attended = attended.astype(BF16).reshape(rows, width)
    branch = dot(attended, w_out, ((1,), (0,))) + b_out
    middle = inputs + s_attn * branch
    xhat2, inv2 = norm_parts(middle)
    normed2 = (xhat2 * g2 + c2).astype(BF16)
    pre = dot(normed2, w_up, ((1,), (0,))) + b_up
    hidden, pull = jax.vjp(lambda e: jax.nn.gelu(e, approximate=False), pre)
    hidden = hidden.astype(BF16)
    top = valid * cot.astype(F32)
    g_mlp = (s_mlp * top).astype(BF16)
    d_down_t = (g_mlp, hidden)
    d_pre = pull(dot(g_mlp, w_down, ((1,), (1,))))[0].astype(BF16)
    d_up = (normed2, d_pre)
    branch_mlp = dot(hidden, w_down, ((1,), (0,))) + b_down
    out = (valid * (middle + s_mlp * branch_mlp)).astype(BF16)
    d_norm2 = dot(d_pre, w_up, ((1,), (1,)))
    back2, d_g2, d_c2 = norm_back(d_norm2, g2, xhat2, inv2)
    d_middle = top + back2
    d_branch = (s_attn * d_middle).astype(BF16)
    d_wout = (attended, d_branch)
    d_att = split(dot(d_branch, w_out, ((1,), (1,))).astype(BF16))
    d_weights = jnp.einsum("nqhe,nkhe->nhqk", d_att, v, preferred_element_type=F32)
    d_scores = probs * (d_weights - jnp.sum(probs * d_weights, -1, keepdims=True))
    d_scores = d_scores.astype(BF16)
    d_q = jnp.einsum("nhqk,nkhe->nqhe", d_scores, k, preferred_element_type=F32) * HEAD**-0.5
    d_k = jnp.einsum("nhqk,nqhe->nkhe", d_scores, q, preferred_element_type=F32) * HEAD**-0.5
    d_v = jnp.einsum("nhqk,nqhe->nkhe", weights, d_att, preferred_element_type=F32)
    d_proj = jnp.concatenate([e.astype(BF16).reshape(rows, width) for e in (d_q, d_k, d_v)], -1)
    d_qkv = (normed, d_proj)
    d_norm1 = dot(d_proj, w_qkv, ((1,), (1,)))
    back1, d_g1, d_c1 = norm_back(d_norm1, g1, xhat1, inv1)
    grad_in = (d_middle + back1).astype(BF16)

    def total(entry):
        return jnp.sum(entry.astype(F32), 0)

    small = (
        total(d_proj[:, :width]),
        total(d_proj[:, 2 * width :]),
        total(d_branch),
        d_g1,
        d_c1,
        d_g2,
        d_c2,
        total(d_pre),
        total(g_mlp),
        total(d_middle * branch),
        total(top * branch_mlp),
    )
    return out, grad_in, d_down_t, d_up, d_wout, d_qkv, small


def halve(entry, axis, bit):
    got = swap(entry[1], axis, 1 << bit)
    return (entry[0].astype(F32) + got.astype(F32)).astype(BF16)


def both(entry, axis, bit):
    return (entry.astype(F32) + swap(entry, axis, 1 << bit).astype(F32)).astype(BF16)


def join(entry, axis, bit, dim):
    got = swap(entry, axis, 1 << bit)
    high = (lax.axis_index(axis) >> bit) & 1
    first = jnp.where(high == 1, got, entry)
    second = jnp.where(high == 1, entry, got)
    return jnp.concatenate([first, second], dim)


def scatter(blocks, order):
    r, c = blocks.shape[1:]
    if order == "yzx":
        b = blocks.reshape(2, 2, 2, r, c)
        b = halve(jnp.moveaxis(b, 2, 0), "img", 0)
        b = halve(jnp.moveaxis(b, 1, 0), "img", 1)
        b = halve(b, "img", 2)
        return both(b, "band", 1)
    b = blocks.reshape(2, 2, 2, 2, r // 2, c)
    high = (lax.axis_index("band") >> 1) & 1
    mine = lax.dynamic_index_in_dim(b, high, 3, False)
    other = lax.dynamic_index_in_dim(b, 1 - high, 3, False)
    b = (mine.astype(F32) + swap(other, "band", 2).astype(F32)).astype(BF16)
    b = halve(jnp.moveaxis(b, 2, 0), "img", 0)
    b = halve(jnp.moveaxis(b, 1, 0), "img", 1)
    b = halve(b, "img", 2)
    return join(b, "band", 1, 0)


def reduce_fast(left, right, width_blocks, col_type, cut):
    me = lax.axis_index("img")
    core = lax.axis_index("band") & 1
    perm = jnp.arange(8) ^ me
    if col_type:
        half = left.shape[1] // 2
        keep_l = lax.dynamic_slice_in_dim(left, core * half, half, 1)
        send_l = lax.dynamic_slice_in_dim(left, (1 - core) * half, half, 1)

        def make(l):
            g = dot(l, right, ((0,), (0,))).astype(BF16)
            return g.reshape(half, 8, -1).transpose(1, 0, 2)[perm]

        send, keep = make(send_l), make(keep_l)
    else:
        half = right.shape[1] // 2
        keep_r = lax.dynamic_slice_in_dim(right, core * half, half, 1)
        send_r = lax.dynamic_slice_in_dim(right, (1 - core) * half, half, 1)

        def make(r):
            g = dot(left, r, ((0,), (0,))).astype(BF16)
            return g.reshape(8, -1, half)[perm]

        send, keep = make(send_r), make(keep_r)
    got = swap(send, "band", 1)
    blocks = (keep.astype(F32) + got.astype(F32)).astype(BF16)
    if cut:
        if col_type:
            parts = [scatter(blocks[:, :cut], "yzx"), scatter(blocks[:, cut:], "xyz")]
            mine = jnp.concatenate(parts, 0)
        else:
            parts = [scatter(blocks[:, :, :cut], "yzx"), scatter(blocks[:, :, cut:], "xyz")]
            mine = jnp.concatenate(parts, 1)
    else:
        mine = scatter(blocks, "yzx")
    whole = join(mine, "band", 0, 0 if col_type else 1).astype(F32)
    return whole.T if col_type else whole


def reduce_plain(left, right, scale=None):
    grad = dot(left, right, ((0,), (0,)))
    part = lax.psum_scatter(grad, "img", scatter_dimension=0, tiled=True)
    return lax.psum(part.astype(BF16), "band").astype(F32)


def shards(
    tokens, cotangent, grid_side, visible, w_qkv, q_bias, v_bias, w_out, b_out, ln1_gain, ln1_shift,
    ln2_gain, ln2_shift, w_up, b_up, w_down, b_down, scale_attn, scale_mlp,
):
    images, band_rows, width = tokens.shape
    bands = lax.axis_size("band")
    band = lax.axis_index("band")
    mine = images // bands
    slots = bands * band_rows

    def to_images(entry):
        parts = []
        for q in range(bands):
            piece = lax.dynamic_slice_in_dim(entry, mine * (band ^ q), mine, 0)
            parts.append(swap(piece, "band", q) if q else piece)
        return jnp.concatenate(parts, 1).reshape(mine * slots, width)

    def to_bands(entry):
        entry = entry.reshape(mine, bands, band_rows, width)
        result = jnp.zeros((images, band_rows, width), entry.dtype)
        for q in range(bands):
            piece = entry[:, q]
            if q:
                piece = swap(piece, "band", q)
            result = lax.dynamic_update_slice_in_dim(result, piece, mine * (band ^ q), 0)
        return result

    sides = lax.dynamic_slice_in_dim(grid_side, band * mine, mine, 0)
    seen = lax.dynamic_slice_in_dim(visible, band * mine, mine, 0)
    order = jnp.arange(bands, dtype=jnp.int32) ^ band
    index = (order[:, None] * band_rows + jnp.arange(band_rows, dtype=jnp.int32)[None, :]).reshape(-1)
    inside = (index[None, :] // GRID < sides[:, None]) & (index[None, :] % GRID < sides[:, None])
    seen = seen.reshape(mine, bands, band_rows)[:, order].reshape(mine, slots)
    key_ok = inside & (seen == 1)
    valid = inside.astype(F32).reshape(mine * slots, 1)
    params = (
        w_qkv, q_bias, v_bias, w_out, b_out, ln1_gain, ln1_shift, ln2_gain, ln2_shift, w_up, b_up, w_down, b_down,
        scale_attn, scale_mlp,
    )
    x = to_images(tokens)
    cot = to_images(cotangent)
    out, grad_in, d_down, d_up, d_wout, d_qkv, small = local_layer(x, cot, valid, key_ok, params)
    output = to_bands(out)
    input_grad = to_bands(grad_in)
    if lax.axis_size("img") == 8 and bands == 4:
        grad_w_down = reduce_fast(d_down[0], d_down[1], 8, True, 224)
        grad_w_up = reduce_fast(*d_up, 8, False, 7 * 128)
        grad_w_out = reduce_fast(*d_wout, 8, False, 0)
        grad_w_qkv = reduce_fast(*d_qkv, 8, False, 5 * 128)
    else:
        grad_w_down = reduce_plain(d_down[1], d_down[0])
        grad_w_up = reduce_plain(*d_up)
        grad_w_out = reduce_plain(*d_wout)
        grad_w_qkv = reduce_plain(*d_qkv)
    small = lax.psum(jnp.concatenate(small), ("img", "band"))
    img = lax.axis_index("img")
    shares = []
    at = 0
    for size in (width,) * 7 + (w_up.shape[1],) + (width,) * 3:
        part = size // lax.axis_size("img")
        shares.append(lax.dynamic_slice_in_dim(small, at + img * part, part, 0))
        at += size
    (s_qb, s_vb, s_bo, s_g1, s_c1, s_g2, s_c2, s_bu, s_bd, s_sa, s_sm) = shares
    return (
        output, input_grad, grad_w_qkv, s_qb, s_vb, grad_w_out, s_bo, s_g1, s_c1, s_g2, s_c2, grad_w_up, s_bu,
        grad_w_down, s_bd, s_sa, s_sm,
    )


def solution(mesh):
    cut = P("img", "band", None)
    in_specs = (cut, cut, P("img"), P("img", None)) + (P(),) * 15
    row, vec = P("img", None), P("img")
    out_specs = (cut, cut, row, vec, vec, row, vec, vec, vec, vec, vec, row, vec, row, vec, vec, vec)
    return jax.shard_map(shards, mesh=mesh, in_specs=in_specs, out_specs=out_specs, check_vma=False)
```

```python
import functools

import jax
import jax.numpy as jnp
from jax import lax
from jax.experimental import pallas as pl
from jax.experimental.pallas import tpu as pltpu
from jax.sharding import PartitionSpec as P

HEAD = 64
GRID = 16
NEG_BIG = -1e30
EPSILON = 1e-06
F32 = jnp.float32
BF16 = jnp.bfloat16
VM = pl.BlockSpec(memory_space=pltpu.VMEM)
SM = pl.BlockSpec(memory_space=pltpu.SMEM)
NN, NT, TN = ((1,), (0,)), ((1,), (1,)), ((0,), (0,))
Q_BIAS, V_BIAS, B_OUT, G1, C1, G2, C2, B_DOWN, S_ATTN, S_MLP, B_UP = range(11)


def dot(left, right, dims=NN):
    return lax.dot_general(left, right, (dims, ((), ())), preferred_element_type=F32)


def struct(*shape, dtype=BF16):
    return jax.ShapeDtypeStruct(shape, dtype)


def call(kernel, outs, place, *args, scratch=(), limit=24, flops=10**9):
    return pl.pallas_call(
        kernel,
        out_shape=outs,
        in_specs=[SM] + [VM] * len(args),
        out_specs=[VM] * len(outs),
        scratch_shapes=list(scratch),
        compiler_params=pltpu.CompilerParams(vmem_limit_bytes=limit * 2**20),
        cost_estimate=pl.CostEstimate(flops=flops, bytes_accessed=1 << 20, transcendentals=0),
    )(place, *args)


def norm_parts(entry):
    center = entry - jnp.mean(entry, -1, keepdims=True)
    spread = jnp.mean(center * center, -1, keepdims=True)
    inverse = lax.rsqrt(spread + EPSILON)
    return center * inverse, inverse


def norm_back(grad, gain, xhat, inverse):
    scaled = grad * gain
    inner = scaled - jnp.mean(scaled, -1, keepdims=True)
    return (inner - xhat * jnp.mean(scaled * xhat, -1, keepdims=True)) * inverse


def normal_parts(entry):
    size = jnp.abs(entry)
    base = 1.0 + 0.2316418882 * size
    t = pltpu.reciprocal(base, approx=True)
    t = t * (2.0 - base * t)
    bell = jnp.exp2((-0.5 * 1.4426950408889634) * (entry * entry))
    poly = t * (0.127414796 + t * (-0.142248368 + t * (0.7107068705 + t * (-0.7265760135 + t * 0.5307027145))))
    tail = poly * bell
    return jnp.where(entry < 0, tail, 1.0 - tail), 0.3989422804014327 * bell


def pick(entry, head):
    lane = lax.broadcasted_iota(jnp.int32, entry.shape, 1)
    return jnp.where((lane < HEAD) if head == 0 else (lane >= HEAD), entry, jnp.zeros_like(entry))


def whole_images(place, local, got):
    mine, band_rows, width = got[0].shape
    own = local[pl.ds(place[0] * mine, mine)]
    parts = [own] + [g[...] for g in got]
    return jnp.concatenate([p[:, None] for p in parts], 1).reshape(mine * len(parts) * band_rows, width)


def forward_kernel(place, local, *refs, bands):
    got = refs[: bands - 1]
    (bias, vec, w_qkv, w_out, w_up,
     x_o, normed_o, q_o, k_o, v_o, p_o, att_o, branch_o, mid_o, normed2_o, hidden_o, slope_o) = refs[bands - 1 :]
    mine = got[0].shape[0]
    width = x_o.shape[1]
    rows = x_o.shape[0]
    slots = rows // mine
    x_o[...] = whole_images(place, local, got)
    xhat, _ = norm_parts(x_o[...].astype(F32))
    normed_o[...] = (xhat * vec[G1 : G1 + 1] + vec[C1 : C1 + 1]).astype(BF16)
    normed = normed_o[...]
    queries = (dot(normed, w_qkv[:, :width]) + vec[Q_BIAS : Q_BIAS + 1]).astype(BF16)
    q_o[...] = (queries.astype(F32) * HEAD**-0.5).astype(BF16)
    k_o[...] = dot(normed, w_qkv[:, width : 2 * width]).astype(BF16)
    v_o[...] = (dot(normed, w_qkv[:, 2 * width :]) + vec[V_BIAS : V_BIAS + 1]).astype(BF16)
    pairs = width // (2 * HEAD)
    for n in range(mine):
        rs = slice(n * slots, (n + 1) * slots)
        mask = jnp.broadcast_to(bias[rs, :], (slots, slots))
        for pr in range(pairs):
            cs = slice(pr * 2 * HEAD, (pr + 1) * 2 * HEAD)
            q, k, v = q_o[rs, cs], k_o[rs, cs], v_o[rs, cs]
            total = None
            for h in range(2):
                s = dot(pick(k, h), q, NT) + mask
                e = jnp.exp(s - jnp.max(s, 0, keepdims=True))
                p = (e * (1.0 / jnp.sum(e, 0, keepdims=True))).astype(BF16)
                p_o[(n * pairs + pr) * 2 + h] = p
                part = dot(p, pick(v, h), TN)
                total = part if total is None else total + part
            att_o[rs, cs] = total.astype(BF16)
    branch = dot(att_o[...], w_out[...]) + vec[B_OUT : B_OUT + 1]
    branch_o[...] = branch.astype(BF16)
    middle = x_o[...].astype(F32) + vec[S_ATTN : S_ATTN + 1] * branch
    mid_o[...] = middle
    xhat2, _ = norm_parts(middle)
    normed2_o[...] = (xhat2 * vec[G2 : G2 + 1] + vec[C2 : C2 + 1]).astype(BF16)
    for j in range(hidden_o.shape[1] // width):
        js = slice(j * width, (j + 1) * width)
        pre = dot(normed2_o[...], w_up[:, js]) + vec[B_UP + j : B_UP + j + 1]
        cdf, pdf = normal_parts(pre)
        hidden_o[:, js] = (pre * cdf).astype(BF16)
        slope_o[:, js] = (cdf + pre * pdf).astype(BF16)


def forward(place, tok, got, bias, vec, w_qkv, w_out, w_up):
    mine, band_rows, width = got[0].shape
    bands = len(got) + 1
    slots = bands * band_rows
    rows = mine * slots
    row, wide = struct(rows, width), struct(rows, w_up.shape[1])
    p = struct(mine * width // HEAD, slots, slots)
    outs = [row, row, row, row, row, p, row, row, struct(rows, width, dtype=F32), row, wide, wide]
    return call(functools.partial(forward_kernel, bands=bands), outs, place, tok, *got, bias, vec, w_qkv, w_out, w_up)


def sums(entry):
    return jnp.sum(entry, 0, keepdims=True)


def down_kernel(place, local, *refs, bands):
    got = refs[: bands - 1]
    valid, vec, hidden, top_o, gm_o, send_o, keep_o, sum_o = refs[bands - 1 :]
    top = valid[...] * whole_images(place, local, got).astype(F32)
    top_o[...] = top.astype(BF16)
    gm_o[...] = (vec[S_MLP : S_MLP + 1] * top).astype(BF16)
    sum_o[...] = sums(gm_o[...].astype(F32))
    blocks, half, _ = send_o.shape
    first = place[1] == 0
    for p in range(blocks):
        at = pl.multiple_of((p ^ place[2]) * (2 * half), 128)
        grad = dot(hidden[:, pl.ds(at, 2 * half)], gm_o[...], TN).astype(BF16)
        keep_o[p] = jnp.where(first, grad[:half], grad[half:])
        send_o[p] = jnp.where(first, grad[half:], grad[:half])


def down(place, cot, got, valid, vec, hidden, blocks):
    rows, ff = hidden.shape
    width = cot.shape[2]
    part = struct(blocks, ff // blocks // 2, width)
    outs = [struct(rows, width), struct(rows, width), part, part, struct(1, width, dtype=F32)]
    return call(functools.partial(down_kernel, bands=len(got) + 1), outs, place, cot, *got, valid, vec, hidden)


def cut_rows(place, left, right, send_o, keep_o, at_o, tile):
    blocks, rows, _ = send_o.shape
    half = right.shape[1] // 2
    for target, core in ((send_o, 1 - place[1]), (keep_o, place[1])):
        for j in range(half // tile):
            at = pl.multiple_of(core * half + j * tile, 128)
            grad = dot(left[...], right[:, pl.ds(at, tile)], TN).astype(BF16)
            for i in range(blocks):
                target[i ^ place[2], :, at_o + j * tile : at_o + (j + 1) * tile] = grad[i * rows : (i + 1) * rows]


def up_kernel(place, gm, slope, w_down, normed2, dpre_o, send_o, keep_o, sum_o):
    ff = slope.shape[1]
    tile = gm.shape[1]
    for j in range(ff // tile):
        js = slice(j * tile, (j + 1) * tile)
        grad = (dot(gm[...], w_down[js, :], NT) * slope[:, js].astype(F32)).astype(BF16)
        dpre_o[:, js] = grad
        sum_o[j : j + 1] = sums(grad.astype(F32))
    cut_rows(place, normed2, dpre_o, send_o, keep_o, 0, ff // 4)


def up(place, gm, slope, w_down, normed2, blocks):
    rows, ff = slope.shape
    width = gm.shape[1]
    part = struct(blocks, width // blocks, ff // 2)
    outs = [struct(rows, ff), part, part, struct(ff // width, width, dtype=F32)]
    return call(up_kernel, outs, place, gm, slope, w_down, normed2)


def out_kernel(place, dpre, w_up, mid, top, vec, branch, att, w_out, dmid_o, datt_o, send_o, keep_o, sum_o, db_s):
    grad = dot(dpre[...], w_up[...], NT)
    xhat, inverse = norm_parts(mid[...])
    sum_o[0:1] = sums(grad * xhat)
    sum_o[1:2] = sums(grad)
    dmid = top[...].astype(F32) + norm_back(grad, vec[G2 : G2 + 1], xhat, inverse)
    dmid_o[...] = dmid
    sum_o[2:3] = sums(dmid * branch[...].astype(F32))
    db_s[...] = (vec[S_ATTN : S_ATTN + 1] * dmid).astype(BF16)
    sum_o[3:4] = sums(db_s[...].astype(F32))
    datt_o[...] = dot(db_s[...], w_out[...], NT).astype(BF16)
    cut_rows(place, att, db_s, send_o, keep_o, 0, db_s.shape[1] // 2)


def attention_out(place, dpre, w_up, mid, top, vec, branch, att, w_out, blocks):
    rows, width = mid.shape
    part = struct(blocks, width // blocks, width // 2)
    outs = [struct(rows, width, dtype=F32), struct(rows, width), part, part, struct(4, width, dtype=F32)]
    return call(out_kernel, outs, place, dpre, w_up, mid, top, vec, branch, att, w_out,
                scratch=[pltpu.VMEM((rows, width), BF16)])


def attention_kernel(place, q, k, v, p, datt, normed, dproj_o, send_o, keep_o, sum_o):
    rows, width = q.shape
    slots = p.shape[1]
    pairs = width // (2 * HEAD)
    for n in range(rows // slots):
        rs = slice(n * slots, (n + 1) * slots)
        for pr in range(pairs):
            cs = slice(pr * 2 * HEAD, (pr + 1) * 2 * HEAD)
            qp, kp, vp, da = q[rs, cs], k[rs, cs], v[rs, cs], datt[rs, cs]
            dq = dk = dv = None
            for h in range(2):
                weights = p[(n * pairs + pr) * 2 + h]
                probs = weights.astype(F32)
                dw = dot(pick(vp, h), da, NT)
                ds = (probs * (dw - jnp.sum(probs * dw, 0, keepdims=True))).astype(BF16)
                a = dot(ds, pick(kp, h), TN)
                b = dot(ds, pick(qp, h))
                c = dot(weights, pick(da, h))
                dq, dk, dv = (a, b, c) if dq is None else (dq + a, dk + b, dv + c)
            dproj_o[rs, pr * 128 : pr * 128 + 128] = (dq * HEAD**-0.5).astype(BF16)
            dproj_o[rs, width + pr * 128 : width + pr * 128 + 128] = dk.astype(BF16)
            dproj_o[rs, 2 * width + pr * 128 : 2 * width + pr * 128 + 128] = dv.astype(BF16)
    sum_o[0:1] = sums(dproj_o[:, :width].astype(F32))
    sum_o[1:2] = sums(dproj_o[:, 2 * width :].astype(F32))
    cut_rows(place, normed, dproj_o, send_o, keep_o, 0, 3 * width // 6)


def attention(place, q, k, v, p, datt, normed, blocks):
    rows, width = q.shape
    part = struct(blocks, width // blocks, 3 * width // 2)
    outs = [struct(rows, 3 * width), part, part, struct(2, width, dtype=F32)]
    return call(attention_kernel, outs, place, q, k, v, p, datt, normed)


def spread(entry, outs, mine):
    band_rows, width = outs[0].shape[1:]
    entry = entry.reshape(mine, len(outs), band_rows, width)
    for b, o in enumerate(outs):
        o[...] = entry[:, b]


def input_kernel(place, dproj, w_qkv, x, dmid, vec, *outs, mine):
    grad = dot(dproj[...], w_qkv[...], NT)
    xhat, inverse = norm_parts(x[...].astype(F32))
    sum_o = outs[-1]
    sum_o[0:1] = sums(grad * xhat)
    sum_o[1:2] = sums(grad)
    result = (dmid[...] + norm_back(grad, vec[G1 : G1 + 1], xhat, inverse)).astype(BF16)
    spread(result, outs[:-1], mine)


def input_back(place, dproj, w_qkv, x, dmid, vec, mine, bands):
    rows, width = x.shape
    outs = [struct(mine, rows // mine // bands, width)] * bands + [struct(2, width, dtype=F32)]
    return call(functools.partial(input_kernel, mine=mine), outs, place, dproj, w_qkv, x, dmid, vec)


def output_kernel(place, hidden, w_down, mid, top, valid, vec, *outs, mine):
    branch = dot(hidden[...], w_down[...]) + vec[B_DOWN : B_DOWN + 1]
    outs[-1][...] = sums(top[...].astype(F32) * branch)
    result = (valid[...] * (mid[...] + vec[S_MLP : S_MLP + 1] * branch)).astype(BF16)
    spread(result, outs[:-1], mine)


def output_rows(place, hidden, w_down, mid, top, valid, vec, mine, bands):
    rows, width = mid.shape
    outs = [struct(mine, rows // mine // bands, width)] * bands + [struct(1, width, dtype=F32)]
    return call(functools.partial(output_kernel, mine=mine), outs, place, hidden, w_down, mid, top, valid, vec)


def place_kernel(place, *refs):
    *parts, out = refs
    mine = parts[0].shape[0]
    for q, part in enumerate(parts):
        out[pl.ds((place[0] ^ q) * mine, mine)] = part[...]


def swap(entry, axis, mask):
    size = lax.axis_size(axis)
    return lax.ppermute(entry, axis, [(i, i ^ mask) for i in range(size)])


def add(left, right):
    return (left.astype(F32) + right.astype(F32)).astype(left.dtype)


def halve(entry, axis, bit, dim):
    keep, send = (lax.index_in_dim(entry, i, dim, False) for i in range(2))
    return add(keep, swap(send, axis, 1 << bit))


def join(entry, axis, bit, dim):
    got = swap(entry, axis, 1 << bit)
    high = (lax.axis_index(axis) >> bit) & 1
    first = jnp.where(high == 1, got, entry)
    second = jnp.where(high == 1, entry, got)
    return jnp.concatenate([first, second], dim)


def scatter(blocks, order):
    r, c = blocks.shape[1:]
    b = blocks.reshape(2, 2, 2, r, c)
    if order == "yzx":
        b = halve(b, "img", 0, 2)
        b = halve(b, "img", 1, 1)
        b = halve(b, "img", 2, 0)
        return add(b, swap(b, "band", 2))
    b = b.reshape(2, 2, 2, 2, r // 2, c)
    high = (lax.axis_index("band") >> 1) & 1
    keep = lax.dynamic_index_in_dim(b, high, 3, False)
    b = add(keep, swap(lax.dynamic_index_in_dim(b, 1 - high, 3, False), "band", 2))
    b = halve(b, "img", 0, 2)
    b = halve(b, "img", 1, 1)
    b = halve(b, "img", 2, 0)
    return join(b, "band", 1, 0)


def reduce_fast(pair, dim, cut):
    send, keep = pair
    blocks = add(keep, swap(send, "band", 1))
    if cut < blocks.shape[2]:
        parts = [scatter(blocks[:, :, :cut], "yzx"), scatter(blocks[:, :, cut:], "xyz")]
        mine = jnp.concatenate(parts, 1)
    else:
        mine = scatter(blocks, "yzx")
    return join(mine, "band", 0, dim - 1).astype(F32)


def reduce_plain(pair, dim):
    send, keep = pair
    grad = jnp.concatenate([keep, send], dim).astype(F32)
    grad = grad.reshape(-1, grad.shape[2])
    part = lax.psum_scatter(grad, "img", scatter_dimension=0, tiled=True)
    return lax.psum(part.astype(BF16), "band").astype(F32)


def shards(
    tokens, cotangent, grid_side, visible, w_qkv, q_bias, v_bias, w_out, b_out, ln1_gain, ln1_shift,
    ln2_gain, ln2_shift, w_up, b_up, w_down, b_down, scale_attn, scale_mlp,
):
    images, band_rows, width = tokens.shape
    bands, imgs = lax.axis_size("band"), lax.axis_size("img")
    band, img = lax.axis_index("band"), lax.axis_index("img")
    mine = images // bands
    slots = bands * band_rows
    fast = imgs == 8 and bands == 4
    blocks = 8
    place = jnp.stack([band, (band & 1) if fast else 0 * band, img if fast else 0 * img]).astype(jnp.int32)

    def to_images(entry):
        parts = [lax.dynamic_slice_in_dim(entry, mine * (band ^ q), mine, 0) for q in range(1, bands)]
        return [swap(part, "band", q + 1) for q, part in enumerate(parts)]

    def to_bands(parts):
        parts = [swap(part, "band", q) if q else part for q, part in enumerate(parts)]
        return call(place_kernel, [struct(images, band_rows, width)], place, *parts)[0]

    sides = lax.dynamic_slice_in_dim(grid_side, band * mine, mine, 0)
    seen = lax.dynamic_slice_in_dim(visible, band * mine, mine, 0)
    order = jnp.arange(bands, dtype=jnp.int32) ^ band
    index = (order[:, None] * band_rows + jnp.arange(band_rows, dtype=jnp.int32)[None, :]).reshape(-1)
    inside = (index[None, :] // GRID < sides[:, None]) & (index[None, :] % GRID < sides[:, None])
    seen = seen.reshape(mine, bands, band_rows)[:, order].reshape(mine, slots)
    valid = inside.astype(F32).reshape(mine * slots, 1)
    bias = jnp.where(inside & (seen == 1), 0.0, NEG_BIG).astype(F32).reshape(mine * slots, 1)
    vec = jnp.concatenate(
        [q_bias, v_bias, b_out, ln1_gain, ln1_shift, ln2_gain, ln2_shift, b_down, scale_attn, scale_mlp, b_up]
    ).reshape(-1, width)

    got_x = to_images(tokens)
    got_c = to_images(cotangent)
    x, normed, q, k, v, p, att, branch, mid, normed2, hidden, slope = forward(
        place, tokens, got_x, bias, vec, w_qkv, w_out, w_up
    )
    top, gm, down_send, down_keep, s_bd = down(place, cotangent, got_c, valid, vec, hidden, blocks)
    dpre, up_send, up_keep, s_bu = up(place, gm, slope, w_down, normed2, blocks)
    dmid, datt, out_send, out_keep, s_o = attention_out(place, dpre, w_up, mid, top, vec, branch, att, w_out, blocks)
    dproj, qkv_send, qkv_keep, s_q = attention(place, q, k, v, p, datt, normed, blocks)
    *grad_in, s_i = input_back(place, dproj, w_qkv, x, dmid, vec, mine, bands)
    *out, s_m = output_rows(place, hidden, w_down, mid, top, valid, vec, mine, bands)
    output = to_bands(out)
    input_grad = to_bands(grad_in)
    rest = jnp.concatenate([out_send, qkv_send], 2), jnp.concatenate([out_keep, qkv_keep], 2)
    if fast:
        grad_w_down = reduce_fast((down_send, down_keep), 1, 384)
        grad_w_up = reduce_fast((up_send, up_keep), 2, 768)
        grad_rest = reduce_fast(rest, 2, 768)
        half = width // 2
        at = 2 * width
        grad_w_out = jnp.concatenate([grad_rest[:, :half], grad_rest[:, at : at + half]], 1)
        grad_w_qkv = jnp.concatenate([grad_rest[:, half:at], grad_rest[:, at + half :]], 1)
    else:
        grad_w_down = reduce_plain((down_send, down_keep), 1)
        grad_w_up = reduce_plain((up_send, up_keep), 2)
        grad_w_out = reduce_plain((out_send, out_keep), 2)
        grad_w_qkv = reduce_plain((qkv_send, qkv_keep), 2)
    small = [s_q[0], s_q[1], s_o[3], s_i[0], s_i[1], s_o[0], s_o[1], s_bu.reshape(-1), s_bd[0], s_o[2], s_m[0]]
    sizes = [entry.shape[0] // imgs for entry in small]
    small = jnp.concatenate([entry.reshape(imgs, -1) for entry in small], 1)
    if fast:
        small = small[jnp.arange(imgs) ^ img].reshape(2, 2, 2, -1)
        small = halve(small, "img", 0, 2)
        small = halve(small, "img", 1, 1)
        small = halve(small, "img", 2, 0)
        small = add(small, swap(small, "band", 1))
        small = add(small, swap(small, "band", 2))
    else:
        small = lax.dynamic_index_in_dim(lax.psum(small, ("img", "band")), img, 0, False)
    shares = []
    at = 0
    for size in sizes:
        shares.append(small[at : at + size])
        at += size
    (s_qb, s_vb, s_bo, s_g1, s_c1, s_g2, s_c2, s_bu, s_bd, s_sa, s_sm) = shares
    return (
        output, input_grad, grad_w_qkv, s_qb, s_vb, grad_w_out, s_bo, s_g1, s_c1, s_g2, s_c2, grad_w_up, s_bu,
        grad_w_down, s_bd, s_sa, s_sm,
    )


def solution(mesh):
    cut = P("img", "band", None)
    in_specs = (cut, cut, P("img"), P("img", None)) + (P(),) * 15
    row, vec = P("img", None), P("img")
    out_specs = (cut, cut, row, vec, vec, row, vec, vec, vec, vec, vec, row, vec, row, vec, vec, vec)
    return jax.shard_map(shards, mesh=mesh, in_specs=in_specs, out_specs=out_specs, check_vma=False)
```

```python
import functools
import math

import jax
import jax.numpy as jnp
from jax import lax
from jax.experimental import pallas as pl
from jax.experimental.pallas import tpu as pltpu
from jax.sharding import PartitionSpec as P

HEAD = 64
GRID = 16
NEG_BIG = -1e30
EPSILON = 1e-06
F32 = jnp.float32
BF16 = jnp.bfloat16
VM = pl.BlockSpec(memory_space=pltpu.VMEM)
SM = pl.BlockSpec(memory_space=pltpu.SMEM)
NN, NT, TN = ((1,), (0,)), ((1,), (1,)), ((0,), (0,))
Q_BIAS, V_BIAS, B_OUT, G1, C1, G2, C2, B_DOWN, S_ATTN, S_MLP, B_UP = range(11)


def dot(left, right, dims=NN):
    return lax.dot_general(left, right, (dims, ((), ())), preferred_element_type=F32)


def struct(*shape, dtype=BF16):
    return jax.ShapeDtypeStruct(shape, dtype)


def call(kernel, outs, place, *args, limit=8, token=None):
    count = len(args)

    def body(place_ref, *refs):
        kernel(place_ref, *refs[:count], *refs[count + 1 : -1])
        refs[-1][...] = jnp.zeros_like(refs[-1])

    token = jnp.zeros((1, 128), F32) if token is None else token
    return pl.pallas_call(
        body,
        out_shape=[*outs, struct(1, 128, dtype=F32)],
        in_specs=[SM] + [VM] * (count + 1),
        out_specs=[VM] * (len(outs) + 1),
        compiler_params=pltpu.CompilerParams(vmem_limit_bytes=limit * 2**20),
        cost_estimate=pl.CostEstimate(flops=1000, bytes_accessed=1000, transcendentals=0),
    )(place, *args, token)


def norm_parts(entry):
    center = entry - jnp.mean(entry, -1, keepdims=True)
    spread = jnp.mean(center * center, -1, keepdims=True)
    inverse = lax.rsqrt(spread + EPSILON)
    return center * inverse, inverse


def norm_back(grad, gain, xhat, inverse):
    scaled = grad * gain
    inner = scaled - jnp.mean(scaled, -1, keepdims=True)
    return (inner - xhat * jnp.mean(scaled * xhat, -1, keepdims=True)) * inverse


def pick(entry, head):
    lane = lax.broadcasted_iota(jnp.int32, entry.shape, 1)
    return jnp.where((lane < HEAD) if head == 0 else (lane >= HEAD), entry, jnp.zeros_like(entry))


def whole_images(parts):
    mine, band_rows, width = parts[0].shape
    return jnp.concatenate([p[...][:, None] for p in parts], 1).reshape(mine * len(parts) * band_rows, width)


def cut_kernel(place, entry, *refs, mine):
    *outs, sem = refs
    copies = [
        pltpu.make_async_copy(entry.at[pl.ds((place[0] ^ q) * mine, mine)], out, sem.at[q]) for q, out in enumerate(outs)
    ]
    for copy in copies:
        copy.start()
    for copy in copies:
        copy.wait()


def cut(place, entry, bands):
    images, band_rows, width = entry.shape
    mine = images // bands
    return pl.pallas_call(
        functools.partial(cut_kernel, mine=mine),
        out_shape=[struct(mine, band_rows, width)] * bands,
        in_specs=[SM, pl.BlockSpec(memory_space=pltpu.HBM)],
        out_specs=[VM] * bands,
        scratch_shapes=[pltpu.SemaphoreType.DMA((bands,))],
        compiler_params=pltpu.CompilerParams(vmem_limit_bytes=2**20),
        cost_estimate=pl.CostEstimate(flops=1000, bytes_accessed=1000, transcendentals=0),
    )(place, entry)


def prepare_kernel(place, sides, visible, *refs, mine, bands, count):
    vectors, (vec_o, bias_o, valid_o), scratch = refs[:count], refs[count : count + 3], refs[count + 3 :]
    seen_s, sem = scratch[-2:]
    copies = [
        pltpu.make_async_copy(a, b, sem.at[i]) for i, (a, b) in enumerate(zip((*vectors, visible), scratch[:-1]))
    ]
    for copy in copies:
        copy.start()
    for copy in copies:
        copy.wait()
    width = vec_o.shape[1]
    lanes = 128
    row = 0
    for s in scratch[:-2]:
        for j in range(s.shape[0]):
            at = row * lanes + j * lanes
            vec_o[at // width : at // width + 1, at % width : at % width + lanes] = s[j : j + 1]
        row += s.shape[0]
    band = place[0]
    slots = seen_s.shape[1]
    band_rows = slots // bands
    at = lax.broadcasted_iota(jnp.int32, (1, slots), 1)
    slot = ((at // band_rows) ^ band) * band_rows + at % band_rows
    for n in range(mine):
        side = sides[band * mine + n]
        row = seen_s[pl.ds(band * mine + n, 1), :]
        parts = [row[:, b * band_rows : (b + 1) * band_rows] for b in range(bands)]
        seen = []
        for q in range(bands):
            part = parts[0]
            for b in range(1, bands):
                part = jnp.where((band ^ q) == b, parts[b], part)
            seen.append(part)
        inside = (slot // GRID < side) & (slot % GRID < side)
        bias = jnp.where(inside & (jnp.concatenate(seen, 1) == 1), 0.0, NEG_BIG)
        for out, entry in ((bias_o, bias), (valid_o, jnp.where(inside, 1.0, 0.0))):
            out[n * slots : (n + 1) * slots, :] = jnp.broadcast_to(entry, (lanes, slots)).T


def prepare(place, grid_side, visible, vectors, bands):
    images, slots = visible.shape
    mine = images // bands
    width = vectors[0].shape[0]
    vectors = [entry.reshape(-1, 128) for entry in vectors]
    rows = sum(entry.shape[0] for entry in vectors) * 128 // width
    flat = struct(mine * slots, 128, dtype=F32)
    any_ref = pl.BlockSpec(memory_space=pltpu.HBM)
    return pl.pallas_call(
        functools.partial(prepare_kernel, mine=mine, bands=bands, count=len(vectors)),
        out_shape=[struct(rows, width, dtype=F32), flat, flat],
        in_specs=[SM, SM] + [any_ref] * (len(vectors) + 1),
        out_specs=[VM] * 3,
        scratch_shapes=[pltpu.VMEM(entry.shape, F32) for entry in vectors]
        + [pltpu.VMEM(visible.shape, jnp.int32), pltpu.SemaphoreType.DMA((len(vectors) + 1,))],
        compiler_params=pltpu.CompilerParams(vmem_limit_bytes=4 * 2**20),
        cost_estimate=pl.CostEstimate(flops=1000, bytes_accessed=1000, transcendentals=0),
    )(place, grid_side, visible, *vectors)


def repeat(entry, width):
    return jnp.concatenate([entry] * (width // entry.shape[1]), 1)


def forward_kernel(place, *refs, bands):
    parts = refs[:bands]
    (bias, vec, w_qkv, w_out, w_up,
     x_o, normed_o, q_o, k_o, v_o, p_o, att_o, branch_o, mid_o, normed2_o, hidden_o, slope_o) = refs[bands:]
    mine = parts[0].shape[0]
    width = x_o.shape[1]
    rows = x_o.shape[0]
    slots = rows // mine
    x_o[...] = whole_images(parts)
    xhat, _ = norm_parts(x_o[...].astype(F32))
    normed_o[...] = (xhat * vec[G1 : G1 + 1] + vec[C1 : C1 + 1]).astype(BF16)
    normed = normed_o[...]
    queries = (dot(normed, w_qkv[:, :width]) + vec[Q_BIAS : Q_BIAS + 1]).astype(BF16)
    q_o[...] = (queries.astype(F32) * HEAD**-0.5).astype(BF16)
    k_o[...] = dot(normed, w_qkv[:, width : 2 * width]).astype(BF16)
    v_o[...] = (dot(normed, w_qkv[:, 2 * width :]) + vec[V_BIAS : V_BIAS + 1]).astype(BF16)
    pairs = width // (2 * HEAD)
    for n in range(mine):
        rs = slice(n * slots, (n + 1) * slots)
        mask = repeat(bias[rs, :], slots)
        for pr in range(pairs):
            cs = slice(pr * 2 * HEAD, (pr + 1) * 2 * HEAD)
            q, k, v = q_o[rs, cs], k_o[rs, cs], v_o[rs, cs]
            total = None
            for h in range(2):
                s = dot(pick(k, h), q, NT) + mask
                e = jnp.exp(s - jnp.max(s, 0, keepdims=True))
                p = (e * (1.0 / jnp.sum(e, 0, keepdims=True))).astype(BF16)
                p_o[(n * pairs + pr) * 2 + h] = p
                part = dot(p, pick(v, h), TN)
                total = part if total is None else total + part
            att_o[rs, cs] = total.astype(BF16)
    branch = dot(att_o[...], w_out[...]) + vec[B_OUT : B_OUT + 1]
    branch_o[...] = branch.astype(BF16)
    middle = x_o[...].astype(F32) + vec[S_ATTN : S_ATTN + 1] * branch
    mid_o[...] = middle
    xhat2, _ = norm_parts(middle)
    normed2_o[...] = (xhat2 * vec[G2 : G2 + 1] + vec[C2 : C2 + 1]).astype(BF16)
    for j in range(hidden_o.shape[1] // width):
        js = slice(j * width, (j + 1) * width)
        pre = dot(normed2_o[...], w_up[:, js]) + vec[B_UP + j : B_UP + j + 1]
        cdf = 0.5 + 0.5 * lax.erf(0.5**0.5 * pre)
        bell = jnp.exp2((-0.5 / math.log(2.0)) * (pre * pre))
        hidden_o[:, js] = (pre * cdf).astype(BF16)
        slope_o[:, js] = (cdf + ((0.5 / math.pi) ** 0.5 * pre) * bell).astype(BF16)


def forward(place, parts, bias, vec, w_qkv, w_out, w_up, **keys):
    mine, band_rows, width = parts[0].shape
    bands = len(parts)
    slots = bands * band_rows
    rows = mine * slots
    row, wide = struct(rows, width), struct(rows, w_up.shape[1])
    p = struct(mine * width // HEAD, slots, slots)
    outs = [row, row, row, row, row, p, row, row, struct(rows, width, dtype=F32), row, wide, wide]
    kernel = functools.partial(forward_kernel, bands=bands)
    return call(kernel, outs, place, *parts, bias, vec, w_qkv, w_out, w_up, limit=20, **keys)


def sums(entry):
    return jnp.sum(entry, 0, keepdims=True)


def down_kernel(place, *refs, bands):
    parts = refs[:bands]
    valid, vec, hidden, top_o, gm_o, send_o, keep_o, sum_o = refs[bands:]
    top = repeat(valid[...], gm_o.shape[1]) * whole_images(parts).astype(F32)
    top_o[...] = top.astype(BF16)
    gm_o[...] = (vec[S_MLP : S_MLP + 1] * top).astype(BF16)
    sum_o[...] = sums(gm_o[...].astype(F32))
    blocks, half, _ = send_o.shape
    first = place[1] == 0
    for p in range(blocks):
        at = pl.multiple_of((p ^ place[2]) * (2 * half), 128)
        grad = dot(hidden[:, pl.ds(at, 2 * half)], gm_o[...], TN).astype(BF16)
        keep_o[p] = jnp.where(first, grad[:half], grad[half:])
        send_o[p] = jnp.where(first, grad[half:], grad[:half])


def down(place, parts, valid, vec, hidden, blocks, **keys):
    rows, ff = hidden.shape
    width = vec.shape[1]
    part = struct(blocks, ff // blocks // 2, width)
    outs = [struct(rows, width), struct(rows, width), part, part, struct(1, width, dtype=F32)]
    return call(functools.partial(down_kernel, bands=len(parts)), outs, place, *parts, valid, vec, hidden, **keys)


def cut_rows(place, left, right, send_o, keep_o, at_o, tile):
    blocks, rows, _ = send_o.shape
    half = right.shape[1] // 2
    for target, core in ((send_o, 1 - place[1]), (keep_o, place[1])):
        for j in range(half // tile):
            at = pl.multiple_of(core * half + j * tile, 128)
            grad = dot(left[...], right[:, pl.ds(at, tile)], TN).astype(BF16)
            for i in range(blocks):
                target[i ^ place[2], :, at_o + j * tile : at_o + (j + 1) * tile] = grad[i * rows : (i + 1) * rows]


def up_kernel(place, gm, slope, w_down, normed2, dpre_o, send_o, keep_o, sum_o):
    ff = slope.shape[1]
    tile = gm.shape[1]
    for j in range(ff // tile):
        js = slice(j * tile, (j + 1) * tile)
        grad = (dot(gm[...], w_down[js, :], NT) * slope[:, js].astype(F32)).astype(BF16)
        dpre_o[:, js] = grad
        sum_o[j : j + 1] = sums(grad.astype(F32))
    cut_rows(place, normed2, dpre_o, send_o, keep_o, 0, ff // 4)


def up(place, gm, slope, w_down, normed2, blocks, **keys):
    rows, ff = slope.shape
    width = gm.shape[1]
    part = struct(blocks, width // blocks, ff // 2)
    outs = [struct(rows, ff), part, part, struct(ff // width, width, dtype=F32)]
    return call(up_kernel, outs, place, gm, slope, w_down, normed2, limit=11, **keys)


def out_kernel(place, dpre, w_up, mid, top, vec, branch, att, w_out, dmid_o, datt_o, send_o, keep_o, sum_o):
    grad = dot(dpre[...], w_up[...], NT)
    xhat, inverse = norm_parts(mid[...])
    sum_o[0:1] = sums(grad * xhat)
    sum_o[1:2] = sums(grad)
    dmid = top[...].astype(F32) + norm_back(grad, vec[G2 : G2 + 1], xhat, inverse)
    dmid_o[...] = dmid
    sum_o[2:3] = sums(dmid * branch[...].astype(F32))
    db = (vec[S_ATTN : S_ATTN + 1] * dmid).astype(BF16)
    sum_o[3:4] = sums(db.astype(F32))
    datt_o[...] = db
    cut_rows(place, att, datt_o, send_o, keep_o, 0, db.shape[1] // 2)
    datt_o[...] = dot(db, w_out[...], NT).astype(BF16)


def attention_out(place, dpre, w_up, mid, top, vec, branch, att, w_out, blocks, **keys):
    rows, width = mid.shape
    part = struct(blocks, width // blocks, width // 2)
    outs = [struct(rows, width, dtype=F32), struct(rows, width), part, part, struct(4, width, dtype=F32)]
    return call(out_kernel, outs, place, dpre, w_up, mid, top, vec, branch, att, w_out, limit=11, **keys)


def attention_kernel(place, q, k, v, p, datt, dproj_o, sum_o):
    rows, width = q.shape
    slots = p.shape[1]
    pairs = width // (2 * HEAD)
    for n in range(rows // slots):
        rs = slice(n * slots, (n + 1) * slots)
        for pr in range(pairs):
            cs = slice(pr * 2 * HEAD, (pr + 1) * 2 * HEAD)
            qp, kp, vp, da = q[rs, cs], k[rs, cs], v[rs, cs], datt[rs, cs]
            dq = dk = dv = None
            for h in range(2):
                weights = p[(n * pairs + pr) * 2 + h]
                probs = weights.astype(F32)
                dw = dot(pick(vp, h), da, NT)
                ds = (probs * (dw - jnp.sum(probs * dw, 0, keepdims=True))).astype(BF16)
                a = dot(ds, pick(kp, h), TN)
                b = dot(ds, pick(qp, h))
                c = dot(weights, pick(da, h))
                dq, dk, dv = (a, b, c) if dq is None else (dq + a, dk + b, dv + c)
            dproj_o[rs, pr * 128 : pr * 128 + 128] = (dq * HEAD**-0.5).astype(BF16)
            dproj_o[rs, width + pr * 128 : width + pr * 128 + 128] = dk.astype(BF16)
            dproj_o[rs, 2 * width + pr * 128 : 2 * width + pr * 128 + 128] = dv.astype(BF16)
    sum_o[0:1] = sums(dproj_o[:, :width].astype(F32))
    sum_o[1:2] = sums(dproj_o[:, 2 * width :].astype(F32))


def attention(place, q, k, v, p, datt, **keys):
    rows, width = q.shape
    outs = [struct(rows, 3 * width), struct(2, width, dtype=F32)]
    return call(attention_kernel, outs, place, q, k, v, p, datt, **keys)


def qkv_kernel(place, normed, dproj, send_o, keep_o):
    cut_rows(place, normed, dproj, send_o, keep_o, 0, 384)


def qkv(place, normed, dproj, blocks, **keys):
    width = normed.shape[1]
    part = struct(blocks, width // blocks, 3 * width // 2)
    return call(qkv_kernel, [part, part], place, normed, dproj, limit=11, **keys)


def spread(entry, outs, mine):
    band_rows, width = outs[0].shape[1:]
    entry = entry.reshape(mine, len(outs), band_rows, width)
    for b, o in enumerate(outs):
        o[...] = entry[:, b]


def input_kernel(place, dproj, w_qkv, x, dmid, vec, *outs, mine):
    grad = dot(dproj[...], w_qkv[...], NT)
    xhat, inverse = norm_parts(x[...].astype(F32))
    sum_o = outs[-1]
    sum_o[0:1] = sums(grad * xhat)
    sum_o[1:2] = sums(grad)
    result = (dmid[...] + norm_back(grad, vec[G1 : G1 + 1], xhat, inverse)).astype(BF16)
    spread(result, outs[:-1], mine)


def input_back(place, dproj, w_qkv, x, dmid, vec, mine, bands, **keys):
    rows, width = x.shape
    outs = [struct(mine, rows // mine // bands, width)] * bands + [struct(2, width, dtype=F32)]
    return call(functools.partial(input_kernel, mine=mine), outs, place, dproj, w_qkv, x, dmid, vec, **keys)


def output_kernel(place, hidden, w_down, mid, top, valid, vec, *outs, mine):
    branch = dot(hidden[...], w_down[...]) + vec[B_DOWN : B_DOWN + 1]
    outs[-1][...] = sums(top[...].astype(F32) * branch)
    result = (repeat(valid[...], mid.shape[1]) * (mid[...] + vec[S_MLP : S_MLP + 1] * branch)).astype(BF16)
    spread(result, outs[:-1], mine)


def output_rows(place, hidden, w_down, mid, top, valid, vec, mine, bands, **keys):
    rows, width = mid.shape
    outs = [struct(mine, rows // mine // bands, width)] * bands + [struct(1, width, dtype=F32)]
    kernel = functools.partial(output_kernel, mine=mine)
    return call(kernel, outs, place, hidden, w_down, mid, top, valid, vec, **keys)


def place_kernel(place, *refs):
    *parts, out = refs
    mine = parts[0].shape[0]
    for q, part in enumerate(parts):
        out[pl.ds((place[0] ^ q) * mine, mine)] = part[...]


def swap(entry, axis, mask):
    size = lax.axis_size(axis)
    return lax.ppermute(entry, axis, [(i, i ^ mask) for i in range(size)])


def total(*entries):
    result = entries[0].astype(F32)
    for entry in entries[1:]:
        result = result + entry.astype(F32)
    return result


class Part:
    def __init__(self, entries, steps):
        self.entries, self.steps = entries, steps

    def shapes(self):
        _, _, groups = self.steps[0]
        _, rows, cols = self.entries[0].shape
        if groups is None:
            return [struct(1, rows, cols)]
        return [struct(len(group), rows, cols) for group in groups]

    def fold(self, refs, outs):
        _, _, groups = self.steps[0]
        if groups is None:
            groups = [range(refs[0].shape[0])]
        for group, out in zip(groups, outs):
            for i, at in enumerate(group):
                out[i] = total(*(ref[at] for ref in refs)).astype(BF16)

    def send(self, outs):
        axis, masks, groups = self.steps[0]
        sent = [outs[0]] * len(masks) if groups is None else outs[1:]
        got = [swap(entry, axis, mask) for entry, mask in zip(sent, masks)]
        return Part([outs[0], *got], self.steps[1:])


def fold(place, parts, token):
    shapes = [part.shapes() for part in parts]
    counts = [len(part.entries) for part in parts]

    def kernel(place_ref, *refs):
        at, out_at = 0, sum(counts)
        for part, count, shape in zip(parts, counts, shapes):
            part.fold(refs[at : at + count], refs[out_at : out_at + len(shape)])
            at += count
            out_at += len(shape)

    entries = [entry for part in parts for entry in part.entries]
    *outs, token = call(kernel, [s for shape in shapes for s in shape], place, *entries, limit=4, token=token)
    sent = []
    for part, shape in zip(parts, shapes):
        sent.append(part.send(outs[: len(shape)]))
        outs = outs[len(shape) :]
    return sent, token


EVEN_ODD = ([0, 2, 4, 6], [1, 3, 5, 7])
STEP_Y = ("img", (1,), EVEN_ODD)
STEP_Z = ("img", (2, 4, 6), ([0], [1], [2], [3]))
STEP_X = ("band", (2,), None)
STEP_C = ("band", (1,), None)
STEP_BAND = ("band", (1, 2, 3), None)


def first_kernel(place, *refs, count, cols, by_x):
    pairs = [(refs[2 * i], refs[2 * i + 1]) for i in range(count)]
    keep_p, send_p, keep_r, send_r = refs[2 * count :]
    at = 0
    rows = pairs[0][0].shape[1]
    half = rows // 2
    mine = pl.multiple_of(place[3] * half, 16)
    other = pl.multiple_of((1 - place[3]) * half, 16)
    for keep, got in pairs:
        width = keep.shape[2]
        low = max(0, min(cols - at, width))
        if low:
            for i in range(8):
                target = send_p if i & 1 else keep_p
                target[i // 2, :, at : at + low] = total(keep[i, :, :low], got[i, :, :low]).astype(BF16)
        if low < width:
            to = slice(at + low - cols, at + width - cols)
            for i in range(8):
                for start, target in ((mine, keep_r), (other, send_r)):
                    rs = pl.ds(start, half)
                    target[i, :, to] = total(keep[i, rs, low:], got[i, rs, low:]).astype(BF16)
        at += width


def first_fold(place, pairs, cols, token):
    rows = pairs[0][0].shape[1]
    width = sum(pair[0].shape[2] for pair in pairs)
    p, r = struct(4, rows, cols), struct(8, rows // 2, width - cols)
    kernel = functools.partial(first_kernel, count=len(pairs), cols=cols, by_x=True)
    args = [entry for pair in pairs for entry in pair]
    keep_p, send_p, keep_r, send_r, token = call(kernel, [p, p, r, r], place, *args, limit=8, token=token)
    part_p = Part([keep_p, swap(send_p, "img", 1)], [STEP_Z, STEP_X, STEP_C])
    part_r = Part([keep_r, swap(send_r, "band", 2)], [STEP_Y, STEP_Z, STEP_BAND])
    return [part_p, part_r], token


def finish(place, part_p, part_r, shapes, by_rows, token):
    cols = part_p.entries[0].shape[2]

    def kernel(place_ref, p0, p1, r0, r1, r2, r3, *outs):
        core, x = place_ref[1], place_ref[3]
        half_rows, half_cols = p0.shape[1], p0.shape[2] + r0.shape[2]
        for c, p in ((core, p0), (1 - core, p1)):
            write(outs, p[0].astype(F32), c, 0, 0, half_rows, half_cols, by_rows)
        for i, r in enumerate((r0, r1, r2, r3)):
            row = (x ^ (i >> 1)) * r.shape[1]
            write(outs, r[0].astype(F32), core ^ (i & 1), row, cols, half_rows, half_cols, by_rows)

    return call(kernel, shapes, place, *part_p.entries, *part_r.entries, limit=6, token=token)


def write(outs, entry, core, row, col, half_rows, half_cols, by_rows):
    rows, width = entry.shape
    if by_rows:
        at = pl.multiple_of(core * half_rows + row, 8)
        outs[0][pl.ds(at, rows), col : col + width] = entry
        return
    start = 0
    for out in outs:
        half = out.shape[1] // 2
        low, high = max(col, start), min(col + width, start + half)
        if low < high:
            at = pl.multiple_of(core * half + (low - start), 128)
            row_at = row if isinstance(row, int) else pl.multiple_of(row, 8)
            out[pl.ds(row_at, rows), pl.ds(at, high - low)] = entry[:, low - col : high - col]
        start += half


def pack_kernel(place, *refs):
    *entries, out = refs
    blocks = out.shape[0]
    out[...] = jnp.zeros_like(out)
    for i in range(blocks):
        at = i ^ place[2]
        row = 0
        rows = []
        for ref, which in entries_of(entries):
            flat = jnp.concatenate([ref[j : j + 1] for j in which], 1)
            size = flat.shape[1] // blocks
            rows.append((size, flat[:, i * size : (i + 1) * size]))
        for row, (size, value) in enumerate(rows):
            out[at, row : row + 1, :size] = value


def entries_of(entries):
    s_q, s_i, s_o, s_bu, s_bd, s_m = entries
    return [
        (s_q, [0]), (s_q, [1]), (s_o, [3]), (s_i, [0]), (s_i, [1]), (s_o, [0]), (s_o, [1]),
        (s_bu, range(s_bu.shape[0])), (s_bd, [0]), (s_o, [2]), (s_m, [0]),
    ]


class Small(Part):
    def shapes(self):
        return [jax.ShapeDtypeStruct(s.shape, F32) for s in super().shapes()]

    def fold(self, refs, outs):
        _, _, groups = self.steps[0]
        if groups is None:
            groups = [range(refs[0].shape[0])]
        for group, out in zip(groups, outs):
            for i, at in enumerate(group):
                out[i] = total(*(ref[at] for ref in refs))

    def send(self, outs):
        part = super().send(outs)
        return Small(part.entries, part.steps)


def reduce_plain(pair, dim):
    send, keep = pair
    grad = jnp.concatenate([keep, send], dim).astype(F32)
    grad = grad.reshape(-1, grad.shape[2])
    part = lax.psum_scatter(grad, "img", scatter_dimension=0, tiled=True)
    return lax.psum(part.astype(BF16), "band").astype(F32)


def shards(
    tokens, cotangent, grid_side, visible, w_qkv, q_bias, v_bias, w_out, b_out, ln1_gain, ln1_shift,
    ln2_gain, ln2_shift, w_up, b_up, w_down, b_down, scale_attn, scale_mlp,
):
    images, band_rows, width = tokens.shape
    bands, imgs = lax.axis_size("band"), lax.axis_size("img")
    band, img = lax.axis_index("band"), lax.axis_index("img")
    mine = images // bands
    fast = imgs == 8 and bands == 4
    blocks = 8
    zero = jnp.zeros_like(band)
    place = jnp.stack([band, band & 1, img, band >> 1] if fast else [band, zero, zero, zero]).astype(jnp.int32)

    def exchange(parts):
        return [swap(part, "band", q) if q else part for q, part in enumerate(parts)]

    def to_bands(parts, token):
        return call(place_kernel, [struct(images, band_rows, width)], place, *parts, limit=4, token=token)

    got_x = exchange(cut(place, tokens, bands))
    got_c = exchange(cut(place, cotangent, bands))
    vectors = (q_bias, v_bias, b_out, ln1_gain, ln1_shift, ln2_gain, ln2_shift, b_down, scale_attn, scale_mlp, b_up)
    vec, bias, valid = prepare(place, grid_side, visible, vectors, bands)

    x, normed, q, k, v, p, att, branch, mid, normed2, hidden, slope, t = forward(
        place, got_x, bias, vec, w_qkv, w_out, w_up
    )
    top, gm, down_send, down_keep, s_bd, t = down(place, got_c, valid, vec, hidden, blocks, token=t)
    if fast:
        down_got = swap(down_send, "band", 1)
    dpre, up_send, up_keep, s_bu, t = up(place, gm, slope, w_down, normed2, blocks, token=t)
    if fast:
        up_got = swap(up_send, "band", 1)
        down_parts, t = first_fold(place, [(down_keep, down_got)], 384, t)
    dmid, datt, out_send, out_keep, s_o, t = attention_out(
        place, dpre, w_up, mid, top, vec, branch, att, w_out, blocks, token=t
    )
    if fast:
        out_got = swap(out_send, "band", 1)
        up_parts, t = first_fold(place, [(up_keep, up_got)], 768, t)
    dproj, s_q, t = attention(place, q, k, v, p, datt, token=t)
    if fast:
        down_parts, t = fold(place, down_parts, t)
    qkv_send, qkv_keep, t = qkv(place, normed, dproj, blocks, token=t)
    if fast:
        qkv_got = swap(qkv_send, "band", 1)
    *grad_in, s_i, t = input_back(place, dproj, w_qkv, x, dmid, vec, mine, bands, token=t)
    grad_in = exchange(grad_in)
    if fast:
        up_parts, t = fold(place, up_parts, t)
    *out, s_m, t = output_rows(place, hidden, w_down, mid, top, valid, vec, mine, bands, token=t)
    out = exchange(out)
    row = lambda size: struct(size // imgs, width, dtype=F32)
    sums_ = (s_q, s_i, s_o, s_bu, s_bd, s_m)
    if fast:
        small, t = call(pack_kernel, [struct(blocks, 16, 384, dtype=F32)], place, *sums_, limit=2, token=t)
        small = Small([small, swap(small, "band", 1)], [])
        rest_parts, t = first_fold(place, [(out_keep, out_got), (qkv_keep, qkv_got)], 768, t)
        down_parts, t = fold(place, down_parts, t)
        small = Small(small.entries, [STEP_Y, STEP_Z, STEP_X, STEP_X])
        (up_p, up_r, small), t = fold(place, [*up_parts, small], t)
        (down_p, down_r), t = fold(place, down_parts, t)
        (rest_p, rest_r, small), t = fold(place, [*rest_parts, small], t)
        input_grad, t = to_bands(grad_in, t)
        output, t = to_bands(out, t)
        (up_p, up_r), t = fold(place, [up_p, up_r], t)
        grad_w_down, t = finish(place, down_p, down_r, [struct(w_down.shape[0] // imgs, width, dtype=F32)], True, t)
        (rest_p, rest_r, small), t = fold(place, [rest_p, rest_r, small], t)
        ff = w_up.shape[1]
        grad_w_up, t = finish(place, up_p, up_r, [struct(width // imgs, ff, dtype=F32)], False, t)
        (rest_p, rest_r), t = fold(place, [rest_p, rest_r], t)
        shapes = [struct(width // imgs, n, dtype=F32) for n in (width, 3 * width)]
        grad_w_out, grad_w_qkv, t = finish(place, rest_p, rest_r, shapes, False, t)
        small = small.entries[0][0] + small.entries[1][0]
        names = [width] * 7 + [ff] + [width] * 3
        shares = [small[i, : size // imgs] for i, size in enumerate(names)]
    else:
        output, t = to_bands(out, t)
        input_grad, t = to_bands(grad_in, t)
        grad_w_down = reduce_plain((down_send, down_keep), 1)
        grad_w_up = reduce_plain((up_send, up_keep), 2)
        grad_w_out = reduce_plain((out_send, out_keep), 2)
        grad_w_qkv = reduce_plain((qkv_send, qkv_keep), 2)
        flat = [jnp.concatenate([ref[j] for j in which]) for ref, which in entries_of(sums_)]
        small = jnp.concatenate([entry.reshape(imgs, -1) for entry in flat], 1)
        small = lax.dynamic_index_in_dim(lax.psum(small, ("img", "band")), img, 0, False)
        shares, at = [], 0
        for entry in flat:
            size = entry.shape[0] // imgs
            shares.append(small[at : at + size])
            at += size
    (s_qb, s_vb, s_bo, s_g1, s_c1, s_g2, s_c2, s_bu, s_bd, s_sa, s_sm) = shares
    return (
        output, input_grad, grad_w_qkv, s_qb, s_vb, grad_w_out, s_bo, s_g1, s_c1, s_g2, s_c2, grad_w_up, s_bu,
        grad_w_down, s_bd, s_sa, s_sm,
    )


def solution(mesh):
    cut = P("img", "band", None)
    in_specs = (cut, cut, P("img"), P("img", None)) + (P(),) * 15
    row, vec = P("img", None), P("img")
    out_specs = (cut, cut, row, vec, vec, row, vec, vec, vec, vec, vec, row, vec, row, vec, vec, vec)
    return jax.shard_map(shards, mesh=mesh, in_specs=in_specs, out_specs=out_specs, check_vma=False)
```

```python
import functools
import math

import jax
import jax.numpy as jnp
from jax import lax
from jax.experimental import pallas as pl
from jax.experimental.pallas import tpu as pltpu
from jax.sharding import PartitionSpec as P

HEAD = 64
GRID = 16
NEG_BIG = -1e30
EPSILON = 1e-06
F32 = jnp.float32
BF16 = jnp.bfloat16
VM = pl.BlockSpec(memory_space=pltpu.VMEM)
SM = pl.BlockSpec(memory_space=pltpu.SMEM)
NN, NT, TN = ((1,), (0,)), ((1,), (1,)), ((0,), (0,))
Q_BIAS, V_BIAS, B_OUT, G1, C1, G2, C2, B_DOWN, S_ATTN, S_MLP, B_UP = range(11)


def dot(left, right, dims=NN):
    return lax.dot_general(left, right, (dims, ((), ())), preferred_element_type=F32)


def struct(*shape, dtype=BF16):
    return jax.ShapeDtypeStruct(shape, dtype)


def call(kernel, outs, place, *args, limit=8, token=None):
    count = len(args)

    def body(place_ref, *refs):
        kernel(place_ref, *refs[:count], *refs[count + 1 : -1])
        refs[-1][...] = jnp.zeros_like(refs[-1])

    token = jnp.zeros((1, 128), F32) if token is None else token
    return pl.pallas_call(
        body,
        out_shape=[*outs, struct(1, 128, dtype=F32)],
        in_specs=[SM] + [VM] * (count + 1),
        out_specs=[VM] * (len(outs) + 1),
        compiler_params=pltpu.CompilerParams(vmem_limit_bytes=limit * 2**20),
        cost_estimate=pl.CostEstimate(flops=1000, bytes_accessed=1000, transcendentals=0),
    )(place, *args, token)


def norm_parts(entry):
    center = entry - jnp.mean(entry, -1, keepdims=True)
    spread = jnp.mean(center * center, -1, keepdims=True)
    inverse = lax.rsqrt(spread + EPSILON)
    return center * inverse, inverse


def norm_back(grad, gain, xhat, inverse):
    scaled = grad * gain
    inner = scaled - jnp.mean(scaled, -1, keepdims=True)
    return (inner - xhat * jnp.mean(scaled * xhat, -1, keepdims=True)) * inverse


def pick(entry, head):
    lane = lax.broadcasted_iota(jnp.int32, entry.shape, 1)
    return jnp.where((lane < HEAD) if head == 0 else (lane >= HEAD), entry, jnp.zeros_like(entry))


def whole_images(parts, bands):
    total, band_rows, width = parts.shape
    mine = total // bands
    rows = [parts[b * mine + n] for n in range(mine) for b in range(bands)]
    return jnp.concatenate(rows, 0)


def split_bands(entry, out, bands):
    total, band_rows, _ = out.shape
    mine = total // bands
    for n in range(mine):
        for b in range(bands):
            at = (n * bands + b) * band_rows
            out[b * mine + n] = entry[at : at + band_rows]


def in_hbm(entry):
    return pltpu.with_memory_space_constraint(entry, pltpu.HBM)


def prepare_kernel(place, sides, visible, *refs, mine, count, weights):
    vectors, matrices = refs[:count], refs[count : count + weights]
    vec_o, bias_o, valid_o, *matrix_o = refs[count + weights : count + 2 * weights + 3]
    *scratch, seen_s, sem = refs[count + 2 * weights + 3 :]
    pairs = (*zip(vectors, scratch), (visible, seen_s), *zip(matrices, matrix_o))
    copies = [pltpu.make_async_copy(a, b, sem.at[i]) for i, (a, b) in enumerate(pairs)]
    for copy in copies:
        copy.start()
    for copy in copies[: count + 1]:
        copy.wait()
    width = vec_o.shape[1]
    lanes = 128
    row = 0
    for s in scratch:
        for j in range(s.shape[0]):
            at = (row + j) * lanes
            vec_o[at // width : at // width + 1, at % width : at % width + lanes] = s[j : j + 1]
        row += s.shape[0]
    slots = seen_s.shape[1]
    slot = lax.broadcasted_iota(jnp.int32, (1, slots), 1)
    for n in range(mine):
        side = sides[place[0] * mine + n]
        inside = (slot // GRID < side) & (slot % GRID < side)
        bias = jnp.where(inside & (seen_s[pl.ds(place[0] * mine + n, 1), :] == 1), 0.0, NEG_BIG)
        for out, entry in ((bias_o, bias), (valid_o, jnp.where(inside, 1.0, 0.0))):
            out[n * slots : (n + 1) * slots, :] = jnp.broadcast_to(entry, (lanes, slots)).T
    for copy in copies[count + 1 :]:
        copy.wait()


def prepare(place, grid_side, visible, vectors, matrices, bands):
    images, slots = visible.shape
    mine = images // bands
    width = vectors[0].shape[0]
    vectors = [in_hbm(entry.reshape(-1, 128)) for entry in vectors]
    rows = sum(entry.shape[0] for entry in vectors) * 128 // width
    flat = struct(mine * slots, 128, dtype=F32)
    ref = pl.BlockSpec(memory_space=pl.ANY)
    return pl.pallas_call(
        functools.partial(prepare_kernel, mine=mine, count=len(vectors), weights=len(matrices)),
        out_shape=[struct(rows, width, dtype=F32), flat, flat] + [struct(*entry.shape) for entry in matrices],
        in_specs=[SM, SM] + [ref] * (len(vectors) + len(matrices) + 1),
        out_specs=[VM] * (len(matrices) + 3),
        scratch_shapes=[pltpu.VMEM(entry.shape, F32) for entry in vectors]
        + [pltpu.VMEM(visible.shape, jnp.int32), pltpu.SemaphoreType.DMA((len(vectors) + len(matrices) + 1,))],
        compiler_params=pltpu.CompilerParams(vmem_limit_bytes=4 * 2**20),
        cost_estimate=pl.CostEstimate(flops=1000, bytes_accessed=1000, transcendentals=0),
    )(place, grid_side, in_hbm(visible), *vectors, *(in_hbm(entry) for entry in matrices))


def repeat(entry, width):
    return jnp.concatenate([entry] * (width // entry.shape[1]), 1)


def forward_kernel(
    place, parts, bias, vec, w_qkv, w_out, w_up,
    x_o, normed_o, q_o, k_o, v_o, p_o, att_o, branch_o, mid_o, normed2_o, hidden_o, slope_o, *, bands,
):
    mine = parts.shape[0] // bands
    rows, width = x_o.shape
    slots = rows // mine
    x_o[...] = whole_images(parts, bands)
    xhat, _ = norm_parts(x_o[...].astype(F32))
    normed_o[...] = (xhat * vec[G1 : G1 + 1] + vec[C1 : C1 + 1]).astype(BF16)
    normed = normed_o[...]
    queries = (dot(normed, w_qkv[:, :width]) + vec[Q_BIAS : Q_BIAS + 1]).astype(BF16)
    q_o[...] = (queries.astype(F32) * HEAD**-0.5).astype(BF16)
    k_o[...] = dot(normed, w_qkv[:, width : 2 * width]).astype(BF16)
    v_o[...] = (dot(normed, w_qkv[:, 2 * width :]) + vec[V_BIAS : V_BIAS + 1]).astype(BF16)
    pairs = width // (2 * HEAD)
    for n in range(mine):
        rs = slice(n * slots, (n + 1) * slots)
        mask = repeat(bias[rs, :], slots)
        for pr in range(pairs):
            cs = slice(pr * 2 * HEAD, (pr + 1) * 2 * HEAD)
            q, k, v = q_o[rs, cs], k_o[rs, cs], v_o[rs, cs]
            total = None
            for h in range(2):
                s = dot(pick(k, h), q, NT) + mask
                e = jnp.exp(s - jnp.max(s, 0, keepdims=True))
                p = (e * (1.0 / jnp.sum(e, 0, keepdims=True))).astype(BF16)
                p_o[(n * pairs + pr) * 2 + h] = p
                part = dot(p, pick(v, h), TN)
                total = part if total is None else total + part
            att_o[rs, cs] = total.astype(BF16)
    branch = dot(att_o[...], w_out[...]) + vec[B_OUT : B_OUT + 1]
    branch_o[...] = branch.astype(BF16)
    middle = x_o[...].astype(F32) + vec[S_ATTN : S_ATTN + 1] * branch
    mid_o[...] = middle
    xhat2, _ = norm_parts(middle)
    normed2_o[...] = (xhat2 * vec[G2 : G2 + 1] + vec[C2 : C2 + 1]).astype(BF16)
    for j in range(hidden_o.shape[1] // width):
        js = slice(j * width, (j + 1) * width)
        pre = dot(normed2_o[...], w_up[:, js]) + vec[B_UP + j : B_UP + j + 1]
        cdf = 0.5 + 0.5 * lax.erf(0.5**0.5 * pre)
        bell = jnp.exp2((-0.5 / math.log(2.0)) * (pre * pre))
        hidden_o[:, js] = (pre * cdf).astype(BF16)
        slope_o[:, js] = (cdf + ((0.5 / math.pi) ** 0.5 * pre) * bell).astype(BF16)


def forward(place, parts, bias, vec, w_qkv, w_out, w_up, bands, **keys):
    total, band_rows, width = parts.shape
    rows, slots = total * band_rows, bands * band_rows
    mine = total // bands
    row, wide = struct(rows, width), struct(rows, w_up.shape[1])
    p = struct(mine * width // HEAD, slots, slots)
    outs = [row, row, row, row, row, p, row, row, struct(rows, width, dtype=F32), row, wide, wide]
    kernel = functools.partial(forward_kernel, bands=bands)
    return call(kernel, outs, place, parts, bias, vec, w_qkv, w_out, w_up, limit=20, **keys)


def sums(entry):
    return jnp.sum(entry, 0, keepdims=True)


def down_kernel(place, parts, valid, vec, hidden, top_o, gm_o, send_o, keep_o, sum_o, *, bands):
    top = repeat(valid[...], gm_o.shape[1]) * whole_images(parts, bands).astype(F32)
    top_o[...] = top.astype(BF16)
    gm_o[...] = (vec[S_MLP : S_MLP + 1] * top).astype(BF16)
    sum_o[...] = sums(gm_o[...].astype(F32))
    blocks, rows, _ = send_o.shape
    first = place[1] == 0
    for i in range(blocks // 2):
        at = i * 4 * rows
        grad = dot(hidden[:, at : at + 4 * rows], gm_o[...], TN).astype(BF16)
        for x in range(2):
            to = (2 * i + x) ^ place[2]
            one, two = grad[x * rows : (x + 1) * rows], grad[(2 + x) * rows : (3 + x) * rows]
            keep_o[to] = jnp.where(first, one, two)
            send_o[to] = jnp.where(first, two, one)


def down(place, parts, valid, vec, hidden, blocks, bands, **keys):
    rows, ff = hidden.shape
    width = vec.shape[1]
    part = struct(blocks, ff // blocks // 2, width)
    outs = [struct(rows, width), struct(rows, width), part, part, struct(1, width, dtype=F32)]
    return call(functools.partial(down_kernel, bands=bands), outs, place, parts, valid, vec, hidden, **keys)


def cut_rows(place, left, right, send_o, keep_o, tile):
    blocks, rows, _ = send_o.shape
    half = right.shape[1] // 2
    for target, core in ((send_o, 1 - place[1]), (keep_o, place[1])):
        for j in range(half // tile):
            at = pl.multiple_of(core * half + j * tile, 128)
            grad = dot(left[...], right[:, pl.ds(at, tile)], TN).astype(BF16)
            for i in range(blocks):
                target[i ^ place[2], :, j * tile : (j + 1) * tile] = grad[i * rows : (i + 1) * rows]


def up_kernel(place, gm, slope, w_down, normed2, dpre_o, send_o, keep_o, sum_o):
    ff = slope.shape[1]
    tile = gm.shape[1]
    for j in range(ff // tile):
        js = slice(j * tile, (j + 1) * tile)
        grad = (dot(gm[...], w_down[js, :], NT) * slope[:, js].astype(F32)).astype(BF16)
        dpre_o[:, js] = grad
        sum_o[j : j + 1] = sums(grad.astype(F32))
    cut_rows(place, normed2, dpre_o, send_o, keep_o, ff // 4)


def up(place, gm, slope, w_down, normed2, blocks, **keys):
    rows, ff = slope.shape
    width = gm.shape[1]
    part = struct(blocks, width // blocks, ff // 2)
    outs = [struct(rows, ff), part, part, struct(ff // width, width, dtype=F32)]
    return call(up_kernel, outs, place, gm, slope, w_down, normed2, limit=11, **keys)


def out_kernel(place, dpre, w_up, mid, top, vec, branch, w_out, dmid_o, db_o, datt_o, sum_o):
    grad = dot(dpre[...], w_up[...], NT)
    xhat, inverse = norm_parts(mid[...])
    sum_o[0:1] = sums(grad * xhat)
    sum_o[1:2] = sums(grad)
    dmid = top[...].astype(F32) + norm_back(grad, vec[G2 : G2 + 1], xhat, inverse)
    dmid_o[...] = dmid
    sum_o[2:3] = sums(dmid * branch[...].astype(F32))
    db_o[...] = (vec[S_ATTN : S_ATTN + 1] * dmid).astype(BF16)
    sum_o[3:4] = sums(db_o[...].astype(F32))
    datt_o[...] = dot(db_o[...], w_out[...], NT).astype(BF16)


def attention_out(place, dpre, w_up, mid, top, vec, branch, w_out, **keys):
    rows, width = mid.shape
    row = struct(rows, width)
    outs = [struct(rows, width, dtype=F32), row, row, struct(4, width, dtype=F32)]
    return call(out_kernel, outs, place, dpre, w_up, mid, top, vec, branch, w_out, limit=11, **keys)


def attention_kernel(place, q, k, v, p, datt, dproj_o, sum_o):
    rows, width = q.shape
    slots = p.shape[1]
    pairs = width // (2 * HEAD)
    for n in range(rows // slots):
        rs = slice(n * slots, (n + 1) * slots)
        for pr in range(pairs):
            cs = slice(pr * 2 * HEAD, (pr + 1) * 2 * HEAD)
            qp, kp, vp, da = q[rs, cs], k[rs, cs], v[rs, cs], datt[rs, cs]
            dq = dk = dv = None
            for h in range(2):
                weights = p[(n * pairs + pr) * 2 + h]
                probs = weights.astype(F32)
                dw = dot(pick(vp, h), da, NT)
                ds = (probs * (dw - jnp.sum(probs * dw, 0, keepdims=True))).astype(BF16)
                a = dot(ds, pick(kp, h), TN)
                b = dot(ds, pick(qp, h))
                c = dot(weights, pick(da, h))
                dq, dk, dv = (a, b, c) if dq is None else (dq + a, dk + b, dv + c)
            dproj_o[rs, pr * 128 : pr * 128 + 128] = (dq * HEAD**-0.5).astype(BF16)
            dproj_o[rs, width + pr * 128 : width + pr * 128 + 128] = dk.astype(BF16)
            dproj_o[rs, 2 * width + pr * 128 : 2 * width + pr * 128 + 128] = dv.astype(BF16)
    sum_o[0:1] = sums(dproj_o[:, :width].astype(F32))
    sum_o[1:2] = sums(dproj_o[:, 2 * width :].astype(F32))


def attention(place, q, k, v, p, datt, **keys):
    rows, width = q.shape
    outs = [struct(rows, 3 * width), struct(2, width, dtype=F32)]
    return call(attention_kernel, outs, place, q, k, v, p, datt, **keys)


def qkv_kernel(place, normed, dproj, att, db, qs_o, qk_o, os_o, ok_o):
    cut_rows(place, normed, dproj, qs_o, qk_o, 384)
    cut_rows(place, att, db, os_o, ok_o, 384)


def qkv(place, normed, dproj, att, db, blocks, **keys):
    width = normed.shape[1]
    wide, part = struct(blocks, width // blocks, 3 * width // 2), struct(blocks, width // blocks, width // 2)
    return call(qkv_kernel, [wide, wide, part, part], place, normed, dproj, att, db, limit=11, **keys)


def input_kernel(place, dproj, w_qkv, x, dmid, vec, out, sum_o, *, bands):
    grad = dot(dproj[...], w_qkv[...], NT)
    xhat, inverse = norm_parts(x[...].astype(F32))
    sum_o[0:1] = sums(grad * xhat)
    sum_o[1:2] = sums(grad)
    split_bands((dmid[...] + norm_back(grad, vec[G1 : G1 + 1], xhat, inverse)).astype(BF16), out, bands)


def input_back(place, dproj, w_qkv, x, dmid, vec, shape, bands, **keys):
    outs = [struct(*shape), struct(2, x.shape[1], dtype=F32)]
    return call(functools.partial(input_kernel, bands=bands), outs, place, dproj, w_qkv, x, dmid, vec, **keys)


def output_kernel(place, hidden, w_down, mid, top, valid, vec, out, sum_o, *, bands):
    branch = dot(hidden[...], w_down[...]) + vec[B_DOWN : B_DOWN + 1]
    sum_o[...] = sums(top[...].astype(F32) * branch)
    result = repeat(valid[...], mid.shape[1]) * (mid[...] + vec[S_MLP : S_MLP + 1] * branch)
    split_bands(result.astype(BF16), out, bands)


def output_rows(place, hidden, w_down, mid, top, valid, vec, shape, bands, **keys):
    outs = [struct(*shape), struct(1, mid.shape[1], dtype=F32)]
    kernel = functools.partial(output_kernel, bands=bands)
    return call(kernel, outs, place, hidden, w_down, mid, top, valid, vec, **keys)


CHAINS = {
    "d": [
        (("x", "y", "z0", "z1"), ("y", "z0", "z1", "x"), [(0, 0, 768)]),
    ],
    "u": [
        (("z0", "x", "y", "z1"), ("z1", "x", "y", "z0"), [(0, 0, 1536)]),
    ],
    "ko": [
        (("z0", "y", "x", "z1"), ("y", "x", "z1", "z0"), [(0, 0, 896)]),
        (("z1", "x", "z0", "y"), ("y", "z0", "x", "z1"), [(0, 896, 1152), (1, 0, 384), (2, 0, 128)]),
    ],
}
PLAN = [
    "fwd",
    "down",
    "up",
    "outp",
    [("u", "c"), ("d", "c")],
    "out1",
    "attn",
    "qkvo",
    "inp",
    [("d", ("ch", 0))],
    "pack",
    [("u", ("ch", 0)), ("ko", "c")],
    [("d", ("ch", 0))],
    [("ko", ("ch", 0))],
    [("u", ("ch", 0))],
    [("ko", ("ch", 1))],
    [("ko", ("ch", 0))],
    [("d", ("ch", 0))],
    [("ko", ("ch", 1))],
    [("u", ("ch", 0))],
    [("ko", ("ch", 0))],
    [("ko", ("ch", 1))],
    [("d", ("ch", 0))],
    [("u", ("ch", 0))],
    [("ko", ("ch", 0))],
    [("ko", ("ch", 1))],
    [("d", "X")],
    [("d", "C")],
    [("u", "X")],
    [("ko", "X")],
    [("u", "C")],
    [("ko", "C")],
]


def small_rows(s_q, s_i, s_o, s_bu, s_bd, s_m):
    first = [(s_q, [0]), (s_q, [1]), (s_o, [3]), (s_i, [0]), (s_i, [1]), (s_o, [0]), (s_o, [1])]
    return first, [(s_bu, range(s_bu.shape[0])), (s_bd, [0]), (s_o, [2]), (s_m, [0])]


def pack_kernel(place, *refs):
    *entries, out = refs
    blocks, _, lanes = out.shape
    out[...] = jnp.zeros_like(out)
    for x, entry in enumerate(small_rows(*entries)):
        flats = [jnp.concatenate([ref[j : j + 1] for j in which], 1) for ref, which in entry]
        for i in range(blocks // 2):
            row = 0
            for flat in flats:
                size = flat.shape[1] // (blocks // 2)
                for at in range(0, size, lanes):
                    n = min(lanes, size - at)
                    value = flat[:, i * size + at : i * size + at + n].astype(BF16)
                    out[(2 * i + x) ^ place[2], row : row + 1, :n] = value
                    row += 1


def swap(entry, axis, mask):
    size = lax.axis_size(axis)
    return lax.ppermute(entry, axis, [(i, i ^ mask) for i in range(size)])


BITS = {"x": 1, "y": 2, "z0": 4, "z1": 8}


def swap_by_core(entry, axes):
    bands = lax.axis_size("band")
    pairs = []
    for img in range(lax.axis_size("img")):
        for band in range(bands):
            bit = BITS[axes[band & 1]]
            to = (img ^ (bit >> 1)) * bands + (band ^ (2 * (bit & 1)))
            pairs.append((img * bands + band, to))
    return lax.ppermute(entry, ("img", "band"), pairs)


def split_labels(labels, axis):
    bit = BITS[axis]
    keep = [at for at, label in enumerate(labels) if not label & bit]
    send = [labels.index(labels[at] | bit) for at in keep]
    return keep, send, [labels[at] for at in keep]


def total(*entries):
    result = entries[0].astype(F32)
    for entry in entries[1:]:
        result = result + entry.astype(F32)
    return result


class Job:
    def __init__(self, entries, outs, body, after):
        self.entries, self.outs, self.body, self.after = entries, outs, body, after


def fold(place, jobs, token):
    def kernel(place_ref, *refs):
        at, out_at = 0, sum(len(job.entries) for job in jobs)
        for job in jobs:
            n, m = len(job.entries), len(job.outs)
            job.body(place_ref, refs[at : at + n], refs[out_at : out_at + m])
            at, out_at = at + n, out_at + m

    entries = [entry for job in jobs for entry in job.entries]
    *outs, token = call(kernel, [out for job in jobs for out in job.outs], place, *entries, limit=8, token=token)
    for job in jobs:
        job.after(outs[: len(job.outs)])
        outs = outs[len(job.outs) :]
    return token


def step_job(table, sources, segments, labels, axes, name, after):
    cuts = [split_labels(labels[core], axes[core]) for core in range(2)]
    rows = sources[0][0].shape[1]
    width = sum(high - low for _, low, high in segments)
    part = struct(len(cuts[0][0]), rows, width)
    counts = [len(source) for source in sources]

    def body(place, refs, outs):
        groups = []
        at = 0
        for count in counts:
            groups.append(refs[at : at + count])
            at += count
        for which, out in enumerate(outs):
            for to in range(part.shape[0]):
                one, two = cuts[0][which][to], cuts[1][which][to]
                index = one if one == two else jnp.where(place[1] == 0, one, two)
                col = 0
                for source, low, high in segments:
                    value = total(*(ref[index, :, low:high] for ref in groups[source]))
                    out[to, :, col : col + high - low] = value.astype(BF16)
                    col += high - low

    def then(outs):
        keep, send = outs
        after([keep, swap_by_core(send, axes)], [cut[2] for cut in cuts])

    return Job([entry for source in sources for entry in source], [part, part], body, then)


class Gradient:
    def __init__(self, place, sources, chains, finish):
        self.place, self.sources, self.chains, self.finish = place, sources, chains, finish
        self.jobs = {}
        self.done = {}
        self.result = None

    def first(self):
        jobs = []
        for which, (one, two, segments) in enumerate(self.chains):
            jobs.append(
                step_job(
                    self.place, self.sources, segments, [list(range(16))] * 2, (one[0], two[0]), None,
                    functools.partial(self.arrive, which, 1),
                )
            )
        return jobs

    def arrive(self, which, at, entries, labels):
        one, two, _ = self.chains[which]
        if at < len(one):
            segments = [(0, 0, entries[0].shape[2])]
            self.jobs["ch", which] = step_job(
                self.place, [entries], segments, labels, (one[at], two[at]), None,
                functools.partial(self.arrive, which, at + 1),
            )
        else:
            self.done[which] = entries

    def take(self, name):
        if name == "c":
            return self.first()
        if isinstance(name, tuple) and name not in self.jobs:
            entries = self.done[name[1]]
            if len(self.done) < len(self.chains) or self.parked_left(name[1]):
                return [self.park(name[1], entries)]
            return [self.merge()]
        return [self.jobs.pop(name)]

    def parked_left(self, which):
        return any(len(entries) == 2 for at, entries in self.done.items() if at != which)

    def park(self, which, entries):
        def body(place, refs, outs):
            outs[0][...] = total(*(ref[...] for ref in refs)).astype(BF16)

        def after(outs):
            self.done[which] = outs

        return Job(entries, [struct(*entries[0].shape)], body, after)

    def merge(self):
        groups = [self.done[which] for which in range(len(self.chains))]
        rows = groups[0][0].shape[1]
        widths = [group[0].shape[2] for group in groups]

        def body(place, refs, outs):
            at = col = 0
            for group, width in zip(groups, widths):
                outs[0][:, col : col + width] = total(*(ref[0] for ref in refs[at : at + len(group)])).astype(BF16)
                at, col = at + len(group), col + width

        def after(outs):
            self.cross([outs[0], swap(outs[0], "band", 2)])

        return Job([entry for group in groups for entry in group], [struct(rows, sum(widths))], body, after)

    def merge_name(self):
        return ("ch", 0)

    def cross(self, entries):
        def body(place, refs, outs):
            outs[0][place[3]] = refs[0][...]
            outs[0][1 - place[3]] = refs[1][...]

        def after(outs):
            entries = [outs[0], swap(outs[0], "band", 1)]
            self.jobs["C"] = Job(entries, self.finish[0], self.finish[1], self.finished)

        self.jobs["X"] = Job(entries, [struct(2, *entries[0].shape)], body, after)

    def finished(self, outs):
        self.result = outs


def by_rows(place, refs, outs):
    rows = refs[0].shape[1]
    for core, ref in ((place[1], refs[0]), (1 - place[1], refs[1])):
        for x in range(2):
            outs[0][pl.ds(pl.multiple_of((2 * core + x) * rows, 8), rows), :] = ref[x].astype(F32)


def by_columns(segments):
    def body(place, refs, outs):
        rows = refs[0].shape[1]
        for core, ref in ((place[1], refs[0]), (1 - place[1], refs[1])):
            col = 0
            for to, low, high in segments:
                half = outs[to].shape[1] // 2
                at = pl.multiple_of(core * half + low, 128)
                for x in range(2):
                    value = ref[x, :, col : col + high - low].astype(F32)
                    outs[to][x * rows : (x + 1) * rows, pl.ds(at, high - low)] = value
                col += high - low

    return body


def reduce_plain(pair, by_core):
    send, keep = pair
    if by_core:
        keep, send = (entry.reshape(8, -1, entry.shape[2]) for entry in (keep, send))
        grad = jnp.concatenate([keep, send], 1)
    else:
        grad = jnp.concatenate([keep, send], 2)
    grad = grad.astype(F32).reshape(-1, grad.shape[2])
    part = lax.psum_scatter(grad, "img", scatter_dimension=0, tiled=True)
    return lax.psum(part.astype(BF16), "band").astype(F32)


def shards(
    tokens, cotangent, grid_side, visible, w_qkv, q_bias, v_bias, w_out, b_out, ln1_gain, ln1_shift,
    ln2_gain, ln2_shift, w_up, b_up, w_down, b_down, scale_attn, scale_mlp,
):
    width = tokens.shape[2]
    ff = w_up.shape[1]
    bands, imgs = lax.axis_size("band"), lax.axis_size("img")
    band, img = lax.axis_index("band"), lax.axis_index("img")
    fast = imgs == 8 and bands == 4
    blocks = 16
    zero = jnp.zeros_like(band)
    place = [band, band & 1, img * 2 + (band >> 1), band >> 1] if fast else [band, zero, zero, zero]
    place = jnp.stack(place).astype(jnp.int32)

    def exchange(entry):
        return lax.all_to_all(entry, "band", 0, 0, tiled=True)

    got_x = exchange(tokens)
    got_c = exchange(cotangent)
    vectors = (q_bias, v_bias, b_out, ln1_gain, ln1_shift, ln2_gain, ln2_shift, b_down, scale_attn, scale_mlp, b_up)
    vec, bias, valid, wv_qkv, wv_out, wv_up = prepare(place, grid_side, visible, vectors, (w_qkv, w_out, w_up), bands)

    s = {}
    plan = PLAN if fast else [step for step in PLAN if isinstance(step, str)]
    grads = {}
    token = None
    for step in plan:
        if step == "fwd":
            x, normed, q, k, v, p, att, branch, mid, normed2, hidden, slope, token = forward(
                place, got_x, bias, vec, wv_qkv, wv_out, wv_up, bands
            )
        elif step == "down":
            top, gm, *d_pair, s["bd"], token = down(place, got_c, valid, vec, hidden, blocks, bands, token=token)
            if fast:
                finish = ([struct(w_down.shape[0] // imgs, width, dtype=F32)], by_rows)
                sources = [(d_pair[1], swap(d_pair[0], "band", 1))]
                grads["d"] = Gradient(place, sources, CHAINS["d"], finish)
        elif step == "up":
            dpre, *u_pair, s["bu"], token = up(place, gm, slope, w_down, normed2, blocks, token=token)
            if fast:
                segments = [segment for chain in CHAINS["u"] for segment in chain[2]]
                finish = ([struct(width // imgs, ff, dtype=F32)], by_columns(segments))
                sources = [(u_pair[1], swap(u_pair[0], "band", 1))]
                grads["u"] = Gradient(place, sources, CHAINS["u"], finish)
        elif step == "outp":
            out, s["m"], token = output_rows(
                place, hidden, w_down, mid, top, valid, vec, tokens.shape, bands, token=token
            )
            output = exchange(out)
        elif step == "out1":
            dmid, db, datt, s["o"], token = attention_out(
                place, dpre, wv_up, mid, top, vec, branch, wv_out, token=token
            )
        elif step == "attn":
            dproj, s["q"], token = attention(place, q, k, v, p, datt, token=token)
        elif step == "qkvo":
            *q_pair, o_send, o_keep, token = qkv(place, normed, dproj, att, db, blocks, token=token)
            if fast:
                ko = [(q_pair[1], swap(q_pair[0], "band", 1)), (o_keep, swap(o_send, "band", 1))]
        elif step == "inp":
            grad_in, s["i"], token = input_back(place, dproj, wv_qkv, x, dmid, vec, tokens.shape, bands, token=token)
            input_grad = exchange(grad_in)
        elif step == "pack":
            small = [s[name] for name in ("q", "i", "o", "bu", "bd", "m")]
            if fast:
                packed, token = call(
                    pack_kernel, [struct(blocks, width // blocks, 128)], place, *small, limit=2, token=token
                )
                ko.append((packed, swap(packed, "band", 1)))
                shapes = [struct(width // imgs, n, dtype=F32) for n in (3 * width, width)]
                segments = [segment for chain in CHAINS["ko"] for segment in chain[2]]
                grads["ko"] = Gradient(
                    place, ko, CHAINS["ko"], (shapes + [struct(16, 128, dtype=F32)], with_small(segments))
                )
        else:
            jobs = [job for name, which in step for job in grads[name].take(which)]
            token = fold(place, jobs, token)
    first, second = small_rows(*small)
    if fast:
        (grad_w_down,), (grad_w_up,) = grads["d"].result, grads["u"].result
        grad_w_qkv, grad_w_out, sums_ = grads["ko"].result
        size = width // imgs
        shares = [sums_[i, :size] for i in range(len(first))]
        rows = ff // imgs // 128
        at = len(first)
        shares += [sums_[at : at + rows].reshape(-1)] + [sums_[at + rows + i, :size] for i in range(3)]
    else:
        grad_w_down = reduce_plain(d_pair, True)
        grad_w_up = reduce_plain(u_pair, False)
        grad_w_out = reduce_plain((o_send, o_keep), False)
        grad_w_qkv = reduce_plain(q_pair, False)
        flat = [jnp.concatenate([ref[j] for j in which]) for ref, which in first + second]
        joined = jnp.concatenate([entry.reshape(imgs, -1) for entry in flat], 1)
        joined = lax.dynamic_index_in_dim(lax.psum(joined, ("img", "band")), img, 0, False)
        shares, at = [], 0
        for entry in flat:
            size = entry.shape[0] // imgs
            shares.append(joined[at : at + size])
            at += size
    (s_qb, s_vb, s_bo, s_g1, s_c1, s_g2, s_c2, s_bu, s_bd, s_sa, s_sm) = shares
    return (
        output, input_grad, grad_w_qkv, s_qb, s_vb, grad_w_out, s_bo, s_g1, s_c1, s_g2, s_c2, grad_w_up, s_bu,
        grad_w_down, s_bd, s_sa, s_sm,
    )


def with_small(segments):
    columns = by_columns([segment for segment in segments if segment[0] < 2])

    def body(place, refs, outs):
        columns(place, refs, outs)
        at = sum(high - low for source, low, high in segments if source < 2)
        out = outs[2]
        out[...] = jnp.zeros_like(out)
        out[0:7, :] = refs[0][0, 0:7, at : at + 128].astype(F32)
        out[7:16, :] = refs[0][1, 0:9, at : at + 128].astype(F32)

    return body


def solution(mesh):
    cut = P("img", "band", None)
    in_specs = (cut, cut, P("img"), P("img", None)) + (P(),) * 15
    row, vec = P("img", None), P("img")
    out_specs = (cut, cut, row, vec, vec, row, vec, vec, vec, vec, vec, row, vec, row, vec, vec, vec)
    return jax.shard_map(shards, mesh=mesh, in_specs=in_specs, out_specs=out_specs, check_vma=False)
```

```python
import functools
import math

import jax
import jax.numpy as jnp
from jax import lax
from jax.experimental import pallas as pl
from jax.experimental.pallas import tpu as pltpu
from jax.sharding import PartitionSpec as P

HEAD = 64
GRID = 16
NEG_BIG = -1e30
EPSILON = 1e-06
F32 = jnp.float32
BF16 = jnp.bfloat16
SCALE = 4e9
VM = pl.BlockSpec(memory_space=pltpu.VMEM)
SM = pl.BlockSpec(memory_space=pltpu.SMEM)
NN, NT, TN = ((1,), (0,)), ((1,), (1,)), ((0,), (0,))
Q_BIAS, V_BIAS, B_OUT, G1, C1, G2, C2, B_DOWN, S_ATTN, S_MLP, B_UP = range(11)


def dot(left, right, dims=NN):
    return lax.dot_general(left, right, (dims, ((), ())), preferred_element_type=F32)


def struct(*shape, dtype=BF16):
    return jax.ShapeDtypeStruct(shape, dtype)


def estimate(cost):
    return pl.CostEstimate(flops=int(cost * SCALE), bytes_accessed=1000, transcendentals=0)


def call(kernel, outs, place, *args, limit=8, token=None, cost=1.0):
    count = len(args)

    def body(place_ref, *refs):
        kernel(place_ref, *refs[:count], *refs[count + 1 : -1])
        refs[-1][...] = jnp.zeros_like(refs[-1])

    token = jnp.zeros((1, 128), F32) if token is None else token
    return pl.pallas_call(
        body,
        out_shape=[*outs, struct(1, 128, dtype=F32)],
        in_specs=[SM] + [VM] * (count + 1),
        out_specs=[VM] * (len(outs) + 1),
        compiler_params=pltpu.CompilerParams(vmem_limit_bytes=limit * 2**20),
        cost_estimate=estimate(cost),
    )(place, *args, token)


def norm_parts(entry):
    center = entry - jnp.mean(entry, -1, keepdims=True)
    spread = jnp.mean(center * center, -1, keepdims=True)
    inverse = lax.rsqrt(spread + EPSILON)
    return center * inverse, inverse


def norm_back(grad, gain, xhat, inverse):
    scaled = grad * gain
    inner = scaled - jnp.mean(scaled, -1, keepdims=True)
    return (inner - xhat * jnp.mean(scaled * xhat, -1, keepdims=True)) * inverse


def pick(entry, head):
    lane = lax.broadcasted_iota(jnp.int32, entry.shape, 1)
    return jnp.where((lane < HEAD) if head == 0 else (lane >= HEAD), entry, jnp.zeros_like(entry))


def cut_kernel(place, entry, *refs, mine):
    *outs, sem = refs
    copies = [
        pltpu.make_async_copy(entry.at[pl.ds((place[0] ^ q) * mine, mine)], out, sem.at[q]) for q, out in enumerate(outs)
    ]
    for copy in copies:
        copy.start()
    for copy in copies:
        copy.wait()


def cut(place, entry, bands):
    images, band_rows, width = entry.shape
    mine = images // bands
    return pl.pallas_call(
        functools.partial(cut_kernel, mine=mine),
        out_shape=[struct(mine, band_rows, width)] * bands,
        in_specs=[SM, pl.BlockSpec(memory_space=pl.ANY)],
        out_specs=[VM] * bands,
        scratch_shapes=[pltpu.SemaphoreType.DMA((bands,))],
        compiler_params=pltpu.CompilerParams(vmem_limit_bytes=2**20),
        cost_estimate=estimate(1.0),
    )(place, in_hbm(entry))


def whole_images(place, parts, out):
    mine, band_rows, _ = parts[0].shape
    for q, part in enumerate(parts):
        for n in range(mine):
            at = pl.multiple_of((n * len(parts) + (place[0] ^ q)) * band_rows, 16)
            out[pl.ds(at, band_rows), :] = part[n]


def split_bands(place, rows_s, far, near):
    _, mine, band_rows, _ = far.shape
    bands = rows_s.shape[0] // mine // band_rows
    for q in range(bands):
        for n in range(mine):
            at = pl.multiple_of((n * bands + (place[0] ^ q)) * band_rows, 16)
            (far if q & 2 else near)[q & 1, n] = rows_s[pl.ds(at, band_rows), :]


def in_hbm(entry):
    return pltpu.with_memory_space_constraint(entry, pltpu.HBM)


def prepare_kernel(place, sides, visible, *refs, mine, count, weights):
    vectors, matrices = refs[:count], refs[count : count + weights]
    vec_o, bias_o, valid_o, *matrix_o = refs[count + weights : count + 2 * weights + 3]
    *scratch, seen_s, sem = refs[count + 2 * weights + 3 :]
    pairs = (*zip(vectors, scratch), (visible, seen_s), *zip(matrices, matrix_o))
    copies = [pltpu.make_async_copy(a, b, sem.at[i]) for i, (a, b) in enumerate(pairs)]
    for copy in copies:
        copy.start()
    for copy in copies[: count + 1]:
        copy.wait()
    width = vec_o.shape[1]
    lanes = 128
    row = 0
    for s in scratch:
        for j in range(s.shape[0]):
            at = (row + j) * lanes
            vec_o[at // width : at // width + 1, at % width : at % width + lanes] = s[j : j + 1]
        row += s.shape[0]
    slots = seen_s.shape[1]
    slot = lax.broadcasted_iota(jnp.int32, (1, slots), 1)
    for n in range(mine):
        side = sides[place[0] * mine + n]
        inside = (slot // GRID < side) & (slot % GRID < side)
        bias = jnp.where(inside & (seen_s[pl.ds(place[0] * mine + n, 1), :] == 1), 0.0, NEG_BIG)
        for out, entry in ((bias_o, bias), (valid_o, jnp.where(inside, 1.0, 0.0))):
            out[n * slots : (n + 1) * slots, :] = jnp.broadcast_to(entry, (lanes, slots)).T
    for copy in copies[count + 1 :]:
        copy.wait()


def prepare(place, grid_side, visible, vectors, matrices, bands):
    images, slots = visible.shape
    mine = images // bands
    width = vectors[0].shape[0]
    vectors = [in_hbm(entry.reshape(-1, 128)) for entry in vectors]
    rows = sum(entry.shape[0] for entry in vectors) * 128 // width
    flat = struct(mine * slots, 128, dtype=F32)
    ref = pl.BlockSpec(memory_space=pl.ANY)
    return pl.pallas_call(
        functools.partial(prepare_kernel, mine=mine, count=len(vectors), weights=len(matrices)),
        out_shape=[struct(rows, width, dtype=F32), flat, flat] + [struct(*entry.shape) for entry in matrices],
        in_specs=[SM, SM] + [ref] * (len(vectors) + len(matrices) + 1),
        out_specs=[VM] * (len(matrices) + 3),
        scratch_shapes=[pltpu.VMEM(entry.shape, F32) for entry in vectors]
        + [pltpu.VMEM(visible.shape, jnp.int32), pltpu.SemaphoreType.DMA((len(vectors) + len(matrices) + 1,))],
        compiler_params=pltpu.CompilerParams(vmem_limit_bytes=4 * 2**20),
        cost_estimate=estimate(5.0),
    )(place, grid_side, in_hbm(visible), *vectors, *(in_hbm(entry) for entry in matrices))


def repeat(entry, width):
    return jnp.concatenate([entry] * (width // entry.shape[1]), 1)


def forward_kernel(place, *refs, bands):
    parts = refs[:bands]
    (bias, vec, w_qkv, w_out, w_up,
     x_o, normed_o, q_o, k_o, v_o, p_o, att_o, branch_o, mid_o, normed2_o, hidden_o, slope_o) = refs[bands:]
    mine = parts[0].shape[0]
    rows, width = x_o.shape
    slots = rows // mine
    whole_images(place, parts, x_o)
    xhat, _ = norm_parts(x_o[...].astype(F32))
    normed_o[...] = (xhat * vec[G1 : G1 + 1] + vec[C1 : C1 + 1]).astype(BF16)
    normed = normed_o[...]
    queries = (dot(normed, w_qkv[:, :width]) + vec[Q_BIAS : Q_BIAS + 1]).astype(BF16)
    q_o[...] = (queries.astype(F32) * HEAD**-0.5).astype(BF16)
    k_o[...] = dot(normed, w_qkv[:, width : 2 * width]).astype(BF16)
    v_o[...] = (dot(normed, w_qkv[:, 2 * width :]) + vec[V_BIAS : V_BIAS + 1]).astype(BF16)
    pairs = width // (2 * HEAD)
    for n in range(mine):
        rs = slice(n * slots, (n + 1) * slots)
        mask = repeat(bias[rs, :], slots)
        for pr in range(pairs):
            cs = slice(pr * 2 * HEAD, (pr + 1) * 2 * HEAD)
            q, k, v = q_o[rs, cs], k_o[rs, cs], v_o[rs, cs]
            total = None
            for h in range(2):
                s = dot(pick(k, h), q, NT) + mask
                e = jnp.exp(s - jnp.max(s, 0, keepdims=True))
                p = (e * (1.0 / jnp.sum(e, 0, keepdims=True))).astype(BF16)
                p_o[(n * pairs + pr) * 2 + h] = p
                part = dot(p, pick(v, h), TN)
                total = part if total is None else total + part
            att_o[rs, cs] = total.astype(BF16)
    branch = dot(att_o[...], w_out[...]) + vec[B_OUT : B_OUT + 1]
    branch_o[...] = branch.astype(BF16)
    middle = x_o[...].astype(F32) + vec[S_ATTN : S_ATTN + 1] * branch
    mid_o[...] = middle
    xhat2, _ = norm_parts(middle)
    normed2_o[...] = (xhat2 * vec[G2 : G2 + 1] + vec[C2 : C2 + 1]).astype(BF16)
    tile = 256
    for j in range(hidden_o.shape[1] // tile):
        js = slice(j * tile, (j + 1) * tile)
        row, col = B_UP + j * tile // width, j * tile % width
        pre = dot(normed2_o[...], w_up[:, js]) + vec[row : row + 1, col : col + tile]
        cdf = 0.5 + 0.5 * lax.erf(0.5**0.5 * pre)
        bell = jnp.exp2((-0.5 / math.log(2.0)) * (pre * pre))
        hidden_o[:, js] = (pre * cdf).astype(BF16)
        slope_o[:, js] = (cdf + ((0.5 / math.pi) ** 0.5 * pre) * bell).astype(BF16)


def forward(place, parts, bias, vec, w_qkv, w_out, w_up, **keys):
    mine, band_rows, width = parts[0].shape
    bands = len(parts)
    slots = bands * band_rows
    rows = mine * slots
    row, wide = struct(rows, width), struct(rows, w_up.shape[1])
    p = struct(mine * width // HEAD, slots, slots)
    outs = [row, row, row, row, row, p, row, row, struct(rows, width, dtype=F32), row, wide, wide]
    kernel = functools.partial(forward_kernel, bands=bands)
    return call(kernel, outs, place, *parts, bias, vec, w_qkv, w_out, w_up, limit=10, cost=13.6, **keys)


def sums(entry):
    return jnp.sum(entry, 0, keepdims=True)


def down_kernel(place, *refs, bands):
    parts = refs[:bands]
    valid, vec, hidden, top_o, gm_o, send_o, keep_o, sum_o = refs[bands:]
    whole_images(place, parts, top_o)
    top = repeat(valid[...], gm_o.shape[1]) * top_o[...].astype(F32)
    top_o[...] = top.astype(BF16)
    gm_o[...] = (vec[S_MLP : S_MLP + 1] * top).astype(BF16)
    sum_o[...] = sums(gm_o[...].astype(F32))
    blocks, rows, _ = send_o.shape
    first = place[1] == 0
    for i in range(blocks // 2):
        at = i * 4 * rows
        grad = dot(hidden[:, at : at + 4 * rows], gm_o[...], TN).astype(BF16)
        for x in range(2):
            to = (2 * i + x) ^ place[2]
            one, two = grad[x * rows : (x + 1) * rows], grad[(2 + x) * rows : (3 + x) * rows]
            keep_o[to] = jnp.where(first, one, two)
            send_o[to] = jnp.where(first, two, one)


def down(place, parts, valid, vec, hidden, blocks, **keys):
    rows, ff = hidden.shape
    width = vec.shape[1]
    part = struct(blocks, ff // blocks // 2, width)
    outs = [struct(rows, width), struct(rows, width), part, part, struct(1, width, dtype=F32)]
    kernel = functools.partial(down_kernel, bands=len(parts))
    return call(kernel, outs, place, *parts, valid, vec, hidden, cost=3.6, **keys)


def cut_rows(place, left, right, send_o, keep_o, tile):
    blocks, rows, _ = send_o.shape
    half = right.shape[1] // 2
    for target, core in ((send_o, 1 - place[1]), (keep_o, place[1])):
        for j in range(half // tile):
            at = pl.multiple_of(core * half + j * tile, 128)
            grad = dot(left[...], right[:, pl.ds(at, tile)], TN).astype(BF16)
            for i in range(blocks):
                target[i ^ place[2], :, j * tile : (j + 1) * tile] = grad[i * rows : (i + 1) * rows]


def up_kernel(place, gm, slope, w_down, normed2, dpre_o, send_o, keep_o, sum_o):
    ff = slope.shape[1]
    tile = gm.shape[1]
    for j in range(ff // tile):
        js = slice(j * tile, (j + 1) * tile)
        grad = (dot(gm[...], w_down[js, :], NT) * slope[:, js].astype(F32)).astype(BF16)
        dpre_o[:, js] = grad
        sum_o[j : j + 1] = sums(grad.astype(F32))
    cut_rows(place, normed2, dpre_o, send_o, keep_o, ff // 4)


def up(place, gm, slope, w_down, normed2, blocks, **keys):
    rows, ff = slope.shape
    width = gm.shape[1]
    part = struct(blocks, width // blocks, ff // 2)
    outs = [struct(rows, ff), part, part, struct(ff // width, width, dtype=F32)]
    return call(up_kernel, outs, place, gm, slope, w_down, normed2, limit=11, cost=6.0, **keys)


def out_kernel(place, dpre, w_up, mid, top, vec, branch, w_out, dmid_o, db_o, datt_o, sum_o):
    grad = dot(dpre[...], w_up[...], NT)
    xhat, inverse = norm_parts(mid[...])
    sum_o[0:1] = sums(grad * xhat)
    sum_o[1:2] = sums(grad)
    dmid = top[...].astype(F32) + norm_back(grad, vec[G2 : G2 + 1], xhat, inverse)
    dmid_o[...] = dmid
    sum_o[2:3] = sums(dmid * branch[...].astype(F32))
    db_o[...] = (vec[S_ATTN : S_ATTN + 1] * dmid).astype(BF16)
    sum_o[3:4] = sums(db_o[...].astype(F32))
    datt_o[...] = dot(db_o[...], w_out[...], NT).astype(BF16)


def attention_out(place, dpre, w_up, mid, top, vec, branch, w_out, **keys):
    rows, width = mid.shape
    row = struct(rows, width)
    outs = [struct(rows, width, dtype=F32), row, row, struct(4, width, dtype=F32)]
    return call(out_kernel, outs, place, dpre, w_up, mid, top, vec, branch, w_out, limit=11, cost=6.0, **keys)


def attention_kernel(place, q, k, v, p, datt, dproj_o, sum_o):
    rows, width = q.shape
    slots = p.shape[1]
    pairs = width // (2 * HEAD)
    for n in range(rows // slots):
        rs = slice(n * slots, (n + 1) * slots)
        for pr in range(pairs):
            cs = slice(pr * 2 * HEAD, (pr + 1) * 2 * HEAD)
            qp, kp, vp, da = q[rs, cs], k[rs, cs], v[rs, cs], datt[rs, cs]
            dq = dk = dv = None
            for h in range(2):
                weights = p[(n * pairs + pr) * 2 + h]
                probs = weights.astype(F32)
                dw = dot(pick(vp, h), da, NT)
                ds = (probs * (dw - jnp.sum(probs * dw, 0, keepdims=True))).astype(BF16)
                a = dot(ds, pick(kp, h), TN)
                b = dot(ds, pick(qp, h))
                c = dot(weights, pick(da, h))
                dq, dk, dv = (a, b, c) if dq is None else (dq + a, dk + b, dv + c)
            dproj_o[rs, pr * 128 : pr * 128 + 128] = (dq * HEAD**-0.5).astype(BF16)
            dproj_o[rs, width + pr * 128 : width + pr * 128 + 128] = dk.astype(BF16)
            dproj_o[rs, 2 * width + pr * 128 : 2 * width + pr * 128 + 128] = dv.astype(BF16)
    sum_o[0:1] = sums(dproj_o[:, :width].astype(F32))
    sum_o[1:2] = sums(dproj_o[:, 2 * width :].astype(F32))


def attention(place, q, k, v, p, datt, **keys):
    rows, width = q.shape
    outs = [struct(rows, 3 * width), struct(2, width, dtype=F32)]
    return call(attention_kernel, outs, place, q, k, v, p, datt, cost=6.4, **keys)


def qkv_kernel(place, normed, dproj, att, db, qs_o, qk_o, os_o, ok_o):
    cut_rows(place, normed, dproj, qs_o, qk_o, 384)
    cut_rows(place, att, db, os_o, ok_o, 384)


def qkv(place, normed, dproj, att, db, blocks, **keys):
    width = normed.shape[1]
    wide, part = struct(blocks, width // blocks, 3 * width // 2), struct(blocks, width // blocks, width // 2)
    return call(qkv_kernel, [wide, wide, part, part], place, normed, dproj, att, db, limit=11, cost=4.0, **keys)


def input_kernel(place, dproj, w_qkv, x, dmid, vec, far, near, sum_o, rows_o):
    grad = dot(dproj[...], w_qkv[...], NT)
    xhat, inverse = norm_parts(x[...].astype(F32))
    sum_o[0:1] = sums(grad * xhat)
    sum_o[1:2] = sums(grad)
    rows_o[...] = (dmid[...] + norm_back(grad, vec[G1 : G1 + 1], xhat, inverse)).astype(BF16)
    split_bands(place, rows_o, far, near)


def input_back(place, dproj, w_qkv, x, dmid, vec, bands, slots, **keys):
    rows, width = x.shape
    half = struct(2, rows // slots, slots // bands, width)
    outs = [half, half, struct(2, width, dtype=F32), struct(rows, width)]
    far, near, total, _, token = call(input_kernel, outs, place, dproj, w_qkv, x, dmid, vec, cost=3.2, **keys)
    return far, near, total, token


def output_kernel(place, hidden, w_down, mid, top, valid, vec, far, near, sum_o, rows_o):
    branch = dot(hidden[...], w_down[...]) + vec[B_DOWN : B_DOWN + 1]
    sum_o[...] = sums(top[...].astype(F32) * branch)
    result = repeat(valid[...], mid.shape[1]) * (mid[...] + vec[S_MLP : S_MLP + 1] * branch)
    rows_o[...] = result.astype(BF16)
    split_bands(place, rows_o, far, near)


def output_rows(place, hidden, w_down, mid, top, valid, vec, bands, slots, **keys):
    rows, width = mid.shape
    half = struct(2, rows // slots, slots // bands, width)
    outs = [half, half, struct(1, width, dtype=F32), struct(rows, width)]
    args = (hidden, w_down, mid, top, valid, vec)
    far, near, total, _, token = call(output_kernel, outs, place, *args, cost=3.4, **keys)
    return far, near, total, token


CHAINS = {
    "d": [
        (("z0", "y", "z1", "x"), ("x", "z0", "y", "z1"), [(0, 0, 768)]),
    ],
    "u": [
        (("y", "z0", "x", "z1"), ("z0", "x", "y", "z1"), [(0, 0, 1536)]),
    ],
    "ko": [
        (("y", "x", "z0", "z1"), ("x", "z0", "y", "z1"), [(0, 0, 768)]),
        (("z0", "x", "y", "z1"), ("y", "z0", "x", "z1"), [(0, 768, 1152), (1, 0, 384), (2, 0, 128)]),
    ],
}
PLAN = [
    "fwd",
    "down",
    "up",
    "outp",
    [("d", "c")],
    [("u", "c")],
    "out1",
    "attn",
    [("o", "x")],
    "inp",
    [("o", "c")],
    "pack",
    [("d", ("ch", 0))],
    "qkvo",
    [("u", ("ch", 0))],
    [("i", "x")],
    [("d", ("ch", 0))],
    [("i", "c")],
    [("ko", "c")],
    [("u", ("ch", 0))],
    [("d", ("ch", 0))],
    [("ko", ("ch", 0))],
    [("ko", ("ch", 1))],
    [("d", ("ch", 0))],
    [("ko", ("ch", 0)), ("u", ("ch", 0))],
    [("ko", ("ch", 1))],
    [("ko", ("ch", 0))],
    [("d", "X")],
    [("ko", ("ch", 1))],
    [("d", "C")],
    [("u", ("ch", 0))],
    [("ko", ("ch", 0))],
    [("ko", ("ch", 1))],
    [("u", "X")],
    [("u", "C")],
    [("ko", "X")],
    [("ko", "C")],
]


def small_rows(s_q, s_i, s_o, s_bu, s_bd, s_m):
    first = [(s_q, [0]), (s_q, [1]), (s_o, [3]), (s_i, [0]), (s_i, [1]), (s_o, [0]), (s_o, [1])]
    return first, [(s_bu, range(s_bu.shape[0])), (s_bd, [0]), (s_o, [2]), (s_m, [0])]


def pack_kernel(place, *refs):
    *entries, out = refs
    blocks, _, lanes = out.shape
    out[...] = jnp.zeros_like(out)
    for x, entry in enumerate(small_rows(*entries)):
        flats = [jnp.concatenate([ref[j : j + 1] for j in which], 1) for ref, which in entry]
        for i in range(blocks // 2):
            row = 0
            for flat in flats:
                size = flat.shape[1] // (blocks // 2)
                for at in range(0, size, lanes):
                    n = min(lanes, size - at)
                    value = flat[:, i * size + at : i * size + at + n].astype(BF16)
                    out[(2 * i + x) ^ place[2], row : row + 1, :n] = value
                    row += 1


def swap(entry, axis, mask):
    size = lax.axis_size(axis)
    return lax.ppermute(entry, axis, [(i, i ^ mask) for i in range(size)])


BITS = {"x": 1, "y": 2, "z0": 4, "z1": 8}


def swap_by_core(entry, axes):
    bands = lax.axis_size("band")
    pairs = []
    for img in range(lax.axis_size("img")):
        for band in range(bands):
            bit = BITS[axes[band & 1]]
            to = (img ^ (bit >> 1)) * bands + (band ^ (2 * (bit & 1)))
            pairs.append((img * bands + band, to))
    return lax.ppermute(entry, ("img", "band"), pairs)


def split_labels(labels, axis):
    bit = BITS[axis]
    keep = [at for at, label in enumerate(labels) if not label & bit]
    send = [labels.index(labels[at] | bit) for at in keep]
    return keep, send, [labels[at] for at in keep]


def total(*entries):
    result = entries[0].astype(F32)
    for entry in entries[1:]:
        result = result + entry.astype(F32)
    return result


class Job:
    def __init__(self, entries, outs, body, after):
        self.entries, self.outs, self.body, self.after = entries, outs, body, after


def fold(place, jobs, token):
    def kernel(place_ref, *refs):
        at, out_at = 0, sum(len(job.entries) for job in jobs)
        for job in jobs:
            n, m = len(job.entries), len(job.outs)
            job.body(place_ref, refs[at : at + n], refs[out_at : out_at + m])
            at, out_at = at + n, out_at + m

    entries = [entry for job in jobs for entry in job.entries]
    *outs, token = call(kernel, [out for job in jobs for out in job.outs], place, *entries, limit=8, token=token)
    for job in jobs:
        job.after(outs[: len(job.outs)])
        outs = outs[len(job.outs) :]
    return token


def step_job(sources, segments, labels, axes, after):
    cuts = [split_labels(labels[core], axes[core]) for core in range(2)]
    rows = sources[0][0].shape[1]
    width = sum(high - low for _, low, high in segments)
    part = struct(len(cuts[0][0]), rows, width)
    counts = [len(source) for source in sources]

    def body(place, refs, outs):
        groups = []
        at = 0
        for count in counts:
            groups.append(refs[at : at + count])
            at += count
        for which, out in enumerate(outs):
            for to in range(part.shape[0]):
                one, two = cuts[0][which][to], cuts[1][which][to]
                index = one if one == two else jnp.where(place[1] == 0, one, two)
                col = 0
                for source, low, high in segments:
                    value = total(*(ref[index, :, low:high] for ref in groups[source]))
                    out[to, :, col : col + high - low] = value.astype(BF16)
                    col += high - low

    def then(outs):
        keep, send = outs
        after([keep, swap_by_core(send, axes)], [cut[2] for cut in cuts])

    return Job([entry for source in sources for entry in source], [part, part], body, then)


class Gradient:
    def __init__(self, sources, chains, finish):
        self.sources, self.chains, self.finish = sources, chains, finish
        self.jobs = {}
        self.done = {}
        self.result = None

    def first(self):
        jobs = []
        for which, (one, two, segments) in enumerate(self.chains):
            jobs.append(
                step_job(
                    self.sources, segments, [list(range(16))] * 2, (one[0], two[0]),
                    functools.partial(self.arrive, which, 1),
                )
            )
        return jobs

    def arrive(self, which, at, entries, labels):
        one, two, _ = self.chains[which]
        if at < len(one):
            segments = [(0, 0, entries[0].shape[2])]
            self.jobs["ch", which] = step_job(
                [entries], segments, labels, (one[at], two[at]),
                functools.partial(self.arrive, which, at + 1),
            )
        else:
            self.done[which] = entries

    def take(self, names):
        ended = [name[1] for name in names if isinstance(name, tuple) and name not in self.jobs]
        jobs = []
        for name in names:
            if name == "c":
                jobs += self.first()
            elif name in self.jobs:
                jobs.append(self.jobs.pop(name))
        if ended:
            left = [at for at in range(len(self.chains)) if at not in ended and len(self.done.get(at, "..")) > 1]
            jobs += [self.park(at) for at in ended] if left else [self.merge()]
        return jobs

    def park(self, which):
        entries = self.done[which]

        def body(place, refs, outs):
            outs[0][...] = total(*(ref[...] for ref in refs)).astype(BF16)

        def after(outs):
            self.done[which] = outs

        return Job(entries, [struct(*entries[0].shape)], body, after)

    def merge(self):
        groups = [self.done[which] for which in range(len(self.chains))]
        rows = groups[0][0].shape[1]
        widths = [group[0].shape[2] for group in groups]

        def body(place, refs, outs):
            at = col = 0
            for group, width in zip(groups, widths):
                outs[0][:, col : col + width] = total(*(ref[0] for ref in refs[at : at + len(group)])).astype(BF16)
                at, col = at + len(group), col + width

        def after(outs):
            self.cross([outs[0], swap(outs[0], "band", 2)])

        return Job([entry for group in groups for entry in group], [struct(rows, sum(widths))], body, after)

    def cross(self, entries):
        def body(place, refs, outs):
            outs[0][place[3]] = refs[0][...]
            outs[0][1 - place[3]] = refs[1][...]

        def after(outs):
            entries = [outs[0], swap(outs[0], "band", 1)]
            self.jobs["C"] = Job(entries, self.finish[0], self.finish[1], self.finished)

        self.jobs["X"] = Job(entries, [struct(2, *entries[0].shape)], body, after)

    def finished(self, outs):
        self.result = outs


class Exchange:
    def __init__(self, far, near):
        self.jobs, self.result = {}, None
        got = swap(far, "band", 2)

        def relay(place, refs, outs):
            outs[0][0] = refs[0][1]
            outs[0][1] = refs[1][1]

        def after(outs):
            entries = [near, got, swap(outs[0], "band", 1)]
            self.jobs["c"] = Job(entries, [struct(4 * far.shape[1], *far.shape[2:])], self.put, self.finished)

        self.jobs["x"] = Job([near, got], [struct(*far.shape)], relay, after)

    def put(self, place, refs, outs):
        near, far, core = refs
        mine = near.shape[1]
        for q, value in enumerate((near[0], core[0], far[0], core[1])):
            outs[0][pl.ds((place[0] ^ q) * mine, mine)] = value

    def finished(self, outs):
        self.result = outs[0]

    def take(self, names):
        return [self.jobs.pop(name) for name in names]


def in_order(place, own, other):
    first = place[1] == 0
    return jnp.where(first, own, other).astype(F32), jnp.where(first, other, own).astype(F32)


def by_rows(place, refs, outs):
    rows = refs[0].shape[1]
    for x in range(2):
        for core, value in enumerate(in_order(place, refs[0][x], refs[1][x])):
            at = (2 * core + x) * rows
            outs[0][at : at + rows, :] = value


def by_columns(segments):
    def body(place, refs, outs):
        rows = refs[0].shape[1]
        for x in range(2):
            col = 0
            for to, low, high in segments:
                half = outs[to].shape[1] // 2
                to_col = col + high - low
                pair = in_order(place, refs[0][x, :, col:to_col], refs[1][x, :, col:to_col])
                for core, value in enumerate(pair):
                    outs[to][x * rows : (x + 1) * rows, core * half + low : core * half + high] = value
                col = to_col

    return body


def reduce_plain(pair, by_core):
    send, keep = pair
    if by_core:
        keep, send = (entry.reshape(8, -1, entry.shape[2]) for entry in (keep, send))
        grad = jnp.concatenate([keep, send], 1)
    else:
        grad = jnp.concatenate([keep, send], 2)
    grad = grad.astype(F32).reshape(-1, grad.shape[2])
    part = lax.psum_scatter(grad, "img", scatter_dimension=0, tiled=True)
    return lax.psum(part.astype(BF16), "band").astype(F32)


def shards(
    tokens, cotangent, grid_side, visible, w_qkv, q_bias, v_bias, w_out, b_out, ln1_gain, ln1_shift,
    ln2_gain, ln2_shift, w_up, b_up, w_down, b_down, scale_attn, scale_mlp,
):
    width = tokens.shape[2]
    ff = w_up.shape[1]
    bands, imgs = lax.axis_size("band"), lax.axis_size("img")
    band, img = lax.axis_index("band"), lax.axis_index("img")
    fast = imgs == 8 and bands == 4
    blocks = 16
    zero = jnp.zeros_like(band)
    place = [band, band & 1, img * 2 + (band >> 1), band >> 1] if fast else [band, zero, zero, zero]
    place = jnp.stack(place).astype(jnp.int32)

    def to_images(entry):
        parts = cut(place, entry, bands)
        return [swap(part, "band", q) if q else part for q, part in enumerate(parts)]

    got_x = to_images(tokens)
    got_c = to_images(cotangent)
    vectors = (q_bias, v_bias, b_out, ln1_gain, ln1_shift, ln2_gain, ln2_shift, b_down, scale_attn, scale_mlp, b_up)
    vec, bias, valid, wv_qkv, wv_out, wv_up = prepare(place, grid_side, visible, vectors, (w_qkv, w_out, w_up), bands)

    s = {}
    exchanges = [[("i", "x"), ("o", "x")], [("i", "c"), ("o", "c")]]
    plan = PLAN if fast else [step for step in PLAN if isinstance(step, str)] + exchanges
    grads, ko = {}, {}
    token = None
    for step in plan:
        if step == "fwd":
            x, normed, q, k, v, p, att, branch, mid, normed2, hidden, slope, token = forward(
                place, got_x, bias, vec, wv_qkv, wv_out, wv_up
            )
        elif step == "down":
            top, gm, *d_pair, s["bd"], token = down(place, got_c, valid, vec, hidden, blocks, token=token)
            if fast:
                finish = ([struct(w_down.shape[0] // imgs, width, dtype=F32)], by_rows)
                sources = [(d_pair[1], swap(d_pair[0], "band", 1))]
                grads["d"] = Gradient(sources, CHAINS["d"], finish)
        elif step == "up":
            dpre, *u_pair, s["bu"], token = up(place, gm, slope, w_down, normed2, blocks, token=token)
            if fast:
                segments = [segment for chain in CHAINS["u"] for segment in chain[2]]
                finish = ([struct(width // imgs, ff, dtype=F32)], by_columns(segments))
                sources = [(u_pair[1], swap(u_pair[0], "band", 1))]
                grads["u"] = Gradient(sources, CHAINS["u"], finish)
        elif step == "outp":
            args = (hidden, w_down, mid, top, valid, vec)
            far, near, s["m"], token = output_rows(place, *args, bands, visible.shape[1], token=token)
            grads["o"] = Exchange(far, near)
        elif step == "out1":
            dmid, db, datt, s["o"], token = attention_out(
                place, dpre, w_up, mid, top, vec, branch, w_out, token=token
            )
        elif step == "attn":
            dproj, s["q"], token = attention(place, q, k, v, p, datt, token=token)
        elif step == "qkvo":
            *q_pair, o_send, o_keep, token = qkv(place, normed, dproj, att, db, blocks, token=token)
            if fast:
                ko["q"] = q_pair[1], swap(q_pair[0], "band", 1)
                ko["o"] = o_keep, swap(o_send, "band", 1)
        elif step == "inp":
            args = (dproj, w_qkv, x, dmid, vec)
            far, near, s["i"], token = input_back(place, *args, bands, visible.shape[1], token=token)
            grads["i"] = Exchange(far, near)
        elif step == "pack":
            small = [s[name] for name in ("q", "i", "o", "bu", "bd", "m")]
            if fast:
                packed, token = call(
                    pack_kernel, [struct(blocks, width // blocks, 128)], place, *small, limit=2, token=token
                )
                ko["s"] = packed, swap(packed, "band", 1)
        else:
            if ("ko", "c") in step:
                shapes = [struct(width // imgs, n, dtype=F32) for n in (3 * width, width)]
                segments = [segment for chain in CHAINS["ko"] for segment in chain[2]]
                finish = (shapes + [struct(16, 128, dtype=F32)], with_small(segments))
                grads["ko"] = Gradient([ko["q"], ko["o"], ko["s"]], CHAINS["ko"], finish)
            names = list(dict.fromkeys(name for name, _ in step))
            jobs = [job for name in names for job in grads[name].take([what for to, what in step if to == name])]
            token = fold(place, jobs, token)
    output, input_grad = grads["o"].result, grads["i"].result
    first, second = small_rows(*small)
    if fast:
        (grad_w_down,), (grad_w_up,) = grads["d"].result, grads["u"].result
        grad_w_qkv, grad_w_out, sums_ = grads["ko"].result
        size = width // imgs
        shares = [sums_[i, :size] for i in range(len(first))]
        rows = ff // imgs // 128
        at = len(first)
        shares += [sums_[at : at + rows].reshape(-1)] + [sums_[at + rows + i, :size] for i in range(3)]
    else:
        grad_w_down = reduce_plain(d_pair, True)
        grad_w_up = reduce_plain(u_pair, False)
        grad_w_out = reduce_plain((o_send, o_keep), False)
        grad_w_qkv = reduce_plain(q_pair, False)
        flat = [jnp.concatenate([ref[j] for j in which]) for ref, which in first + second]
        joined = jnp.concatenate([entry.reshape(imgs, -1) for entry in flat], 1)
        joined = lax.dynamic_index_in_dim(lax.psum(joined, ("img", "band")), img, 0, False)
        shares, at = [], 0
        for entry in flat:
            size = entry.shape[0] // imgs
            shares.append(joined[at : at + size])
            at += size
    (s_qb, s_vb, s_bo, s_g1, s_c1, s_g2, s_c2, s_bu, s_bd, s_sa, s_sm) = shares
    return (
        output, input_grad, grad_w_qkv, s_qb, s_vb, grad_w_out, s_bo, s_g1, s_c1, s_g2, s_c2, grad_w_up, s_bu,
        grad_w_down, s_bd, s_sa, s_sm,
    )


def with_small(segments):
    columns = by_columns([segment for segment in segments if segment[0] < 2])

    def body(place, refs, outs):
        columns(place, refs, outs)
        at = sum(high - low for source, low, high in segments if source < 2)
        out = outs[2]
        out[...] = jnp.zeros_like(out)
        out[0:7, :] = refs[0][0, 0:7, at : at + 128].astype(F32)
        out[7:16, :] = refs[0][1, 0:9, at : at + 128].astype(F32)

    return body


def solution(mesh):
    cut = P("img", "band", None)
    in_specs = (cut, cut, P("img"), P("img", None)) + (P(),) * 15
    row, vec = P("img", None), P("img")
    out_specs = (cut, cut, row, vec, vec, row, vec, vec, vec, vec, vec, row, vec, row, vec, vec, vec)
    return jax.shard_map(shards, mesh=mesh, in_specs=in_specs, out_specs=out_specs, check_vma=False)
```

```python
import functools
import math

import jax
import jax.numpy as jnp
from jax import lax
from jax.experimental import pallas as pl
from jax.experimental.pallas import tpu as pltpu
from jax.sharding import PartitionSpec as P

HEAD = 64
GRID = 16
NEG_BIG = -1e30
EPSILON = 1e-06
F32 = jnp.float32
BF16 = jnp.bfloat16
SCALE = 4e9
VM = pl.BlockSpec(memory_space=pltpu.VMEM)
SM = pl.BlockSpec(memory_space=pltpu.SMEM)
NN, NT, TN = ((1,), (0,)), ((1,), (1,)), ((0,), (0,))
Q_BIAS, V_BIAS, B_OUT, G1, C1, G2, C2, B_DOWN, S_ATTN, S_MLP, B_UP = range(11)


def dot(left, right, dims=NN):
    return lax.dot_general(left, right, (dims, ((), ())), preferred_element_type=F32)


def struct(*shape, dtype=BF16):
    return jax.ShapeDtypeStruct(shape, dtype)


def estimate(cost):
    return pl.CostEstimate(flops=int(cost * SCALE), bytes_accessed=1000, transcendentals=0)


def call(kernel, outs, place, *args, limit=8, token=None, cost=1.0):
    count = len(args)

    def body(place_ref, *refs):
        kernel(place_ref, *refs[:count], *refs[count + 1 : -1])
        refs[-1][...] = jnp.zeros_like(refs[-1])

    token = jnp.zeros((1, 128), F32) if token is None else token
    return pl.pallas_call(
        body,
        out_shape=[*outs, struct(1, 128, dtype=F32)],
        in_specs=[SM] + [VM] * (count + 1),
        out_specs=[VM] * (len(outs) + 1),
        compiler_params=pltpu.CompilerParams(vmem_limit_bytes=limit * 2**20),
        cost_estimate=estimate(cost),
    )(place, *args, token)


def norm_parts(entry):
    center = entry - jnp.mean(entry, -1, keepdims=True)
    spread = jnp.mean(center * center, -1, keepdims=True)
    inverse = lax.rsqrt(spread + EPSILON)
    return center * inverse, inverse


def norm_back(grad, gain, xhat, inverse):
    scaled = grad * gain
    inner = scaled - jnp.mean(scaled, -1, keepdims=True)
    return (inner - xhat * jnp.mean(scaled * xhat, -1, keepdims=True)) * inverse


def stack_heads(entry):
    lane = lax.broadcasted_iota(jnp.int32, entry.shape, 1)
    zero = jnp.zeros_like(entry)
    return jnp.concatenate([jnp.where(lane < HEAD, entry, zero), jnp.where(lane >= HEAD, entry, zero)], 0)


def cut_kernel(place, entry, *refs, mine):
    *outs, sem = refs
    copies = [
        pltpu.make_async_copy(entry.at[pl.ds((place[0] ^ q) * mine, mine)], out, sem.at[q]) for q, out in enumerate(outs)
    ]
    for copy in copies:
        copy.start()
    for copy in copies:
        copy.wait()


def cut(place, entry, bands):
    images, band_rows, width = entry.shape
    mine = images // bands
    return pl.pallas_call(
        functools.partial(cut_kernel, mine=mine),
        out_shape=[struct(mine, band_rows, width)] * bands,
        in_specs=[SM, pl.BlockSpec(memory_space=pl.ANY)],
        out_specs=[VM] * bands,
        scratch_shapes=[pltpu.SemaphoreType.DMA((bands,))],
        compiler_params=pltpu.CompilerParams(vmem_limit_bytes=2**20),
        cost_estimate=estimate(1.0),
    )(place, in_hbm(entry))


def whole_images(place, parts, out):
    mine, band_rows, _ = parts[0].shape
    for q, part in enumerate(parts):
        for n in range(mine):
            at = pl.multiple_of((n * len(parts) + (place[0] ^ q)) * band_rows, 16)
            out[pl.ds(at, band_rows), :] = part[n]


def split_bands(place, rows_s, far, near):
    _, mine, band_rows, _ = far.shape
    bands = rows_s.shape[0] // mine // band_rows
    for q in range(bands):
        for n in range(mine):
            at = pl.multiple_of((n * bands + (place[0] ^ q)) * band_rows, 16)
            (far if q & 2 else near)[q & 1, n] = rows_s[pl.ds(at, band_rows), :]


def in_hbm(entry):
    return pltpu.with_memory_space_constraint(entry, pltpu.HBM)


def prepare_kernel(place, sides, visible, *refs, mine, count, weights):
    vectors, matrices = refs[:count], refs[count : count + weights]
    vec_o, bias_o, valid_o, *matrix_o = refs[count + weights : count + 2 * weights + 3]
    *scratch, seen_s, sem = refs[count + 2 * weights + 3 :]
    pairs = (*zip(vectors, scratch), (visible, seen_s), *zip(matrices, matrix_o))
    copies = [pltpu.make_async_copy(a, b, sem.at[i]) for i, (a, b) in enumerate(pairs)]
    for copy in copies:
        copy.start()
    for copy in copies[: count + 1]:
        copy.wait()
    width = vec_o.shape[1]
    lanes = 128
    row = 0
    for s in scratch:
        for j in range(s.shape[0]):
            at = (row + j) * lanes
            vec_o[at // width : at // width + 1, at % width : at % width + lanes] = s[j : j + 1]
        row += s.shape[0]
    slots = seen_s.shape[1]
    slot = lax.broadcasted_iota(jnp.int32, (1, slots), 1)
    for n in range(mine):
        side = sides[place[0] * mine + n]
        inside = (slot // GRID < side) & (slot % GRID < side)
        bias = jnp.where(inside & (seen_s[pl.ds(place[0] * mine + n, 1), :] == 1), 0.0, NEG_BIG)
        for out, entry in ((bias_o, bias), (valid_o, jnp.where(inside, 1.0, 0.0))):
            out[n * slots : (n + 1) * slots, :] = jnp.broadcast_to(entry, (lanes, slots)).T
    for copy in copies[count + 1 :]:
        copy.wait()


def prepare(place, grid_side, visible, vectors, matrices, bands):
    images, slots = visible.shape
    mine = images // bands
    width = vectors[0].shape[0]
    vectors = [in_hbm(entry.reshape(-1, 128)) for entry in vectors]
    rows = sum(entry.shape[0] for entry in vectors) * 128 // width
    flat = struct(mine * slots, 128, dtype=F32)
    ref = pl.BlockSpec(memory_space=pl.ANY)
    return pl.pallas_call(
        functools.partial(prepare_kernel, mine=mine, count=len(vectors), weights=len(matrices)),
        out_shape=[struct(rows, width, dtype=F32), flat, flat] + [struct(*entry.shape) for entry in matrices],
        in_specs=[SM, SM] + [ref] * (len(vectors) + len(matrices) + 1),
        out_specs=[VM] * (len(matrices) + 3),
        scratch_shapes=[pltpu.VMEM(entry.shape, F32) for entry in vectors]
        + [pltpu.VMEM(visible.shape, jnp.int32), pltpu.SemaphoreType.DMA((len(vectors) + len(matrices) + 1,))],
        compiler_params=pltpu.CompilerParams(vmem_limit_bytes=4 * 2**20),
        cost_estimate=estimate(5.0),
    )(place, grid_side, in_hbm(visible), *vectors, *(in_hbm(entry) for entry in matrices))


def repeat(entry, width):
    return jnp.concatenate([entry] * (width // entry.shape[1]), 1)


def forward_kernel(place, *refs, bands):
    parts = refs[:bands]
    (bias, vec, w_qkv, w_out, w_up,
     x_o, normed_o, q_o, k_o, v_o, p_o, att_o, branch_o, mid_o, normed2_o, hidden_o, slope_o) = refs[bands:]
    mine = parts[0].shape[0]
    rows, width = x_o.shape
    slots = rows // mine
    whole_images(place, parts, x_o)
    xhat, _ = norm_parts(x_o[...].astype(F32))
    normed_o[...] = (xhat * vec[G1 : G1 + 1] + vec[C1 : C1 + 1]).astype(BF16)
    normed = normed_o[...]
    queries = (dot(normed, w_qkv[:, :width]) + vec[Q_BIAS : Q_BIAS + 1]).astype(BF16)
    q_o[...] = (queries.astype(F32) * HEAD**-0.5).astype(BF16)
    k_o[...] = dot(normed, w_qkv[:, width : 2 * width]).astype(BF16)
    v_o[...] = (dot(normed, w_qkv[:, 2 * width :]) + vec[V_BIAS : V_BIAS + 1]).astype(BF16)
    pairs = width // (2 * HEAD)
    for n in range(mine):
        rs = slice(n * slots, (n + 1) * slots)
        mask = repeat(bias[rs, :], slots)
        for pr in range(pairs):
            cs = slice(pr * 2 * HEAD, (pr + 1) * 2 * HEAD)
            q, k, v = q_o[rs, cs], k_o[rs, cs], v_o[rs, cs]
            both = dot(stack_heads(k), q, NT).reshape(2, slots, slots) + mask
            e = jnp.exp(both - jnp.max(both, 1, keepdims=True))
            p = (e * (1.0 / jnp.sum(e, 1, keepdims=True))).astype(BF16)
            at = (n * pairs + pr) * 2
            p_o[at : at + 2] = p
            total = dot(p.reshape(2 * slots, slots), stack_heads(v), TN)
            att_o[rs, cs] = total.astype(BF16)
    branch = dot(att_o[...], w_out[...]) + vec[B_OUT : B_OUT + 1]
    branch_o[...] = branch.astype(BF16)
    middle = x_o[...].astype(F32) + vec[S_ATTN : S_ATTN + 1] * branch
    mid_o[...] = middle
    xhat2, _ = norm_parts(middle)
    normed2_o[...] = (xhat2 * vec[G2 : G2 + 1] + vec[C2 : C2 + 1]).astype(BF16)
    tile = 256
    for j in range(hidden_o.shape[1] // tile):
        js = slice(j * tile, (j + 1) * tile)
        row, col = B_UP + j * tile // width, j * tile % width
        pre = dot(normed2_o[...], w_up[:, js]) + vec[row : row + 1, col : col + tile]
        cdf = 0.5 + 0.5 * lax.erf(0.5**0.5 * pre)
        bell = jnp.exp2((-0.5 / math.log(2.0)) * (pre * pre))
        hidden_o[:, js] = (pre * cdf).astype(BF16)
        slope_o[:, js] = (cdf + ((0.5 / math.pi) ** 0.5 * pre) * bell).astype(BF16)


def forward(place, parts, bias, vec, w_qkv, w_out, w_up, **keys):
    mine, band_rows, width = parts[0].shape
    bands = len(parts)
    slots = bands * band_rows
    rows = mine * slots
    row, wide = struct(rows, width), struct(rows, w_up.shape[1])
    p = struct(mine * width // HEAD, slots, slots)
    outs = [row, row, row, row, row, p, row, row, struct(rows, width, dtype=F32), row, wide, wide]
    kernel = functools.partial(forward_kernel, bands=bands)
    return call(kernel, outs, place, *parts, bias, vec, w_qkv, w_out, w_up, limit=10, cost=13.6, **keys)


def sums(entry):
    return jnp.sum(entry, 0, keepdims=True)


def down_kernel(place, *refs, bands):
    parts = refs[:bands]
    valid, vec, hidden, top_o, gm_o, send_o, keep_o, sum_o = refs[bands:]
    whole_images(place, parts, top_o)
    top = repeat(valid[...], gm_o.shape[1]) * top_o[...].astype(F32)
    top_o[...] = top.astype(BF16)
    gm_o[...] = (vec[S_MLP : S_MLP + 1] * top).astype(BF16)
    sum_o[...] = sums(gm_o[...].astype(F32))
    blocks, rows, _ = send_o.shape
    first = place[1] == 0
    for i in range(blocks // 2):
        at = i * 4 * rows
        grad = dot(hidden[:, at : at + 4 * rows], gm_o[...], TN).astype(BF16)
        for x in range(2):
            to = (2 * i + x) ^ place[2]
            one, two = grad[x * rows : (x + 1) * rows], grad[(2 + x) * rows : (3 + x) * rows]
            keep_o[to] = jnp.where(first, one, two)
            send_o[to] = jnp.where(first, two, one)


def down(place, parts, valid, vec, hidden, blocks, **keys):
    rows, ff = hidden.shape
    width = vec.shape[1]
    part = struct(blocks, ff // blocks // 2, width)
    outs = [struct(rows, width), struct(rows, width), part, part, struct(1, width, dtype=F32)]
    kernel = functools.partial(down_kernel, bands=len(parts))
    return call(kernel, outs, place, *parts, valid, vec, hidden, cost=3.6, **keys)


def cut_rows(place, left, right, send_o, keep_o, tile):
    blocks, rows, _ = send_o.shape
    half = right.shape[1] // 2
    for target, core in ((send_o, 1 - place[1]), (keep_o, place[1])):
        for j in range(half // tile):
            at = pl.multiple_of(core * half + j * tile, 128)
            grad = dot(left[...], right[:, pl.ds(at, tile)], TN).astype(BF16)
            for i in range(blocks):
                target[i ^ place[2], :, j * tile : (j + 1) * tile] = grad[i * rows : (i + 1) * rows]


def up_kernel(place, gm, slope, w_down, normed2, dpre_o, send_o, keep_o, sum_o):
    ff = slope.shape[1]
    tile = gm.shape[1]
    for j in range(ff // tile):
        js = slice(j * tile, (j + 1) * tile)
        grad = (dot(gm[...], w_down[js, :], NT) * slope[:, js].astype(F32)).astype(BF16)
        dpre_o[:, js] = grad
        sum_o[j : j + 1] = sums(grad.astype(F32))
    cut_rows(place, normed2, dpre_o, send_o, keep_o, ff // 4)


def up(place, gm, slope, w_down, normed2, blocks, **keys):
    rows, ff = slope.shape
    width = gm.shape[1]
    part = struct(blocks, width // blocks, ff // 2)
    outs = [struct(rows, ff), part, part, struct(ff // width, width, dtype=F32)]
    return call(up_kernel, outs, place, gm, slope, w_down, normed2, limit=11, cost=6.0, **keys)


def out_kernel(place, dpre, w_up, mid, top, vec, branch, w_out, dmid_o, db_o, datt_o, sum_o):
    grad = dot(dpre[...], w_up[...], NT)
    xhat, inverse = norm_parts(mid[...])
    sum_o[0:1] = sums(grad * xhat)
    sum_o[1:2] = sums(grad)
    dmid = top[...].astype(F32) + norm_back(grad, vec[G2 : G2 + 1], xhat, inverse)
    dmid_o[...] = dmid
    sum_o[2:3] = sums(dmid * branch[...].astype(F32))
    db_o[...] = (vec[S_ATTN : S_ATTN + 1] * dmid).astype(BF16)
    sum_o[3:4] = sums(db_o[...].astype(F32))
    datt_o[...] = dot(db_o[...], w_out[...], NT).astype(BF16)


def attention_out(place, dpre, w_up, mid, top, vec, branch, w_out, **keys):
    rows, width = mid.shape
    row = struct(rows, width)
    outs = [struct(rows, width, dtype=F32), row, row, struct(4, width, dtype=F32)]
    return call(out_kernel, outs, place, dpre, w_up, mid, top, vec, branch, w_out, limit=11, cost=6.0, **keys)


def attention_kernel(place, q, k, v, p, datt, dproj_o, sum_o):
    rows, width = q.shape
    slots = p.shape[1]
    pairs = width // (2 * HEAD)
    for n in range(rows // slots):
        rs = slice(n * slots, (n + 1) * slots)
        for pr in range(pairs):
            cs = slice(pr * 2 * HEAD, (pr + 1) * 2 * HEAD)
            qp, kp, vp, da = q[rs, cs], k[rs, cs], v[rs, cs], datt[rs, cs]
            at = (n * pairs + pr) * 2
            weights = p[at : at + 2]
            probs = weights.astype(F32)
            dw = dot(stack_heads(vp), da, NT).reshape(2, slots, slots)
            ds = (probs * (dw - jnp.sum(probs * dw, 1, keepdims=True))).astype(BF16)
            dq = dot(ds.reshape(2 * slots, slots), stack_heads(kp), TN)
            dk = dot(jnp.concatenate([ds[0], ds[1]], 1), stack_heads(qp))
            dv = dot(jnp.concatenate([weights[0], weights[1]], 1), stack_heads(da))
            dproj_o[rs, pr * 128 : pr * 128 + 128] = (dq * HEAD**-0.5).astype(BF16)
            dproj_o[rs, width + pr * 128 : width + pr * 128 + 128] = dk.astype(BF16)
            dproj_o[rs, 2 * width + pr * 128 : 2 * width + pr * 128 + 128] = dv.astype(BF16)
    sum_o[0:1] = sums(dproj_o[:, :width].astype(F32))
    sum_o[1:2] = sums(dproj_o[:, 2 * width :].astype(F32))


def attention(place, q, k, v, p, datt, **keys):
    rows, width = q.shape
    outs = [struct(rows, 3 * width), struct(2, width, dtype=F32)]
    return call(attention_kernel, outs, place, q, k, v, p, datt, cost=6.4, **keys)


def qkv_kernel(place, normed, dproj, att, db, qs_o, qk_o, os_o, ok_o):
    cut_rows(place, normed, dproj, qs_o, qk_o, 384)
    cut_rows(place, att, db, os_o, ok_o, 384)


def qkv(place, normed, dproj, att, db, blocks, **keys):
    width = normed.shape[1]
    wide, part = struct(blocks, width // blocks, 3 * width // 2), struct(blocks, width // blocks, width // 2)
    return call(qkv_kernel, [wide, wide, part, part], place, normed, dproj, att, db, limit=11, cost=4.0, **keys)


def input_kernel(place, dproj, w_qkv, x, dmid, vec, out_far, out_near, far, near, sum_o, rows_o):
    grad = dot(dproj[...], w_qkv[...], NT)
    xhat, inverse = norm_parts(x[...].astype(F32))
    sum_o[0:1] = sums(grad * xhat)
    sum_o[1:2] = sums(grad)
    rows_o[...] = (dmid[...] + norm_back(grad, vec[G1 : G1 + 1], xhat, inverse)).astype(BF16)
    split_bands(place, rows_o, far.at[1], near.at[1])
    far[0] = out_far[...]
    near[0] = out_near[...]


def input_back(place, dproj, w_qkv, x, dmid, vec, out_far, out_near, **keys):
    both = struct(2, *out_far.shape)
    outs = [both, both, struct(2, x.shape[1], dtype=F32), struct(*x.shape)]
    args = (dproj, w_qkv, x, dmid, vec, out_far, out_near)
    far, near, total, _, token = call(input_kernel, outs, place, *args, cost=3.2, **keys)
    return far, near, total, token


def output_kernel(place, hidden, w_down, mid, top, valid, vec, far, near, sum_o, rows_o):
    branch = dot(hidden[...], w_down[...]) + vec[B_DOWN : B_DOWN + 1]
    sum_o[...] = sums(top[...].astype(F32) * branch)
    result = repeat(valid[...], mid.shape[1]) * (mid[...] + vec[S_MLP : S_MLP + 1] * branch)
    rows_o[...] = result.astype(BF16)
    split_bands(place, rows_o, far, near)


def output_rows(place, hidden, w_down, mid, top, valid, vec, bands, slots, **keys):
    rows, width = mid.shape
    half = struct(2, rows // slots, slots // bands, width)
    outs = [half, half, struct(1, width, dtype=F32), struct(rows, width)]
    args = (hidden, w_down, mid, top, valid, vec)
    far, near, total, _, token = call(output_kernel, outs, place, *args, cost=3.4, **keys)
    return far, near, total, token


CHAINS = {
    "d": [
        ((("y",), ("z0",), ("z1",), ("x",)), (("z0",), ("x",), ("y",), ("z1",)), [(0, 0, 768)]),
    ],
    "u": [
        ((("x",), ("z0",), ("y",), ("z1",)), (("z0",), ("y",), ("z1",), ("x",)), [(0, 0, 1536)]),
    ],
    "ko": [
        ((("z0",), ("y",), ("x",), ("z1",)), (("y",), ("x",), ("z0",), ("z1",)), [(0, 0, 1024)]),
        ((("x",), ("y",), ("z1",), ("z0",)), (("x",), ("z0",), ("z1",), ("y",)), [(0, 1024, 1152), (1, 0, 384)]),
    ],
}
PLAN = [
    "fwd",
    "down",
    "up",
    [("d", "c")],
    "out1",
    [("u", "c")],
    "attn",
    "qkvo",
    [("d", ("ch", 0))],
    "outp",
    "inp",
    [("u", ("ch", 0)), ("ko", "c")],
    [("d", ("ch", 0))],
    "pack",
    [("u", ("ch", 0))],
    [("ko", ("ch", 0)), ("ko", ("ch", 1))],
    [("d", ("ch", 0))],
    [("io", "x"), ("u", ("ch", 0))],
    [("ko", ("ch", 0)), ("ko", ("ch", 1))],
    [("d", ("ch", 0)), ("io", "c")],
    [("u", ("ch", 0))],
    [("ko", ("ch", 0))],
    [("ko", ("ch", 1))],
    [("d", "X")],
    [("u", "X")],
    [("ko", ("ch", 0))],
    [("ko", ("ch", 1)), ("d", "C")],
    [("u", "C")],
    [("ko", "X")],
    [("ko", "C")],
]


def small_rows(s_q, s_i, s_o, s_bu, s_bd, s_m):
    return [
        (s_q, [0]), (s_q, [1]), (s_o, [3]), (s_i, [0]), (s_i, [1]), (s_o, [0]), (s_o, [1]),
        (s_bu, range(s_bu.shape[0])), (s_bd, [0]), (s_o, [2]), (s_m, [0]),
    ]


def pack_kernel(place, *refs):
    *entries, out = refs
    blocks, _, lanes = out.shape
    out[...] = jnp.zeros_like(out)
    flats = [jnp.concatenate([ref[j : j + 1] for j in which], 1) for ref, which in small_rows(*entries)]
    for i in range(blocks):
        row = 0
        for flat in flats:
            size = flat.shape[1] // blocks
            for at in range(0, size, lanes):
                n = min(lanes, size - at)
                value = flat[:, i * size + at : i * size + at + n].astype(BF16)
                out[i ^ (place[2] >> 1), row : row + 1, :n] = value
                row += 1


def swap(entry, axis, mask):
    size = lax.axis_size(axis)
    return lax.ppermute(entry, axis, [(i, i ^ mask) for i in range(size)])


BITS = {"x": 1, "y": 2, "z0": 4, "z1": 8}


def swap_by_core(entry, masks):
    bands = lax.axis_size("band")
    pairs = []
    for img in range(lax.axis_size("img")):
        for band in range(bands):
            mask = masks[band & 1]
            to = (img ^ (mask >> 1)) * bands + (band ^ (2 * (mask & 1)))
            pairs.append((img * bands + band, to))
    return lax.ppermute(entry, ("img", "band"), pairs)


def masks_of(axes):
    bits = [BITS[axis] for axis in axes]
    return bits if len(bits) == 1 else [*bits, bits[0] | bits[1]]


def split_labels(labels, axes):
    masks = masks_of(axes)
    every = sum(BITS[axis] for axis in axes)
    keep = [at for at, label in enumerate(labels) if not label & every]
    sent = [[labels.index(labels[at] | mask) for at in keep] for mask in masks]
    return [keep, *sent], [labels[at] for at in keep]


def total(*entries):
    result = entries[0].astype(F32)
    for entry in entries[1:]:
        result = result + entry.astype(F32)
    return result


class Job:
    def __init__(self, entries, outs, body, after):
        self.entries, self.outs, self.body, self.after = entries, outs, body, after


def fold(place, jobs, token):
    def kernel(place_ref, *refs):
        at, out_at = 0, sum(len(job.entries) for job in jobs)
        for job in jobs:
            n, m = len(job.entries), len(job.outs)
            job.body(place_ref, refs[at : at + n], refs[out_at : out_at + m])
            at, out_at = at + n, out_at + m

    entries = [entry for job in jobs for entry in job.entries]
    *outs, token = call(kernel, [out for job in jobs for out in job.outs], place, *entries, limit=8, token=token)
    for job in jobs:
        job.after(outs[: len(job.outs)])
        outs = outs[len(job.outs) :]
    return token


def step_job(sources, segments, labels, axes, after):
    cuts = [split_labels(labels[core], axes[core]) for core in range(2)]
    rows = sources[0][0].shape[1]
    width = sum(high - low for _, low, high in segments)
    part = struct(len(cuts[0][1]), rows, width)
    counts = [len(source) for source in sources]

    def body(place, refs, outs):
        groups = []
        at = 0
        for count in counts:
            groups.append(refs[at : at + count])
            at += count
        for which, out in enumerate(outs):
            for to in range(part.shape[0]):
                one, two = (cut[0][which][to] for cut in cuts)
                index = one if one == two else jnp.where(place[1] == 0, one, two)
                col = 0
                for source, low, high in segments:
                    value = total(*(ref[index, :, low:high] for ref in groups[source]))
                    out[to, :, col : col + high - low] = value.astype(BF16)
                    col += high - low

    def then(outs):
        keep, *sent = outs
        masks = zip(*(masks_of(axes[core]) for core in range(2)))
        after([keep, *(swap_by_core(entry, mask) for entry, mask in zip(sent, masks))], [cut[1] for cut in cuts])

    entries = [entry for source in sources for entry in source]
    return Job(entries, [part] * len(cuts[0][0]), body, then)


class Gradient:
    def __init__(self, sources, chains, finish):
        self.sources, self.chains, self.finish = sources, chains, finish
        self.jobs, self.waiting, self.done = {}, {}, {}
        self.extra = self.result = None

    def first(self):
        jobs = []
        for which, (one, two, segments) in enumerate(self.chains):
            after = functools.partial(self.arrive, which, 1)
            jobs.append(step_job(self.sources, segments, [list(range(16))] * 2, (one[0], two[0]), after))
        return jobs

    def arrive(self, which, at, entries, labels):
        if at < len(self.chains[which][0]):
            self.waiting[which] = at, entries, labels
        else:
            self.done[which] = entries

    def step(self, which):
        at, entries, labels = self.waiting.pop(which)
        one, two, _ = self.chains[which]
        sources, segments = [entries], [(0, 0, entries[0].shape[2])]
        if at == 1 and which == len(self.chains) - 1 and self.extra is not None:
            sources.append([self.extra])
            segments.append((1, 0, self.extra.shape[2]))
        return step_job(sources, segments, labels, (one[at], two[at]), functools.partial(self.arrive, which, at + 1))

    def take(self, names):
        jobs, ended = [], []
        for name in names:
            if name == "c":
                jobs += self.first()
            elif name in self.jobs:
                jobs.append(self.jobs.pop(name))
            elif name[1] in self.waiting:
                jobs.append(self.step(name[1]))
            else:
                ended.append(name[1])
        if ended:
            left = [at for at in range(len(self.chains)) if at not in ended and len(self.done.get(at, "..")) > 1]
            jobs += [self.park(at) for at in ended] if left else [self.merge()]
        return jobs

    def park(self, which):
        entries = self.done[which]

        def body(place, refs, outs):
            outs[0][...] = total(*(ref[...] for ref in refs)).astype(BF16)

        def after(outs):
            self.done[which] = outs

        return Job(entries, [struct(*entries[0].shape)], body, after)

    def merge(self):
        groups = [self.done[which] for which in range(len(self.chains))]
        rows = groups[0][0].shape[1]
        widths = [group[0].shape[2] for group in groups]

        def body(place, refs, outs):
            at = col = 0
            for group, width in zip(groups, widths):
                outs[0][:, col : col + width] = total(*(ref[0] for ref in refs[at : at + len(group)])).astype(BF16)
                at, col = at + len(group), col + width

        def after(outs):
            self.cross([outs[0], swap(outs[0], "band", 2)])

        return Job([entry for group in groups for entry in group], [struct(rows, sum(widths))], body, after)

    def cross(self, entries):
        def body(place, refs, outs):
            outs[0][place[3]] = refs[0][...]
            outs[0][1 - place[3]] = refs[1][...]

        def after(outs):
            entries = [outs[0], swap(outs[0], "band", 1)]
            self.jobs["C"] = Job(entries, self.finish[0], self.finish[1], self.finished)

        self.jobs["X"] = Job(entries, [struct(2, *entries[0].shape)], body, after)

    def finished(self, outs):
        self.result = outs


class Exchange:
    def __init__(self, far, near):
        self.jobs, self.result = {}, None
        got = swap(far, "band", 2)
        count, _, mine, band_rows, width = far.shape

        def relay(place, refs, outs):
            for i in range(count):
                outs[0][i, 0] = refs[0][i, 1]
                outs[0][i, 1] = refs[1][i, 1]

        def after(outs):
            entries = [near, got, swap(outs[0], "band", 1)]
            self.jobs["c"] = Job(entries, [struct(4 * mine, band_rows, width)] * count, self.put, self.finished)

        self.jobs["x"] = Job([near, got], [struct(*far.shape)], relay, after)

    def put(self, place, refs, outs):
        near, far, core = refs
        mine = near.shape[2]
        for i, out in enumerate(outs):
            for q, value in enumerate((near[i, 0], core[i, 0], far[i, 0], core[i, 1])):
                out[pl.ds((place[0] ^ q) * mine, mine)] = value

    def finished(self, outs):
        self.result = outs

    def take(self, names):
        return [self.jobs.pop(name) for name in names]


def in_order(place, own, other):
    first = place[1] == 0
    return jnp.where(first, own, other).astype(F32), jnp.where(first, other, own).astype(F32)


def by_rows(place, refs, outs):
    rows = refs[0].shape[1]
    for x in range(2):
        for core, value in enumerate(in_order(place, refs[0][x], refs[1][x])):
            at = (2 * core + x) * rows
            outs[0][at : at + rows, :] = value


def by_columns(segments):
    def body(place, refs, outs):
        rows = refs[0].shape[1]
        for x in range(2):
            col = 0
            for to, low, high in segments:
                half = outs[to].shape[1] // 2
                to_col = col + high - low
                pair = in_order(place, refs[0][x, :, col:to_col], refs[1][x, :, col:to_col])
                for core, value in enumerate(pair):
                    outs[to][x * rows : (x + 1) * rows, core * half + low : core * half + high] = value
                col = to_col

    return body


def reduce_plain(pair, by_core):
    send, keep = pair
    if by_core:
        keep, send = (entry.reshape(8, -1, entry.shape[2]) for entry in (keep, send))
        grad = jnp.concatenate([keep, send], 1)
    else:
        grad = jnp.concatenate([keep, send], 2)
    grad = grad.astype(F32).reshape(-1, grad.shape[2])
    part = lax.psum_scatter(grad, "img", scatter_dimension=0, tiled=True)
    return lax.psum(part.astype(BF16), "band").astype(F32)


def shards(
    tokens, cotangent, grid_side, visible, w_qkv, q_bias, v_bias, w_out, b_out, ln1_gain, ln1_shift,
    ln2_gain, ln2_shift, w_up, b_up, w_down, b_down, scale_attn, scale_mlp,
):
    width = tokens.shape[2]
    ff = w_up.shape[1]
    bands, imgs = lax.axis_size("band"), lax.axis_size("img")
    band, img = lax.axis_index("band"), lax.axis_index("img")
    fast = imgs == 8 and bands == 4
    blocks = 16
    zero = jnp.zeros_like(band)
    place = [band, band & 1, img * 2 + (band >> 1), band >> 1] if fast else [band, zero, zero, zero]
    place = jnp.stack(place).astype(jnp.int32)

    def to_images(entry):
        parts = cut(place, entry, bands)
        return [swap(part, "band", q) if q else part for q, part in enumerate(parts)]

    got_x = to_images(tokens)
    got_c = to_images(cotangent)
    vectors = (q_bias, v_bias, b_out, ln1_gain, ln1_shift, ln2_gain, ln2_shift, b_down, scale_attn, scale_mlp, b_up)
    vec, bias, valid, wv_qkv, wv_out, wv_up = prepare(place, grid_side, visible, vectors, (w_qkv, w_out, w_up), bands)

    s = {}
    exchanges = [[("io", "x")], [("io", "c")]]
    plan = PLAN if fast else [step for step in PLAN if isinstance(step, str)] + exchanges
    grads, ko = {}, {}
    token = None
    for step in plan:
        if step == "fwd":
            x, normed, q, k, v, p, att, branch, mid, normed2, hidden, slope, token = forward(
                place, got_x, bias, vec, wv_qkv, wv_out, wv_up
            )
        elif step == "down":
            top, gm, *d_pair, s["bd"], token = down(place, got_c, valid, vec, hidden, blocks, token=token)
            if fast:
                finish = ([struct(w_down.shape[0] // imgs, width, dtype=F32)], by_rows)
                sources = [(d_pair[1], swap(d_pair[0], "band", 1))]
                grads["d"] = Gradient(sources, CHAINS["d"], finish)
        elif step == "up":
            dpre, *u_pair, s["bu"], token = up(place, gm, slope, w_down, normed2, blocks, token=token)
            if fast:
                segments = [segment for chain in CHAINS["u"] for segment in chain[2]]
                finish = ([struct(width // imgs, ff, dtype=F32)], by_columns(segments))
                sources = [(u_pair[1], swap(u_pair[0], "band", 1))]
                grads["u"] = Gradient(sources, CHAINS["u"], finish)
        elif step == "outp":
            args = (hidden, w_down, mid, top, valid, vec)
            out_far, out_near, s["m"], token = output_rows(place, *args, bands, visible.shape[1], token=token)
        elif step == "out1":
            dmid, db, datt, s["o"], token = attention_out(
                place, dpre, w_up, mid, top, vec, branch, w_out, token=token
            )
        elif step == "attn":
            dproj, s["q"], token = attention(place, q, k, v, p, datt, token=token)
        elif step == "qkvo":
            *q_pair, o_send, o_keep, token = qkv(place, normed, dproj, att, db, blocks, token=token)
            if fast:
                ko["q"] = q_pair[1], swap(q_pair[0], "band", 1)
                ko["o"] = o_keep, swap(o_send, "band", 1)
        elif step == "inp":
            args = (dproj, w_qkv, x, dmid, vec, out_far, out_near)
            far, near, s["i"], token = input_back(place, *args, token=token)
            grads["io"] = Exchange(far, near)
        elif step == "pack":
            small = [s[name] for name in ("q", "i", "o", "bu", "bd", "m")]
            if fast:
                shape = struct(imgs, width // blocks, 128)
                grads["ko"].extra, token = call(pack_kernel, [shape], place, *small, limit=2, token=token)
        else:
            if ("ko", "c") in step:
                shapes = [struct(width // imgs, n, dtype=F32) for n in (3 * width, width)]
                segments = [segment for chain in CHAINS["ko"] for segment in chain[2]]
                finish = (shapes + [struct(16, 128, dtype=F32)], with_small(segments))
                grads["ko"] = Gradient([ko["q"], ko["o"]], CHAINS["ko"], finish)
            names = list(dict.fromkeys(name for name, _ in step))
            jobs = [job for name in names for job in grads[name].take([what for to, what in step if to == name])]
            token = fold(place, jobs, token)
    output, input_grad = grads["io"].result
    names = small_rows(*small)
    if fast:
        (grad_w_down,), (grad_w_up,) = grads["d"].result, grads["u"].result
        grad_w_qkv, grad_w_out, sums_ = grads["ko"].result
        size = width // imgs
        rows = ff // imgs // 128
        shares = [sums_[i, :size] for i in range(7)]
        shares += [sums_[7 : 7 + rows].reshape(-1)] + [sums_[7 + rows + i, :size] for i in range(3)]
    else:
        grad_w_down = reduce_plain(d_pair, True)
        grad_w_up = reduce_plain(u_pair, False)
        grad_w_out = reduce_plain((o_send, o_keep), False)
        grad_w_qkv = reduce_plain(q_pair, False)
        flat = [jnp.concatenate([ref[j] for j in which]) for ref, which in names]
        joined = jnp.concatenate([entry.reshape(imgs, -1) for entry in flat], 1)
        joined = lax.dynamic_index_in_dim(lax.psum(joined, ("img", "band")), img, 0, False)
        shares, at = [], 0
        for entry in flat:
            size = entry.shape[0] // imgs
            shares.append(joined[at : at + size])
            at += size
    (s_qb, s_vb, s_bo, s_g1, s_c1, s_g2, s_c2, s_bu, s_bd, s_sa, s_sm) = shares
    return (
        output, input_grad, grad_w_qkv, s_qb, s_vb, grad_w_out, s_bo, s_g1, s_c1, s_g2, s_c2, grad_w_up, s_bu,
        grad_w_down, s_bd, s_sa, s_sm,
    )


def with_small(segments):
    columns = by_columns(segments)
    at = sum(high - low for _, low, high in segments)

    def body(place, refs, outs):
        columns(place, refs, outs)
        rows, lanes = outs[2].shape
        outs[2][...] = total(*(ref[x, :rows, at : at + lanes] for ref in refs for x in range(2)))

    return body


def solution(mesh):
    cut = P("img", "band", None)
    in_specs = (cut, cut, P("img"), P("img", None)) + (P(),) * 15
    row, vec = P("img", None), P("img")
    out_specs = (cut, cut, row, vec, vec, row, vec, vec, vec, vec, vec, row, vec, row, vec, vec, vec)
    return jax.shard_map(shards, mesh=mesh, in_specs=in_specs, out_specs=out_specs, check_vma=False)
```

```python
import functools
import math

import jax
import jax.numpy as jnp
from jax import lax
from jax.experimental import pallas as pl
from jax.experimental.pallas import tpu as pltpu
from jax.sharding import PartitionSpec as P

HEAD = 64
GRID = 16
NEG_BIG = -1e30
EPSILON = 1e-06
F32 = jnp.float32
BF16 = jnp.bfloat16
SCALE = 6000000000.0
VM = pl.BlockSpec(memory_space=pltpu.VMEM)
SM = pl.BlockSpec(memory_space=pltpu.SMEM)
NN, NT, TN = ((1,), (0,)), ((1,), (1,)), ((0,), (0,))
Q_BIAS, V_BIAS, B_OUT, G1, C1, G2, C2, B_DOWN, S_ATTN, S_MLP, B_UP = range(11)


def dot(left, right, dims=NN):
    return lax.dot_general(left, right, (dims, ((), ())), preferred_element_type=F32)


def struct(*shape, dtype=BF16):
    return jax.ShapeDtypeStruct(shape, dtype)


def estimate(cost):
    return pl.CostEstimate(flops=int(cost * SCALE), bytes_accessed=1000, transcendentals=0)


def call(kernel, outs, place, *args, limit=8, token=None, cost=1.0):
    count = len(args)

    def body(place_ref, *refs):
        kernel(place_ref, *refs[:count], *refs[count + 1 : -1])
        refs[-1][...] = jnp.zeros_like(refs[-1])

    token = jnp.zeros((1, 128), F32) if token is None else token
    return pl.pallas_call(
        body,
        out_shape=[*outs, struct(1, 128, dtype=F32)],
        in_specs=[SM] + [VM] * (count + 1),
        out_specs=[VM] * (len(outs) + 1),
        compiler_params=pltpu.CompilerParams(vmem_limit_bytes=limit * 2**20),
        cost_estimate=estimate(cost),
    )(place, *args, token)


def norm_parts(entry):
    center = entry - jnp.mean(entry, -1, keepdims=True)
    spread = jnp.mean(center * center, -1, keepdims=True)
    inverse = lax.rsqrt(spread + EPSILON)
    return center * inverse, inverse


def norm_back(grad, gain, xhat, inverse):
    scaled = grad * gain
    inner = scaled - jnp.mean(scaled, -1, keepdims=True)
    return (inner - xhat * jnp.mean(scaled * xhat, -1, keepdims=True)) * inverse


def stack_heads(entry):
    lane = lax.broadcasted_iota(jnp.int32, entry.shape, 1)
    zero = jnp.zeros_like(entry)
    return jnp.concatenate([jnp.where(lane < HEAD, entry, zero), jnp.where(lane >= HEAD, entry, zero)], 0)


def cut_kernel(place, entry, *refs, mine):
    *outs, sem = refs
    copies = [
        pltpu.make_async_copy(entry.at[pl.ds((place[0] ^ q) * mine, mine)], out, sem.at[q]) for q, out in enumerate(outs)
    ]
    for copy in copies:
        copy.start()
    for copy in copies:
        copy.wait()


def cut(place, entry, bands):
    images, band_rows, width = entry.shape
    mine = images // bands
    return pl.pallas_call(
        functools.partial(cut_kernel, mine=mine),
        out_shape=[struct(mine, band_rows, width)] * bands,
        in_specs=[SM, pl.BlockSpec(memory_space=pl.ANY)],
        out_specs=[VM] * bands,
        scratch_shapes=[pltpu.SemaphoreType.DMA((bands,))],
        compiler_params=pltpu.CompilerParams(vmem_limit_bytes=2**20),
        cost_estimate=estimate(1.0),
    )(place, in_hbm(entry))


def whole_images(place, parts, out):
    mine, band_rows, _ = parts[0].shape
    for q, part in enumerate(parts):
        for n in range(mine):
            at = pl.multiple_of((n * len(parts) + (place[0] ^ q)) * band_rows, 16)
            out[pl.ds(at, band_rows), :] = part[n]


def in_hbm(entry):
    return pltpu.with_memory_space_constraint(entry, pltpu.HBM)


def prepare_kernel(place, sides, visible, *refs, mine, count, weights):
    vectors, matrices = refs[:count], refs[count : count + weights]
    vec_o, bias_o, valid_o, *matrix_o = refs[count + weights : count + 2 * weights + 3]
    *scratch, seen_s, sem = refs[count + 2 * weights + 3 :]
    pairs = (*zip(vectors, scratch), (visible, seen_s), *zip(matrices, matrix_o))
    copies = [pltpu.make_async_copy(a, b, sem.at[i]) for i, (a, b) in enumerate(pairs)]
    for copy in copies:
        copy.start()
    for copy in copies[: count + 1]:
        copy.wait()
    width = vec_o.shape[1]
    lanes = 128
    row = 0
    for s in scratch:
        for j in range(s.shape[0]):
            at = (row + j) * lanes
            vec_o[at // width : at // width + 1, at % width : at % width + lanes] = s[j : j + 1]
        row += s.shape[0]
    slots = seen_s.shape[1]
    slot = lax.broadcasted_iota(jnp.int32, (1, slots), 1)
    for n in range(mine):
        side = sides[place[0] * mine + n]
        inside = (slot // GRID < side) & (slot % GRID < side)
        bias = jnp.where(inside & (seen_s[pl.ds(place[0] * mine + n, 1), :] == 1), 0.0, NEG_BIG)
        for out, entry in ((bias_o, bias), (valid_o, jnp.where(inside, 1.0, 0.0))):
            out[n * slots : (n + 1) * slots, :] = jnp.broadcast_to(entry, (lanes, slots)).T
    for copy in copies[count + 1 :]:
        copy.wait()


def prepare(place, grid_side, visible, vectors, matrices, bands):
    images, slots = visible.shape
    mine = images // bands
    width = vectors[0].shape[0]
    vectors = [in_hbm(entry.reshape(-1, 128)) for entry in vectors]
    rows = sum(entry.shape[0] for entry in vectors) * 128 // width
    flat = struct(mine * slots, 128, dtype=F32)
    ref = pl.BlockSpec(memory_space=pl.ANY)
    return pl.pallas_call(
        functools.partial(prepare_kernel, mine=mine, count=len(vectors), weights=len(matrices)),
        out_shape=[struct(rows, width, dtype=F32), flat, flat] + [struct(*entry.shape) for entry in matrices],
        in_specs=[SM, SM] + [ref] * (len(vectors) + len(matrices) + 1),
        out_specs=[VM] * (len(matrices) + 3),
        scratch_shapes=[pltpu.VMEM(entry.shape, F32) for entry in vectors]
        + [pltpu.VMEM(visible.shape, jnp.int32), pltpu.SemaphoreType.DMA((len(vectors) + len(matrices) + 1,))],
        compiler_params=pltpu.CompilerParams(vmem_limit_bytes=4 * 2**20),
        cost_estimate=estimate(5.0),
    )(place, grid_side, in_hbm(visible), *vectors, *(in_hbm(entry) for entry in matrices))


def repeat(entry, width):
    return jnp.concatenate([entry] * (width // entry.shape[1]), 1)


def forward_kernel(place, *refs, bands):
    parts = refs[:bands]
    (bias, vec, w_qkv, w_out, w_up,
     x_o, normed_o, q_o, k_o, v_o, p_o, att_o, branch_o, mid_o, normed2_o, hidden_o, slope_o) = refs[bands:]
    mine = parts[0].shape[0]
    rows, width = x_o.shape
    slots = rows // mine
    whole_images(place, parts, x_o)
    pairs = width // (2 * HEAD)
    for n in range(mine):
        rs = slice(n * slots, (n + 1) * slots)
        xhat, _ = norm_parts(x_o[rs, :].astype(F32))
        normed = (xhat * vec[G1 : G1 + 1] + vec[C1 : C1 + 1]).astype(BF16)
        normed_o[rs, :] = normed
        queries = (dot(normed, w_qkv[:, :width]) + vec[Q_BIAS : Q_BIAS + 1]).astype(BF16)
        q_o[rs, :] = (queries.astype(F32) * HEAD**-0.5).astype(BF16)
        k_o[rs, :] = dot(normed, w_qkv[:, width : 2 * width]).astype(BF16)
        v_o[rs, :] = (dot(normed, w_qkv[:, 2 * width :]) + vec[V_BIAS : V_BIAS + 1]).astype(BF16)
    for n in range(mine):
        rs = slice(n * slots, (n + 1) * slots)
        mask = repeat(bias[rs, :], slots)
        for pr in range(pairs):
            cs = slice(pr * 2 * HEAD, (pr + 1) * 2 * HEAD)
            q, k, v = q_o[rs, cs], k_o[rs, cs], v_o[rs, cs]
            both = dot(stack_heads(k), q, NT).reshape(2, slots, slots) + mask
            e = jnp.exp(both - jnp.max(both, 1, keepdims=True))
            p = (e * (1.0 / jnp.sum(e, 1, keepdims=True))).astype(BF16)
            at = (n * pairs + pr) * 2
            p_o[at : at + 2] = p
            att_o[rs, cs] = dot(p.reshape(2 * slots, slots), stack_heads(v), TN).astype(BF16)
    for n in range(mine):
        rs = slice(n * slots, (n + 1) * slots)
        branch = dot(att_o[rs, :], w_out[...]) + vec[B_OUT : B_OUT + 1]
        branch_o[rs, :] = branch.astype(BF16)
        middle = x_o[rs, :].astype(F32) + vec[S_ATTN : S_ATTN + 1] * branch
        mid_o[rs, :] = middle
        xhat2, _ = norm_parts(middle)
        normed2_o[rs, :] = (xhat2 * vec[G2 : G2 + 1] + vec[C2 : C2 + 1]).astype(BF16)
    tile = 256
    for j in range(hidden_o.shape[1] // tile):
        js = slice(j * tile, (j + 1) * tile)
        row, col = B_UP + j * tile // width, j * tile % width
        pre = dot(normed2_o[...], w_up[:, js]) + vec[row : row + 1, col : col + tile]
        cdf = 0.5 + 0.5 * lax.erf(0.5**0.5 * pre)
        bell = jnp.exp2((-0.5 / math.log(2.0)) * (pre * pre))
        hidden_o[:, js] = (pre * cdf).astype(BF16)
        slope_o[:, js] = (cdf + ((0.5 / math.pi) ** 0.5 * pre) * bell).astype(BF16)


def forward(place, parts, bias, vec, w_qkv, w_out, w_up, **keys):
    mine, band_rows, width = parts[0].shape
    bands = len(parts)
    slots = bands * band_rows
    rows = mine * slots
    row, wide = struct(rows, width), struct(rows, w_up.shape[1])
    p = struct(mine * width // HEAD, slots, slots)
    outs = [row, row, row, row, row, p, row, row, struct(rows, width, dtype=F32), row, wide, wide]
    kernel = functools.partial(forward_kernel, bands=bands)
    return call(kernel, outs, place, *parts, bias, vec, w_qkv, w_out, w_up, limit=10, cost=13.6, **keys)


def sums(entry):
    return jnp.sum(entry, 0, keepdims=True)


def down_kernel(place, *refs, bands):
    parts = refs[:bands]
    valid, vec, hidden, top_o, gm_o, send_o, keep_o, sum_o = refs[bands:]
    whole_images(place, parts, top_o)
    top = repeat(valid[...], gm_o.shape[1]) * top_o[...].astype(F32)
    top_o[...] = top.astype(BF16)
    gm_o[...] = (vec[S_MLP : S_MLP + 1] * top).astype(BF16)
    sum_o[...] = sums(gm_o[...].astype(F32))
    blocks, rows, _ = send_o.shape
    first = place[1] == 0
    for i in range(blocks // 2):
        at = i * 4 * rows
        grad = dot(hidden[:, at : at + 4 * rows], gm_o[...], TN).astype(BF16)
        for x in range(2):
            to = (2 * i + x) ^ place[2]
            one, two = grad[x * rows : (x + 1) * rows], grad[(2 + x) * rows : (3 + x) * rows]
            keep_o[to] = jnp.where(first, one, two)
            send_o[to] = jnp.where(first, two, one)


def down(place, parts, valid, vec, hidden, blocks, **keys):
    rows, ff = hidden.shape
    width = vec.shape[1]
    part = struct(blocks, ff // blocks // 2, width)
    outs = [struct(rows, width), struct(rows, width), part, part, struct(1, width, dtype=F32)]
    kernel = functools.partial(down_kernel, bands=len(parts))
    return call(kernel, outs, place, *parts, valid, vec, hidden, cost=3.6, **keys)


def cut_rows(place, left, right, send_o, keep_o, tile):
    blocks, rows, _ = send_o.shape
    half = right.shape[1] // 2
    for target, core in ((send_o, 1 - place[1]), (keep_o, place[1])):
        for j in range(half // tile):
            at = pl.multiple_of(core * half + j * tile, 128)
            grad = dot(left[...], right[:, pl.ds(at, tile)], TN).astype(BF16)
            for i in range(blocks):
                target[i ^ place[2], :, j * tile : (j + 1) * tile] = grad[i * rows : (i + 1) * rows]


def up_kernel(place, gm, slope, w_down, normed2, dpre_o, send_o, keep_o, sum_o):
    ff = slope.shape[1]
    tile = gm.shape[1]
    for j in range(ff // tile):
        js = slice(j * tile, (j + 1) * tile)
        grad = (dot(gm[...], w_down[js, :], NT) * slope[:, js].astype(F32)).astype(BF16)
        dpre_o[:, js] = grad
        sum_o[j : j + 1] = sums(grad.astype(F32))
    cut_rows(place, normed2, dpre_o, send_o, keep_o, ff // 4)


def up(place, gm, slope, w_down, normed2, blocks, **keys):
    rows, ff = slope.shape
    width = gm.shape[1]
    part = struct(blocks, width // blocks, ff // 2)
    outs = [struct(rows, ff), part, part, struct(ff // width, width, dtype=F32)]
    return call(up_kernel, outs, place, gm, slope, w_down, normed2, limit=11, cost=6.0, **keys)


def out_kernel(place, dpre, w_up, mid, top, vec, branch, w_out, dmid_o, db_o, datt_o, sum_o):
    rows = dpre.shape[0]
    step = rows // 2
    parts = []
    for h in range(2):
        rs = slice(h * step, (h + 1) * step)
        grad = dot(dpre[rs, :], w_up[...], NT)
        xhat, inverse = norm_parts(mid[rs, :])
        dmid = top[rs, :].astype(F32) + norm_back(grad, vec[G2 : G2 + 1], xhat, inverse)
        dmid_o[rs, :] = dmid
        db = (vec[S_ATTN : S_ATTN + 1] * dmid).astype(BF16)
        db_o[rs, :] = db
        parts.append((sums(grad * xhat), sums(grad), sums(dmid * branch[rs, :].astype(F32)), sums(db.astype(F32))))
    for n, values in enumerate(zip(*parts)):
        sum_o[n : n + 1] = functools.reduce(jnp.add, values)
    datt_o[...] = dot(db_o[...], w_out[...], NT).astype(BF16)


def attention_out(place, dpre, w_up, mid, top, vec, branch, w_out, **keys):
    rows, width = mid.shape
    row = struct(rows, width)
    outs = [struct(rows, width, dtype=F32), row, row, struct(4, width, dtype=F32)]
    return call(out_kernel, outs, place, dpre, w_up, mid, top, vec, branch, w_out, limit=11, cost=6.0, **keys)


def attention_kernel(place, q, k, v, p, datt, dproj_o, sum_o):
    rows, width = q.shape
    slots = p.shape[1]
    pairs = width // (2 * HEAD)
    for n in range(rows // slots):
        rs = slice(n * slots, (n + 1) * slots)
        for pr in range(pairs):
            cs = slice(pr * 2 * HEAD, (pr + 1) * 2 * HEAD)
            qp, kp, vp, da = q[rs, cs], k[rs, cs], v[rs, cs], datt[rs, cs]
            at = (n * pairs + pr) * 2
            weights = p[at : at + 2]
            probs = weights.astype(F32)
            dw = dot(stack_heads(vp), da, NT).reshape(2, slots, slots)
            ds = (probs * (dw - jnp.sum(probs * dw, 1, keepdims=True))).astype(BF16)
            dq = dot(ds.reshape(2 * slots, slots), stack_heads(kp), TN)
            dk = dot(jnp.concatenate([ds[0], ds[1]], 1), stack_heads(qp))
            dv = dot(jnp.concatenate([weights[0], weights[1]], 1), stack_heads(da))
            dproj_o[rs, pr * 128 : pr * 128 + 128] = (dq * HEAD**-0.5).astype(BF16)
            dproj_o[rs, width + pr * 128 : width + pr * 128 + 128] = dk.astype(BF16)
            dproj_o[rs, 2 * width + pr * 128 : 2 * width + pr * 128 + 128] = dv.astype(BF16)
    sum_o[0:1] = sums(dproj_o[:, :width].astype(F32))
    sum_o[1:2] = sums(dproj_o[:, 2 * width :].astype(F32))


def attention(place, q, k, v, p, datt, **keys):
    rows, width = q.shape
    outs = [struct(rows, 3 * width), struct(2, width, dtype=F32)]
    return call(attention_kernel, outs, place, q, k, v, p, datt, cost=6.4, **keys)


def qkv_kernel(place, normed, dproj, att, db, qs_o, qk_o, os_o, ok_o):
    cut_rows(place, normed, dproj, qs_o, qk_o, 384)
    cut_rows(place, att, db, os_o, ok_o, 384)


def qkv(place, normed, dproj, att, db, blocks, **keys):
    width = normed.shape[1]
    wide, part = struct(blocks, width // blocks, 3 * width // 2), struct(blocks, width // blocks, width // 2)
    return call(qkv_kernel, [wide, wide, part, part], place, normed, dproj, att, db, limit=11, cost=4.0, **keys)


def input_kernel(place, dproj, w_qkv, x, dmid, vec, rows_o, sum_o):
    step = x.shape[0] // 2
    parts = []
    for rs in (slice(0, step), slice(step, 2 * step)):
        grad = dot(dproj[rs, :], w_qkv[...], NT)
        xhat, inverse = norm_parts(x[rs, :].astype(F32))
        rows_o[rs, :] = (dmid[rs, :] + norm_back(grad, vec[G1 : G1 + 1], xhat, inverse)).astype(BF16)
        parts.append((sums(grad * xhat), sums(grad)))
    for n, (one, two) in enumerate(zip(*parts)):
        sum_o[n : n + 1] = one + two


def input_back(place, dproj, w_qkv, x, dmid, vec, **keys):
    outs = [struct(*x.shape), struct(2, x.shape[1], dtype=F32)]
    return call(input_kernel, outs, place, dproj, w_qkv, x, dmid, vec, cost=3.2, **keys)


def output_kernel(place, hidden, w_down, mid, top, valid, vec, rows_o, sum_o):
    step = mid.shape[0] // 2
    parts = []
    for rs in (slice(0, step), slice(step, 2 * step)):
        branch = dot(hidden[rs, :], w_down[...]) + vec[B_DOWN : B_DOWN + 1]
        parts.append(sums(top[rs, :].astype(F32) * branch))
        result = repeat(valid[rs, :], mid.shape[1]) * (mid[rs, :] + vec[S_MLP : S_MLP + 1] * branch)
        rows_o[rs, :] = result.astype(BF16)
    sum_o[...] = parts[0] + parts[1]


def output_rows(place, hidden, w_down, mid, top, valid, vec, **keys):
    outs = [struct(*mid.shape), struct(1, mid.shape[1], dtype=F32)]
    args = (hidden, w_down, mid, top, valid, vec)
    return call(output_kernel, outs, place, *args, cost=3.4, **keys)


CHAINS = {
    "d": [
        ((("y",), ("z0",), ("z1",), ("x",)), (("z0",), ("x",), ("y",), ("z1",)), [(0, 0, 768)]),
    ],
    "u": [
        ((("x",), ("z0",), ("y",), ("z1",)), (("z0",), ("y",), ("z1",), ("x",)), [(0, 0, 1536)]),
    ],
    "ko": [
        ((("z0",), ("y",), ("x",), ("z1",)), (("y",), ("x",), ("z0",), ("z1",)), [(0, 0, 1024)]),
        ((("x",), ("y",), ("z1",), ("z0",)), (("x",), ("z0",), ("z1",), ("y",)), [(0, 1024, 1152), (1, 0, 384)]),
    ],
}
PLAN = [
    "fwd",
    "down",
    "up",
    [("d", "c")],
    "outp",
    [("u", "c"), ("o", "s")],
    "out1",
    "attn",
    "qkvo",
    [("d", ("ch", 0)), ("o", "x")],
    "inp",
    [("u", ("ch", 0)), ("ko", "c"), ("o", "c")],
    [("d", ("ch", 0)), ("i", "s")],
    "pack",
    [("u", ("ch", 0))],
    [("ko", ("ch", 0)), ("ko", ("ch", 1))],
    [("d", ("ch", 0))],
    [("i", "x"), ("u", ("ch", 0))],
    [("ko", ("ch", 0)), ("ko", ("ch", 1))],
    [("d", ("ch", 0)), ("i", "c")],
    [("u", ("ch", 0))],
    [("ko", ("ch", 0))],
    [("ko", ("ch", 1))],
    [("d", "X")],
    [("u", "X")],
    [("ko", ("ch", 0))],
    [("ko", ("ch", 1)), ("d", "C")],
    [("u", "C")],
    [("ko", "X")],
    [("ko", "C")],
]


def small_rows(s_q, s_i, s_o, s_bu, s_bd, s_m):
    return [
        (s_q, [0]), (s_q, [1]), (s_o, [3]), (s_i, [0]), (s_i, [1]), (s_o, [0]), (s_o, [1]),
        (s_bu, range(s_bu.shape[0])), (s_bd, [0]), (s_o, [2]), (s_m, [0]),
    ]


def pack_kernel(place, *refs):
    *entries, out = refs
    blocks, _, lanes = out.shape
    out[...] = jnp.zeros_like(out)
    flats = [jnp.concatenate([ref[j : j + 1] for j in which], 1) for ref, which in small_rows(*entries)]
    for i in range(blocks):
        row = 0
        for flat in flats:
            size = flat.shape[1] // blocks
            for at in range(0, size, lanes):
                n = min(lanes, size - at)
                value = flat[:, i * size + at : i * size + at + n].astype(BF16)
                out[i ^ (place[2] >> 1), row : row + 1, :n] = value
                row += 1


def swap(entry, axis, mask):
    size = lax.axis_size(axis)
    return lax.ppermute(entry, axis, [(i, i ^ mask) for i in range(size)])


BITS = {"x": 1, "y": 2, "z0": 4, "z1": 8}


def swap_by_core(entry, masks):
    bands = lax.axis_size("band")
    pairs = []
    for img in range(lax.axis_size("img")):
        for band in range(bands):
            mask = masks[band & 1]
            to = (img ^ (mask >> 1)) * bands + (band ^ (2 * (mask & 1)))
            pairs.append((img * bands + band, to))
    return lax.ppermute(entry, ("img", "band"), pairs)


def masks_of(axes):
    bits = [BITS[axis] for axis in axes]
    return bits if len(bits) == 1 else [*bits, bits[0] | bits[1]]


def split_labels(labels, axes):
    masks = masks_of(axes)
    every = sum(BITS[axis] for axis in axes)
    keep = [at for at, label in enumerate(labels) if not label & every]
    sent = [[labels.index(labels[at] | mask) for at in keep] for mask in masks]
    return [keep, *sent], [labels[at] for at in keep]


def total(*entries):
    result = entries[0].astype(F32)
    for entry in entries[1:]:
        result = result + entry.astype(F32)
    return result


class Job:
    def __init__(self, entries, outs, body, after):
        self.entries, self.outs, self.body, self.after = entries, outs, body, after


def fold(place, jobs, token):
    def kernel(place_ref, *refs):
        at, out_at = 0, sum(len(job.entries) for job in jobs)
        for job in jobs:
            n, m = len(job.entries), len(job.outs)
            job.body(place_ref, refs[at : at + n], refs[out_at : out_at + m])
            at, out_at = at + n, out_at + m

    entries = [entry for job in jobs for entry in job.entries]
    *outs, token = call(kernel, [out for job in jobs for out in job.outs], place, *entries, limit=8, token=token)
    for job in jobs:
        job.after(outs[: len(job.outs)])
        outs = outs[len(job.outs) :]
    return token


def step_job(sources, segments, labels, axes, after):
    cuts = [split_labels(labels[core], axes[core]) for core in range(2)]
    rows = sources[0][0].shape[1]
    width = sum(high - low for _, low, high in segments)
    part = struct(len(cuts[0][1]), rows, width)
    counts = [len(source) for source in sources]

    def body(place, refs, outs):
        groups = []
        at = 0
        for count in counts:
            groups.append(refs[at : at + count])
            at += count
        for which, out in enumerate(outs):
            for to in range(part.shape[0]):
                one, two = (cut[0][which][to] for cut in cuts)
                index = one if one == two else jnp.where(place[1] == 0, one, two)
                col = 0
                for source, low, high in segments:
                    value = total(*(ref[index, :, low:high] for ref in groups[source]))
                    out[to, :, col : col + high - low] = value.astype(BF16)
                    col += high - low

    def then(outs):
        keep, *sent = outs
        masks = zip(*(masks_of(axes[core]) for core in range(2)))
        after([keep, *(swap_by_core(entry, mask) for entry, mask in zip(sent, masks))], [cut[1] for cut in cuts])

    entries = [entry for source in sources for entry in source]
    return Job(entries, [part] * len(cuts[0][0]), body, then)


class Gradient:
    def __init__(self, sources, chains, finish):
        self.sources, self.chains, self.finish = sources, chains, finish
        self.jobs, self.waiting, self.done = {}, {}, {}
        self.extra = self.result = None

    def first(self):
        jobs = []
        for which, (one, two, segments) in enumerate(self.chains):
            after = functools.partial(self.arrive, which, 1)
            jobs.append(step_job(self.sources, segments, [list(range(16))] * 2, (one[0], two[0]), after))
        return jobs

    def arrive(self, which, at, entries, labels):
        if at < len(self.chains[which][0]):
            self.waiting[which] = at, entries, labels
        else:
            self.done[which] = entries

    def step(self, which):
        at, entries, labels = self.waiting.pop(which)
        one, two, _ = self.chains[which]
        sources, segments = [entries], [(0, 0, entries[0].shape[2])]
        if at == 1 and which == len(self.chains) - 1 and self.extra is not None:
            sources.append([self.extra])
            segments.append((1, 0, self.extra.shape[2]))
        return step_job(sources, segments, labels, (one[at], two[at]), functools.partial(self.arrive, which, at + 1))

    def take(self, names):
        jobs, ended = [], []
        for name in names:
            if name == "c":
                jobs += self.first()
            elif name in self.jobs:
                jobs.append(self.jobs.pop(name))
            elif name[1] in self.waiting:
                jobs.append(self.step(name[1]))
            else:
                ended.append(name[1])
        if ended:
            left = [at for at in range(len(self.chains)) if at not in ended and len(self.done.get(at, "..")) > 1]
            jobs += [self.park(at) for at in ended] if left else [self.merge()]
        return jobs

    def park(self, which):
        entries = self.done[which]

        def body(place, refs, outs):
            outs[0][...] = total(*(ref[...] for ref in refs)).astype(BF16)

        def after(outs):
            self.done[which] = outs

        return Job(entries, [struct(*entries[0].shape)], body, after)

    def merge(self):
        groups = [self.done[which] for which in range(len(self.chains))]
        rows = groups[0][0].shape[1]
        widths = [group[0].shape[2] for group in groups]

        def body(place, refs, outs):
            at = col = 0
            for group, width in zip(groups, widths):
                outs[0][:, col : col + width] = total(*(ref[0] for ref in refs[at : at + len(group)])).astype(BF16)
                at, col = at + len(group), col + width

        def after(outs):
            self.cross([outs[0], swap(outs[0], "band", 2)])

        return Job([entry for group in groups for entry in group], [struct(rows, sum(widths))], body, after)

    def cross(self, entries):
        def body(place, refs, outs):
            outs[0][place[3]] = refs[0][...]
            outs[0][1 - place[3]] = refs[1][...]

        def after(outs):
            entries = [outs[0], swap(outs[0], "band", 1)]
            self.jobs["C"] = Job(entries, self.finish[0], self.finish[1], self.finished)

        self.jobs["X"] = Job(entries, [struct(2, *entries[0].shape)], body, after)

    def finished(self, outs):
        self.result = outs


class Exchange:
    def __init__(self, entries, mine, bands):
        self.jobs, self.result = {}, None
        rows, width = entries[0].shape
        half = struct(len(entries), 2, mine, rows // mine // bands, width)

        def split(place, refs, outs):
            far, near = outs
            band_rows = far.shape[3]
            for i, ref in enumerate(refs):
                for q in range(bands):
                    for n in range(mine):
                        at = pl.multiple_of((n * bands + (place[0] ^ q)) * band_rows, 16)
                        (far if q & 2 else near)[i, q & 1, n] = ref[pl.ds(at, band_rows), :]

        self.jobs["s"] = Job(entries, [half, half], split, self.send)

    def send(self, outs):
        far, near = outs
        got = swap(far, "band", 2)
        count, _, mine, band_rows, width = far.shape

        def relay(place, refs, outs):
            for i in range(count):
                outs[0][i, 0] = refs[0][i, 1]
                outs[0][i, 1] = refs[1][i, 1]

        def after(outs):
            entries = [near, got, swap(outs[0], "band", 1)]
            self.jobs["c"] = Job(entries, [struct(4 * mine, band_rows, width)] * count, self.put, self.finished)

        self.jobs["x"] = Job([near, got], [struct(*far.shape)], relay, after)

    def put(self, place, refs, outs):
        near, far, core = refs
        mine = near.shape[2]
        for i, out in enumerate(outs):
            for q, value in enumerate((near[i, 0], core[i, 0], far[i, 0], core[i, 1])):
                out[pl.ds((place[0] ^ q) * mine, mine)] = value

    def finished(self, outs):
        self.result = outs

    def take(self, names):
        return [self.jobs.pop(name) for name in names]


def in_order(place, own, other):
    first = place[1] == 0
    return jnp.where(first, own, other).astype(F32), jnp.where(first, other, own).astype(F32)


def by_rows(place, refs, outs):
    rows = refs[0].shape[1]
    for x in range(2):
        for core, value in enumerate(in_order(place, refs[0][x], refs[1][x])):
            at = (2 * core + x) * rows
            outs[0][at : at + rows, :] = value


def by_columns(segments):
    def body(place, refs, outs):
        rows = refs[0].shape[1]
        for x in range(2):
            col = 0
            for to, low, high in segments:
                half = outs[to].shape[1] // 2
                to_col = col + high - low
                pair = in_order(place, refs[0][x, :, col:to_col], refs[1][x, :, col:to_col])
                for core, value in enumerate(pair):
                    outs[to][x * rows : (x + 1) * rows, core * half + low : core * half + high] = value
                col = to_col

    return body


def reduce_plain(pair, by_core):
    send, keep = pair
    if by_core:
        keep, send = (entry.reshape(8, -1, entry.shape[2]) for entry in (keep, send))
        grad = jnp.concatenate([keep, send], 1)
    else:
        grad = jnp.concatenate([keep, send], 2)
    grad = grad.astype(F32).reshape(-1, grad.shape[2])
    part = lax.psum_scatter(grad, "img", scatter_dimension=0, tiled=True)
    return lax.psum(part.astype(BF16), "band").astype(F32)


def shards(
    tokens, cotangent, grid_side, visible, w_qkv, q_bias, v_bias, w_out, b_out, ln1_gain, ln1_shift,
    ln2_gain, ln2_shift, w_up, b_up, w_down, b_down, scale_attn, scale_mlp,
):
    width = tokens.shape[2]
    ff = w_up.shape[1]
    bands, imgs = lax.axis_size("band"), lax.axis_size("img")
    band, img = lax.axis_index("band"), lax.axis_index("img")
    fast = imgs == 8 and bands == 4
    blocks = 16
    zero = jnp.zeros_like(band)
    place = [band, band & 1, img * 2 + (band >> 1), band >> 1] if fast else [band, zero, zero, zero]
    place = jnp.stack(place).astype(jnp.int32)

    def to_images(entry):
        parts = cut(place, entry, bands)
        return [swap(part, "band", q) if q else part for q, part in enumerate(parts)]

    got_x = to_images(tokens)
    got_c = to_images(cotangent)
    vectors = (q_bias, v_bias, b_out, ln1_gain, ln1_shift, ln2_gain, ln2_shift, b_down, scale_attn, scale_mlp, b_up)
    vec, bias, valid, wv_qkv, wv_out, wv_up = prepare(place, grid_side, visible, vectors, (w_qkv, w_out, w_up), bands)

    s = {}
    exchanges = [[("o", name), ("i", name)] for name in ("s", "x", "c")]
    plan = PLAN if fast else [step for step in PLAN if isinstance(step, str)] + exchanges
    grads, ko = {}, {}
    token = None
    for step in plan:
        if step == "fwd":
            x, normed, q, k, v, p, att, branch, mid, normed2, hidden, slope, token = forward(
                place, got_x, bias, vec, wv_qkv, wv_out, wv_up
            )
        elif step == "down":
            top, gm, *d_pair, s["bd"], token = down(place, got_c, valid, vec, hidden, blocks, token=token)
            if fast:
                finish = ([struct(w_down.shape[0] // imgs, width, dtype=F32)], by_rows)
                sources = [(d_pair[1], swap(d_pair[0], "band", 1))]
                grads["d"] = Gradient(sources, CHAINS["d"], finish)
        elif step == "up":
            dpre, *u_pair, s["bu"], token = up(place, gm, slope, w_down, normed2, blocks, token=token)
            if fast:
                segments = [segment for chain in CHAINS["u"] for segment in chain[2]]
                finish = ([struct(width // imgs, ff, dtype=F32)], by_columns(segments))
                sources = [(u_pair[1], swap(u_pair[0], "band", 1))]
                grads["u"] = Gradient(sources, CHAINS["u"], finish)
        elif step == "outp":
            args = (hidden, w_down, mid, top, valid, vec)
            out_rows, s["m"], token = output_rows(place, *args, token=token)
        elif step == "out1":
            dmid, db, datt, s["o"], token = attention_out(
                place, dpre, w_up, mid, top, vec, branch, w_out, token=token
            )
        elif step == "attn":
            dproj, s["q"], token = attention(place, q, k, v, p, datt, token=token)
        elif step == "qkvo":
            *q_pair, o_send, o_keep, token = qkv(place, normed, dproj, att, db, blocks, token=token)
            if fast:
                ko["q"] = q_pair[1], swap(q_pair[0], "band", 1)
                ko["o"] = o_keep, swap(o_send, "band", 1)
        elif step == "inp":
            in_rows, s["i"], token = input_back(place, dproj, w_qkv, x, dmid, vec, token=token)
        elif step == "pack":
            small = [s[name] for name in ("q", "i", "o", "bu", "bd", "m")]
            if fast:
                shape = struct(imgs, width // blocks, 128)
                grads["ko"].extra, token = call(pack_kernel, [shape], place, *small, limit=2, token=token)
        else:
            if ("o", "s") in step:
                grads["o"] = Exchange([out_rows], tokens.shape[0] // bands, bands)
            if ("i", "s") in step:
                grads["i"] = Exchange([in_rows], tokens.shape[0] // bands, bands)
            if ("ko", "c") in step:
                shapes = [struct(width // imgs, n, dtype=F32) for n in (3 * width, width)]
                segments = [segment for chain in CHAINS["ko"] for segment in chain[2]]
                finish = (shapes + [struct(16, 128, dtype=F32)], with_small(segments))
                grads["ko"] = Gradient([ko["q"], ko["o"]], CHAINS["ko"], finish)
            names = list(dict.fromkeys(name for name, _ in step))
            jobs = [job for name in names for job in grads[name].take([what for to, what in step if to == name])]
            token = fold(place, jobs, token)
    (output,), (input_grad,) = grads["o"].result, grads["i"].result
    names = small_rows(*small)
    if fast:
        (grad_w_down,), (grad_w_up,) = grads["d"].result, grads["u"].result
        grad_w_qkv, grad_w_out, sums_ = grads["ko"].result
        size = width // imgs
        rows = ff // imgs // 128
        shares = [sums_[i, :size] for i in range(7)]
        shares += [sums_[7 : 7 + rows].reshape(-1)] + [sums_[7 + rows + i, :size] for i in range(3)]
    else:
        grad_w_down = reduce_plain(d_pair, True)
        grad_w_up = reduce_plain(u_pair, False)
        grad_w_out = reduce_plain((o_send, o_keep), False)
        grad_w_qkv = reduce_plain(q_pair, False)
        flat = [jnp.concatenate([ref[j] for j in which]) for ref, which in names]
        joined = jnp.concatenate([entry.reshape(imgs, -1) for entry in flat], 1)
        joined = lax.dynamic_index_in_dim(lax.psum(joined, ("img", "band")), img, 0, False)
        shares, at = [], 0
        for entry in flat:
            size = entry.shape[0] // imgs
            shares.append(joined[at : at + size])
            at += size
    (s_qb, s_vb, s_bo, s_g1, s_c1, s_g2, s_c2, s_bu, s_bd, s_sa, s_sm) = shares
    return (
        output, input_grad, grad_w_qkv, s_qb, s_vb, grad_w_out, s_bo, s_g1, s_c1, s_g2, s_c2, grad_w_up, s_bu,
        grad_w_down, s_bd, s_sa, s_sm,
    )


def with_small(segments):
    columns = by_columns(segments)
    at = sum(high - low for _, low, high in segments)

    def body(place, refs, outs):
        columns(place, refs, outs)
        rows, lanes = outs[2].shape
        outs[2][...] = total(*(ref[x, :rows, at : at + lanes] for ref in refs for x in range(2)))

    return body


def solution(mesh):
    cut = P("img", "band", None)
    in_specs = (cut, cut, P("img"), P("img", None)) + (P(),) * 15
    row, vec = P("img", None), P("img")
    out_specs = (cut, cut, row, vec, vec, row, vec, vec, vec, vec, vec, row, vec, row, vec, vec, vec)
    return jax.shard_map(shards, mesh=mesh, in_specs=in_specs, out_specs=out_specs, check_vma=False)
```

```python
import functools
import math

import jax
import jax.numpy as jnp
from jax import lax
from jax.experimental import pallas as pl
from jax.experimental.pallas import tpu as pltpu
from jax.sharding import PartitionSpec as P

HEAD = 64
GRID = 16
NEG_BIG = -1e30
EPSILON = 1e-06
F32 = jnp.float32
BF16 = jnp.bfloat16
SCALE = 6000000000.0
VM = pl.BlockSpec(memory_space=pltpu.VMEM)
SM = pl.BlockSpec(memory_space=pltpu.SMEM)
NN, NT, TN = ((1,), (0,)), ((1,), (1,)), ((0,), (0,))
Q_BIAS, V_BIAS, B_OUT, G1, C1, G2, C2, B_DOWN, S_ATTN, S_MLP, B_UP = range(11)


def dot(left, right, dims=NN):
    return lax.dot_general(left, right, (dims, ((), ())), preferred_element_type=F32)


def struct(*shape, dtype=BF16):
    return jax.ShapeDtypeStruct(shape, dtype)


def estimate(cost):
    return pl.CostEstimate(flops=int(cost * SCALE), bytes_accessed=1000, transcendentals=0)


def call(kernel, outs, place, *args, limit=8, token=None, cost=1.0):
    count = len(args)

    def body(place_ref, *refs):
        kernel(place_ref, *refs[:count], *refs[count + 1 : -1])
        refs[-1][...] = jnp.zeros_like(refs[-1])

    token = jnp.zeros((1, 128), F32) if token is None else token
    return pl.pallas_call(
        body,
        out_shape=[*outs, struct(1, 128, dtype=F32)],
        in_specs=[SM] + [VM] * (count + 1),
        out_specs=[VM] * (len(outs) + 1),
        compiler_params=pltpu.CompilerParams(vmem_limit_bytes=limit * 2**20),
        cost_estimate=estimate(cost),
    )(place, *args, token)


def norm_parts(entry):
    center = entry - jnp.mean(entry, -1, keepdims=True)
    spread = jnp.mean(center * center, -1, keepdims=True)
    inverse = lax.rsqrt(spread + EPSILON)
    return center * inverse, inverse


def norm_back(grad, gain, xhat, inverse):
    scaled = grad * gain
    inner = scaled - jnp.mean(scaled, -1, keepdims=True)
    return (inner - xhat * jnp.mean(scaled * xhat, -1, keepdims=True)) * inverse


def stack_heads(entry):
    lane = lax.broadcasted_iota(jnp.int32, entry.shape, 1)
    zero = jnp.zeros_like(entry)
    return jnp.concatenate([jnp.where(lane < HEAD, entry, zero), jnp.where(lane >= HEAD, entry, zero)], 0)


def cut_kernel(place, entry, *refs, mine):
    *outs, sem = refs
    copies = [
        pltpu.make_async_copy(entry.at[pl.ds((place[0] ^ q) * mine, mine)], out, sem.at[q]) for q, out in enumerate(outs)
    ]
    for copy in copies:
        copy.start()
    for copy in copies:
        copy.wait()


def cut(place, entry, bands):
    images, band_rows, width = entry.shape
    mine = images // bands
    return pl.pallas_call(
        functools.partial(cut_kernel, mine=mine),
        out_shape=[struct(mine, band_rows, width)] * bands,
        in_specs=[SM, pl.BlockSpec(memory_space=pl.ANY)],
        out_specs=[VM] * bands,
        scratch_shapes=[pltpu.SemaphoreType.DMA((bands,))],
        compiler_params=pltpu.CompilerParams(vmem_limit_bytes=2**20),
        cost_estimate=estimate(1.0),
    )(place, in_hbm(entry))


def whole_images(place, parts, out):
    mine, band_rows, _ = parts[0].shape
    for q, part in enumerate(parts):
        for n in range(mine):
            at = pl.multiple_of((n * len(parts) + (place[0] ^ q)) * band_rows, 16)
            out[pl.ds(at, band_rows), :] = part[n]


def in_hbm(entry):
    return pltpu.with_memory_space_constraint(entry, pltpu.HBM)


def prepare_kernel(place, sides, visible, *refs, mine, count, weights):
    vectors, matrices = refs[:count], refs[count : count + weights]
    vec_o, bias_o, valid_o, *matrix_o = refs[count + weights : count + 2 * weights + 3]
    *scratch, seen_s, sem = refs[count + 2 * weights + 3 :]
    pairs = (*zip(vectors, scratch), (visible, seen_s), *zip(matrices, matrix_o))
    copies = [pltpu.make_async_copy(a, b, sem.at[i]) for i, (a, b) in enumerate(pairs)]
    for copy in copies:
        copy.start()
    for copy in copies[: count + 1]:
        copy.wait()
    width = vec_o.shape[1]
    lanes = 128
    row = 0
    for s in scratch:
        for j in range(s.shape[0]):
            at = (row + j) * lanes
            vec_o[at // width : at // width + 1, at % width : at % width + lanes] = s[j : j + 1]
        row += s.shape[0]
    slots = seen_s.shape[1]
    slot = lax.broadcasted_iota(jnp.int32, (1, slots), 1)
    for n in range(mine):
        side = sides[place[0] * mine + n]
        inside = (slot // GRID < side) & (slot % GRID < side)
        bias = jnp.where(inside & (seen_s[pl.ds(place[0] * mine + n, 1), :] == 1), 0.0, NEG_BIG)
        for out, entry in ((bias_o, bias), (valid_o, jnp.where(inside, 1.0, 0.0))):
            out[n * slots : (n + 1) * slots, :] = jnp.broadcast_to(entry, (lanes, slots)).T
    for copy in copies[count + 1 :]:
        copy.wait()


def prepare(place, grid_side, visible, vectors, matrices, bands):
    images, slots = visible.shape
    mine = images // bands
    width = vectors[0].shape[0]
    vectors = [in_hbm(entry.reshape(-1, 128)) for entry in vectors]
    rows = sum(entry.shape[0] for entry in vectors) * 128 // width
    flat = struct(mine * slots, 128, dtype=F32)
    ref = pl.BlockSpec(memory_space=pl.ANY)
    return pl.pallas_call(
        functools.partial(prepare_kernel, mine=mine, count=len(vectors), weights=len(matrices)),
        out_shape=[struct(rows, width, dtype=F32), flat, flat] + [struct(*entry.shape) for entry in matrices],
        in_specs=[SM, SM] + [ref] * (len(vectors) + len(matrices) + 1),
        out_specs=[VM] * (len(matrices) + 3),
        scratch_shapes=[pltpu.VMEM(entry.shape, F32) for entry in vectors]
        + [pltpu.VMEM(visible.shape, jnp.int32), pltpu.SemaphoreType.DMA((len(vectors) + len(matrices) + 1,))],
        compiler_params=pltpu.CompilerParams(vmem_limit_bytes=4 * 2**20),
        cost_estimate=estimate(5.0),
    )(place, grid_side, in_hbm(visible), *vectors, *(in_hbm(entry) for entry in matrices))


def repeat(entry, width):
    return jnp.concatenate([entry] * (width // entry.shape[1]), 1)


def forward_kernel(place, *refs, bands):
    parts = refs[:bands]
    (bias, vec, w_qkv, w_out, w_up,
     x_o, normed_o, q_o, k_o, v_o, p_o, att_o, branch_o, mid_o, normed2_o, hidden_o, slope_o) = refs[bands:]
    mine = parts[0].shape[0]
    rows, width = x_o.shape
    slots = rows // mine
    whole_images(place, parts, x_o)
    pairs = width // (2 * HEAD)
    for n in range(mine):
        rs = slice(n * slots, (n + 1) * slots)
        xhat, _ = norm_parts(x_o[rs, :].astype(F32))
        normed = (xhat * vec[G1 : G1 + 1] + vec[C1 : C1 + 1]).astype(BF16)
        normed_o[rs, :] = normed
        queries = (dot(normed, w_qkv[:, :width]) + vec[Q_BIAS : Q_BIAS + 1]).astype(BF16)
        q_o[rs, :] = (queries.astype(F32) * HEAD**-0.5).astype(BF16)
        k_o[rs, :] = dot(normed, w_qkv[:, width : 2 * width]).astype(BF16)
        v_o[rs, :] = (dot(normed, w_qkv[:, 2 * width :]) + vec[V_BIAS : V_BIAS + 1]).astype(BF16)
    for n in range(mine):
        rs = slice(n * slots, (n + 1) * slots)
        mask = repeat(bias[rs, :], slots)
        for pr in range(pairs):
            cs = slice(pr * 2 * HEAD, (pr + 1) * 2 * HEAD)
            q, k, v = q_o[rs, cs], k_o[rs, cs], v_o[rs, cs]
            both = dot(stack_heads(k), q, NT).reshape(2, slots, slots) + mask
            e = jnp.exp(both - jnp.max(both, 1, keepdims=True))
            p = (e * (1.0 / jnp.sum(e, 1, keepdims=True))).astype(BF16)
            at = (n * pairs + pr) * 2
            p_o[at : at + 2] = p
            att_o[rs, cs] = dot(p.reshape(2 * slots, slots), stack_heads(v), TN).astype(BF16)
    for n in range(mine):
        rs = slice(n * slots, (n + 1) * slots)
        branch = dot(att_o[rs, :], w_out[...]) + vec[B_OUT : B_OUT + 1]
        branch_o[rs, :] = branch.astype(BF16)
        middle = x_o[rs, :].astype(F32) + vec[S_ATTN : S_ATTN + 1] * branch
        mid_o[rs, :] = middle
        xhat2, _ = norm_parts(middle)
        normed2_o[rs, :] = (xhat2 * vec[G2 : G2 + 1] + vec[C2 : C2 + 1]).astype(BF16)
    tile = 256
    for j in range(hidden_o.shape[1] // tile):
        js = slice(j * tile, (j + 1) * tile)
        row, col = B_UP + j * tile // width, j * tile % width
        pre = dot(normed2_o[...], w_up[:, js]) + vec[row : row + 1, col : col + tile]
        cdf = 0.5 + 0.5 * lax.erf(0.5**0.5 * pre)
        bell = jnp.exp2((-0.5 / math.log(2.0)) * (pre * pre))
        hidden_o[:, js] = (pre * cdf).astype(BF16)
        slope_o[:, js] = (cdf + ((0.5 / math.pi) ** 0.5 * pre) * bell).astype(BF16)


def forward(place, parts, bias, vec, w_qkv, w_out, w_up, **keys):
    mine, band_rows, width = parts[0].shape
    bands = len(parts)
    slots = bands * band_rows
    rows = mine * slots
    row, wide = struct(rows, width), struct(rows, w_up.shape[1])
    p = struct(mine * width // HEAD, slots, slots)
    outs = [row, row, row, row, row, p, row, row, struct(rows, width, dtype=F32), row, wide, wide]
    kernel = functools.partial(forward_kernel, bands=bands)
    return call(kernel, outs, place, *parts, bias, vec, w_qkv, w_out, w_up, limit=10, cost=13.6, **keys)


def sums(entry):
    return jnp.sum(entry, 0, keepdims=True)


def down_kernel(place, *refs, bands):
    parts = refs[:bands]
    valid, vec, hidden, top_o, gm_o, send_o, keep_o, sum_o = refs[bands:]
    whole_images(place, parts, top_o)
    top = repeat(valid[...], gm_o.shape[1]) * top_o[...].astype(F32)
    top_o[...] = top.astype(BF16)
    gm_o[...] = (vec[S_MLP : S_MLP + 1] * top).astype(BF16)
    sum_o[...] = sums(gm_o[...].astype(F32))
    blocks, rows, _ = send_o.shape
    first = place[1] == 0
    for i in range(blocks // 2):
        at = i * 4 * rows
        grad = dot(hidden[:, at : at + 4 * rows], gm_o[...], TN).astype(BF16)
        for x in range(2):
            to = (2 * i + x) ^ place[2]
            one, two = grad[x * rows : (x + 1) * rows], grad[(2 + x) * rows : (3 + x) * rows]
            keep_o[to] = jnp.where(first, one, two)
            send_o[to] = jnp.where(first, two, one)


def down(place, parts, valid, vec, hidden, blocks, **keys):
    rows, ff = hidden.shape
    width = vec.shape[1]
    part = struct(blocks, ff // blocks // 2, width)
    outs = [struct(rows, width), struct(rows, width), part, part, struct(1, width, dtype=F32)]
    kernel = functools.partial(down_kernel, bands=len(parts))
    return call(kernel, outs, place, *parts, valid, vec, hidden, cost=3.6, **keys)


def cut_rows(place, left, right, send_o, keep_o, tile):
    blocks, rows, _ = send_o.shape
    half = right.shape[1] // 2
    for target, core in ((send_o, 1 - place[1]), (keep_o, place[1])):
        for j in range(half // tile):
            at = pl.multiple_of(core * half + j * tile, 128)
            grad = dot(left[...], right[:, pl.ds(at, tile)], TN).astype(BF16)
            for i in range(blocks):
                target[i ^ place[2], :, j * tile : (j + 1) * tile] = grad[i * rows : (i + 1) * rows]


def up_kernel(place, gm, slope, w_down, normed2, dpre_o, send_o, keep_o, sum_o):
    ff = slope.shape[1]
    tile = gm.shape[1]
    for j in range(ff // tile):
        js = slice(j * tile, (j + 1) * tile)
        grad = (dot(gm[...], w_down[js, :], NT) * slope[:, js].astype(F32)).astype(BF16)
        dpre_o[:, js] = grad
        sum_o[j : j + 1] = sums(grad.astype(F32))
    cut_rows(place, normed2, dpre_o, send_o, keep_o, ff // 4)


def up(place, gm, slope, w_down, normed2, blocks, **keys):
    rows, ff = slope.shape
    width = gm.shape[1]
    part = struct(blocks, width // blocks, ff // 2)
    outs = [struct(rows, ff), part, part, struct(ff // width, width, dtype=F32)]
    return call(up_kernel, outs, place, gm, slope, w_down, normed2, limit=11, cost=6.0, **keys)


def out_kernel(place, dpre, w_up, mid, top, vec, branch, w_out, dmid_o, db_o, datt_o, sum_o):
    rows = dpre.shape[0]
    step = rows // 2
    parts = []
    for h in range(2):
        rs = slice(h * step, (h + 1) * step)
        grad = dot(dpre[rs, :], w_up[...], NT)
        xhat, inverse = norm_parts(mid[rs, :])
        dmid = top[rs, :].astype(F32) + norm_back(grad, vec[G2 : G2 + 1], xhat, inverse)
        dmid_o[rs, :] = dmid
        db = (vec[S_ATTN : S_ATTN + 1] * dmid).astype(BF16)
        db_o[rs, :] = db
        parts.append((sums(grad * xhat), sums(grad), sums(dmid * branch[rs, :].astype(F32)), sums(db.astype(F32))))
    for n, values in enumerate(zip(*parts)):
        sum_o[n : n + 1] = functools.reduce(jnp.add, values)
    datt_o[...] = dot(db_o[...], w_out[...], NT).astype(BF16)


def attention_out(place, dpre, w_up, mid, top, vec, branch, w_out, **keys):
    rows, width = mid.shape
    row = struct(rows, width)
    outs = [struct(rows, width, dtype=F32), row, row, struct(4, width, dtype=F32)]
    return call(out_kernel, outs, place, dpre, w_up, mid, top, vec, branch, w_out, limit=11, cost=6.0, **keys)


def attention_kernel(place, q, k, v, p, datt, dproj_o, sum_o):
    rows, width = q.shape
    slots = p.shape[1]
    pairs = width // (2 * HEAD)
    for n in range(rows // slots):
        rs = slice(n * slots, (n + 1) * slots)
        for pr in range(pairs):
            cs = slice(pr * 2 * HEAD, (pr + 1) * 2 * HEAD)
            qp, kp, vp, da = q[rs, cs], k[rs, cs], v[rs, cs], datt[rs, cs]
            at = (n * pairs + pr) * 2
            weights = p[at : at + 2]
            probs = weights.astype(F32)
            dw = dot(stack_heads(vp), da, NT).reshape(2, slots, slots)
            ds = (probs * (dw - jnp.sum(probs * dw, 1, keepdims=True))).astype(BF16)
            dq = dot(ds.reshape(2 * slots, slots), stack_heads(kp), TN)
            dk = dot(jnp.concatenate([ds[0], ds[1]], 1), stack_heads(qp))
            dv = dot(jnp.concatenate([weights[0], weights[1]], 1), stack_heads(da))
            dproj_o[rs, pr * 128 : pr * 128 + 128] = (dq * HEAD**-0.5).astype(BF16)
            dproj_o[rs, width + pr * 128 : width + pr * 128 + 128] = dk.astype(BF16)
            dproj_o[rs, 2 * width + pr * 128 : 2 * width + pr * 128 + 128] = dv.astype(BF16)
    sum_o[0:1] = sums(dproj_o[:, :width].astype(F32))
    sum_o[1:2] = sums(dproj_o[:, 2 * width :].astype(F32))


def attention(place, q, k, v, p, datt, **keys):
    rows, width = q.shape
    outs = [struct(rows, 3 * width), struct(2, width, dtype=F32)]
    return call(attention_kernel, outs, place, q, k, v, p, datt, cost=6.4, **keys)


def qkv_kernel(place, normed, dproj, att, db, qs_o, qk_o, os_o, ok_o):
    cut_rows(place, normed, dproj, qs_o, qk_o, 384)
    cut_rows(place, att, db, os_o, ok_o, 384)


def qkv(place, normed, dproj, att, db, blocks, **keys):
    width = normed.shape[1]
    wide, part = struct(blocks, width // blocks, 3 * width // 2), struct(blocks, width // blocks, width // 2)
    return call(qkv_kernel, [wide, wide, part, part], place, normed, dproj, att, db, limit=11, cost=4.0, **keys)


def input_kernel(place, dproj, w_qkv, x, dmid, vec, rows_o, sum_o):
    step = x.shape[0] // 2
    parts = []
    for rs in (slice(0, step), slice(step, 2 * step)):
        grad = dot(dproj[rs, :], w_qkv[...], NT)
        xhat, inverse = norm_parts(x[rs, :].astype(F32))
        rows_o[rs, :] = (dmid[rs, :] + norm_back(grad, vec[G1 : G1 + 1], xhat, inverse)).astype(BF16)
        parts.append((sums(grad * xhat), sums(grad)))
    for n, (one, two) in enumerate(zip(*parts)):
        sum_o[n : n + 1] = one + two


def input_back(place, dproj, w_qkv, x, dmid, vec, **keys):
    outs = [struct(*x.shape), struct(2, x.shape[1], dtype=F32)]
    return call(input_kernel, outs, place, dproj, w_qkv, x, dmid, vec, cost=3.2, **keys)


def output_kernel(place, hidden, w_down, mid, top, valid, vec, rows_o, sum_o):
    step = mid.shape[0] // 2
    parts = []
    for rs in (slice(0, step), slice(step, 2 * step)):
        branch = dot(hidden[rs, :], w_down[...]) + vec[B_DOWN : B_DOWN + 1]
        parts.append(sums(top[rs, :].astype(F32) * branch))
        result = repeat(valid[rs, :], mid.shape[1]) * (mid[rs, :] + vec[S_MLP : S_MLP + 1] * branch)
        rows_o[rs, :] = result.astype(BF16)
    sum_o[...] = parts[0] + parts[1]


def output_rows(place, hidden, w_down, mid, top, valid, vec, **keys):
    outs = [struct(*mid.shape), struct(1, mid.shape[1], dtype=F32)]
    args = (hidden, w_down, mid, top, valid, vec)
    return call(output_kernel, outs, place, *args, cost=3.4, **keys)


CHAINS = {
    "d": [
        ((("y",), ("z0",), ("z1",), ("x",)), (("z0",), ("x",), ("y",), ("z1",)), [(0, 0, 768)]),
    ],
    "u": [
        ((("x",), ("z0",), ("y",), ("z1",)), (("z0",), ("y",), ("z1",), ("x",)), [(0, 0, 1536)]),
    ],
    "ko": [
        ((("z0",), ("y",), ("x",), ("z1",)), (("y",), ("x",), ("z0",), ("z1",)), [(0, 0, 1024)]),
        ((("x",), ("y",), ("z1",), ("z0",)), (("x",), ("z0",), ("z1",), ("y",)), [(0, 1024, 1152), (1, 0, 384)]),
    ],
}
PLAN = [
    "fwd",
    "down",
    "up",
    [("d", "c")],
    "outp",
    [("u", "c"), ("o", "s")],
    "out1",
    "attn",
    "qkvo",
    [("d", ("ch", 0)), ("o", "x")],
    "inp",
    [("u", ("ch", 0)), ("ko", "c"), ("o", "c")],
    [("d", ("ch", 0)), ("i", "s")],
    "pack",
    [("u", ("ch", 0))],
    [("ko", ("ch", 0)), ("ko", ("ch", 1))],
    [("d", ("ch", 0))],
    [("i", "x"), ("u", ("ch", 0))],
    [("ko", ("ch", 0)), ("ko", ("ch", 1))],
    [("d", ("ch", 0)), ("i", "c")],
    [("u", ("ch", 0))],
    [("ko", ("ch", 0)), ("ko", ("ch", 1))],
    [("d", "X")],
    [("u", "X")],
    [("ko", ("ch", 0)), ("ko", ("ch", 1)), ("d", "C")],
    [("u", "C")],
    [("ko", "X")],
    [("ko", "C")],
]


def small_rows(s_q, s_i, s_o, s_bu, s_bd, s_m):
    return [
        (s_q, [0]), (s_q, [1]), (s_o, [3]), (s_i, [0]), (s_i, [1]), (s_o, [0]), (s_o, [1]),
        (s_bu, range(s_bu.shape[0])), (s_bd, [0]), (s_o, [2]), (s_m, [0]),
    ]


def pack_kernel(place, *refs):
    *entries, out = refs
    blocks, _, lanes = out.shape
    out[...] = jnp.zeros_like(out)
    flats = [jnp.concatenate([ref[j : j + 1] for j in which], 1) for ref, which in small_rows(*entries)]
    for i in range(blocks):
        row = 0
        for flat in flats:
            size = flat.shape[1] // blocks
            for at in range(0, size, lanes):
                n = min(lanes, size - at)
                value = flat[:, i * size + at : i * size + at + n].astype(BF16)
                out[i ^ (place[2] >> 1), row : row + 1, :n] = value
                row += 1


def swap(entry, axis, mask):
    size = lax.axis_size(axis)
    return lax.ppermute(entry, axis, [(i, i ^ mask) for i in range(size)])


BITS = {"x": 1, "y": 2, "z0": 4, "z1": 8}


def swap_by_core(entry, masks):
    bands = lax.axis_size("band")
    pairs = []
    for img in range(lax.axis_size("img")):
        for band in range(bands):
            mask = masks[band & 1]
            to = (img ^ (mask >> 1)) * bands + (band ^ (2 * (mask & 1)))
            pairs.append((img * bands + band, to))
    return lax.ppermute(entry, ("img", "band"), pairs)


def masks_of(axes):
    bits = [BITS[axis] for axis in axes]
    return bits if len(bits) == 1 else [*bits, bits[0] | bits[1]]


def split_labels(labels, axes):
    masks = masks_of(axes)
    every = sum(BITS[axis] for axis in axes)
    keep = [at for at, label in enumerate(labels) if not label & every]
    sent = [[labels.index(labels[at] | mask) for at in keep] for mask in masks]
    return [keep, *sent], [labels[at] for at in keep]


def total(*entries):
    result = entries[0].astype(F32)
    for entry in entries[1:]:
        result = result + entry.astype(F32)
    return result


class Job:
    def __init__(self, entries, outs, body, after):
        self.entries, self.outs, self.body, self.after = entries, outs, body, after


def fold(place, jobs, token):
    def kernel(place_ref, *refs):
        at, out_at = 0, sum(len(job.entries) for job in jobs)
        for job in jobs:
            n, m = len(job.entries), len(job.outs)
            job.body(place_ref, refs[at : at + n], refs[out_at : out_at + m])
            at, out_at = at + n, out_at + m

    entries = [entry for job in jobs for entry in job.entries]
    *outs, token = call(kernel, [out for job in jobs for out in job.outs], place, *entries, limit=8, token=token)
    for job in jobs:
        job.after(outs[: len(job.outs)])
        outs = outs[len(job.outs) :]
    return token


def step_job(sources, segments, labels, axes, after):
    cuts = [split_labels(labels[core], axes[core]) for core in range(2)]
    rows = sources[0][0].shape[1]
    width = sum(high - low for _, low, high in segments)
    part = struct(len(cuts[0][1]), rows, width)
    counts = [len(source) for source in sources]

    def body(place, refs, outs):
        groups = []
        at = 0
        for count in counts:
            groups.append(refs[at : at + count])
            at += count
        for which, out in enumerate(outs):
            for to in range(part.shape[0]):
                one, two = (cut[0][which][to] for cut in cuts)
                index = one if one == two else jnp.where(place[1] == 0, one, two)
                col = 0
                for source, low, high in segments:
                    value = total(*(ref[index, :, low:high] for ref in groups[source]))
                    out[to, :, col : col + high - low] = value.astype(BF16)
                    col += high - low

    def then(outs):
        keep, *sent = outs
        masks = zip(*(masks_of(axes[core]) for core in range(2)))
        after([keep, *(swap_by_core(entry, mask) for entry, mask in zip(sent, masks))], [cut[1] for cut in cuts])

    entries = [entry for source in sources for entry in source]
    return Job(entries, [part] * len(cuts[0][0]), body, then)


class Gradient:
    def __init__(self, sources, chains, finish):
        self.sources, self.chains, self.finish = sources, chains, finish
        self.jobs, self.waiting, self.done = {}, {}, {}
        self.extra = self.result = None

    def first(self):
        jobs = []
        for which, (one, two, segments) in enumerate(self.chains):
            after = functools.partial(self.arrive, which, 1)
            jobs.append(step_job(self.sources, segments, [list(range(16))] * 2, (one[0], two[0]), after))
        return jobs

    def arrive(self, which, at, entries, labels):
        if at < len(self.chains[which][0]):
            self.waiting[which] = at, entries, labels
        else:
            self.done[which] = entries

    def step(self, which):
        at, entries, labels = self.waiting.pop(which)
        one, two, _ = self.chains[which]
        sources, segments = [entries], [(0, 0, entries[0].shape[2])]
        if at == 1 and which == len(self.chains) - 1 and self.extra is not None:
            sources.append([self.extra])
            segments.append((1, 0, self.extra.shape[2]))
        return step_job(sources, segments, labels, (one[at], two[at]), functools.partial(self.arrive, which, at + 1))

    def take(self, names):
        jobs, ended = [], []
        for name in names:
            if name == "c":
                jobs += self.first()
            elif name in self.jobs:
                jobs.append(self.jobs.pop(name))
            elif name[1] in self.waiting:
                jobs.append(self.step(name[1]))
            else:
                ended.append(name[1])
        if ended:
            left = [at for at in range(len(self.chains)) if at not in ended and len(self.done.get(at, "..")) > 1]
            jobs += [self.park(at) for at in ended] if left else [self.merge()]
        return jobs

    def park(self, which):
        entries = self.done[which]

        def body(place, refs, outs):
            outs[0][...] = total(*(ref[...] for ref in refs)).astype(BF16)

        def after(outs):
            self.done[which] = outs

        return Job(entries, [struct(*entries[0].shape)], body, after)

    def merge(self):
        groups = [self.done[which] for which in range(len(self.chains))]
        rows = groups[0][0].shape[1]
        widths = [group[0].shape[2] for group in groups]

        def body(place, refs, outs):
            at = col = 0
            for group, width in zip(groups, widths):
                outs[0][:, col : col + width] = total(*(ref[0] for ref in refs[at : at + len(group)])).astype(BF16)
                at, col = at + len(group), col + width

        def after(outs):
            self.cross([outs[0], swap(outs[0], "band", 2)])

        return Job([entry for group in groups for entry in group], [struct(rows, sum(widths))], body, after)

    def cross(self, entries):
        def body(place, refs, outs):
            outs[0][place[3]] = refs[0][...]
            outs[0][1 - place[3]] = refs[1][...]

        def after(outs):
            entries = [outs[0], swap(outs[0], "band", 1)]
            self.jobs["C"] = Job(entries, self.finish[0], self.finish[1], self.finished)

        self.jobs["X"] = Job(entries, [struct(2, *entries[0].shape)], body, after)

    def finished(self, outs):
        self.result = outs


class Exchange:
    def __init__(self, entries, mine, bands):
        self.jobs, self.result = {}, None
        rows, width = entries[0].shape
        half = struct(len(entries), 2, mine, rows // mine // bands, width)

        def split(place, refs, outs):
            far, near = outs
            band_rows = far.shape[3]
            for i, ref in enumerate(refs):
                for q in range(bands):
                    for n in range(mine):
                        at = pl.multiple_of((n * bands + (place[0] ^ q)) * band_rows, 16)
                        (far if q & 2 else near)[i, q & 1, n] = ref[pl.ds(at, band_rows), :]

        self.jobs["s"] = Job(entries, [half, half], split, self.send)

    def send(self, outs):
        far, near = outs
        got = swap(far, "band", 2)
        count, _, mine, band_rows, width = far.shape

        def relay(place, refs, outs):
            for i in range(count):
                outs[0][i, 0] = refs[0][i, 1]
                outs[0][i, 1] = refs[1][i, 1]

        def after(outs):
            entries = [near, got, swap(outs[0], "band", 1)]
            self.jobs["c"] = Job(entries, [struct(4 * mine, band_rows, width)] * count, self.put, self.finished)

        self.jobs["x"] = Job([near, got], [struct(*far.shape)], relay, after)

    def put(self, place, refs, outs):
        near, far, core = refs
        mine = near.shape[2]
        for i, out in enumerate(outs):
            for q, value in enumerate((near[i, 0], core[i, 0], far[i, 0], core[i, 1])):
                out[pl.ds((place[0] ^ q) * mine, mine)] = value

    def finished(self, outs):
        self.result = outs

    def take(self, names):
        return [self.jobs.pop(name) for name in names]


def in_order(place, own, other):
    first = place[1] == 0
    return jnp.where(first, own, other).astype(F32), jnp.where(first, other, own).astype(F32)


def by_rows(place, refs, outs):
    rows = refs[0].shape[1]
    for x in range(2):
        for core, value in enumerate(in_order(place, refs[0][x], refs[1][x])):
            at = (2 * core + x) * rows
            outs[0][at : at + rows, :] = value


def by_columns(segments):
    def body(place, refs, outs):
        rows = refs[0].shape[1]
        for x in range(2):
            col = 0
            for to, low, high in segments:
                half = outs[to].shape[1] // 2
                to_col = col + high - low
                pair = in_order(place, refs[0][x, :, col:to_col], refs[1][x, :, col:to_col])
                for core, value in enumerate(pair):
                    outs[to][x * rows : (x + 1) * rows, core * half + low : core * half + high] = value
                col = to_col

    return body


def reduce_plain(pair, by_core):
    send, keep = pair
    if by_core:
        keep, send = (entry.reshape(8, -1, entry.shape[2]) for entry in (keep, send))
        grad = jnp.concatenate([keep, send], 1)
    else:
        grad = jnp.concatenate([keep, send], 2)
    grad = grad.astype(F32).reshape(-1, grad.shape[2])
    part = lax.psum_scatter(grad, "img", scatter_dimension=0, tiled=True)
    return lax.psum(part.astype(BF16), "band").astype(F32)


def shards(
    tokens, cotangent, grid_side, visible, w_qkv, q_bias, v_bias, w_out, b_out, ln1_gain, ln1_shift,
    ln2_gain, ln2_shift, w_up, b_up, w_down, b_down, scale_attn, scale_mlp,
):
    width = tokens.shape[2]
    ff = w_up.shape[1]
    bands, imgs = lax.axis_size("band"), lax.axis_size("img")
    band, img = lax.axis_index("band"), lax.axis_index("img")
    fast = imgs == 8 and bands == 4
    blocks = 16
    zero = jnp.zeros_like(band)
    place = [band, band & 1, img * 2 + (band >> 1), band >> 1] if fast else [band, zero, zero, zero]
    place = jnp.stack(place).astype(jnp.int32)

    def to_images(entry):
        parts = cut(place, entry, bands)
        return [swap(part, "band", q) if q else part for q, part in enumerate(parts)]

    got_x = to_images(tokens)
    got_c = to_images(cotangent)
    vectors = (q_bias, v_bias, b_out, ln1_gain, ln1_shift, ln2_gain, ln2_shift, b_down, scale_attn, scale_mlp, b_up)
    vec, bias, valid, wv_qkv, wv_out, wv_up = prepare(place, grid_side, visible, vectors, (w_qkv, w_out, w_up), bands)

    s = {}
    exchanges = [[("o", name), ("i", name)] for name in ("s", "x", "c")]
    plan = PLAN if fast else [step for step in PLAN if isinstance(step, str)] + exchanges
    grads, ko = {}, {}
    token = None
    for step in plan:
        if step == "fwd":
            x, normed, q, k, v, p, att, branch, mid, normed2, hidden, slope, token = forward(
                place, got_x, bias, vec, wv_qkv, wv_out, wv_up
            )
        elif step == "down":
            top, gm, *d_pair, s["bd"], token = down(place, got_c, valid, vec, hidden, blocks, token=token)
            if fast:
                finish = ([struct(w_down.shape[0] // imgs, width, dtype=F32)], by_rows)
                sources = [(d_pair[1], swap(d_pair[0], "band", 1))]
                grads["d"] = Gradient(sources, CHAINS["d"], finish)
        elif step == "up":
            dpre, *u_pair, s["bu"], token = up(place, gm, slope, w_down, normed2, blocks, token=token)
            if fast:
                segments = [segment for chain in CHAINS["u"] for segment in chain[2]]
                finish = ([struct(width // imgs, ff, dtype=F32)], by_columns(segments))
                sources = [(u_pair[1], swap(u_pair[0], "band", 1))]
                grads["u"] = Gradient(sources, CHAINS["u"], finish)
        elif step == "outp":
            args = (hidden, w_down, mid, top, valid, vec)
            out_rows, s["m"], token = output_rows(place, *args, token=token)
        elif step == "out1":
            dmid, db, datt, s["o"], token = attention_out(
                place, dpre, w_up, mid, top, vec, branch, w_out, token=token
            )
        elif step == "attn":
            dproj, s["q"], token = attention(place, q, k, v, p, datt, token=token)
        elif step == "qkvo":
            *q_pair, o_send, o_keep, token = qkv(place, normed, dproj, att, db, blocks, token=token)
            if fast:
                ko["q"] = q_pair[1], swap(q_pair[0], "band", 1)
                ko["o"] = o_keep, swap(o_send, "band", 1)
        elif step == "inp":
            in_rows, s["i"], token = input_back(place, dproj, w_qkv, x, dmid, vec, token=token)
        elif step == "pack":
            small = [s[name] for name in ("q", "i", "o", "bu", "bd", "m")]
            if fast:
                shape = struct(imgs, width // blocks, 128)
                grads["ko"].extra, token = call(pack_kernel, [shape], place, *small, limit=2, token=token)
        else:
            if ("o", "s") in step:
                grads["o"] = Exchange([out_rows], tokens.shape[0] // bands, bands)
            if ("i", "s") in step:
                grads["i"] = Exchange([in_rows], tokens.shape[0] // bands, bands)
            if ("ko", "c") in step:
                shapes = [struct(width // imgs, n, dtype=F32) for n in (3 * width, width)]
                segments = [segment for chain in CHAINS["ko"] for segment in chain[2]]
                vectors = [struct(1, n // imgs, dtype=F32) for n in [width] * 7 + [ff] + [width] * 3]
                finish = (shapes + vectors, with_small(segments))
                grads["ko"] = Gradient([ko["q"], ko["o"]], CHAINS["ko"], finish)
            names = list(dict.fromkeys(name for name, _ in step))
            jobs = [job for name in names for job in grads[name].take([what for to, what in step if to == name])]
            token = fold(place, jobs, token)
    (output,), (input_grad,) = grads["o"].result, grads["i"].result
    names = small_rows(*small)
    if fast:
        (grad_w_down,), (grad_w_up,) = grads["d"].result, grads["u"].result
        grad_w_qkv, grad_w_out, *shares = grads["ko"].result
        shares = [entry.reshape(-1) for entry in shares]
    else:
        grad_w_down = reduce_plain(d_pair, True)
        grad_w_up = reduce_plain(u_pair, False)
        grad_w_out = reduce_plain((o_send, o_keep), False)
        grad_w_qkv = reduce_plain(q_pair, False)
        flat = [jnp.concatenate([ref[j] for j in which]) for ref, which in names]
        joined = jnp.concatenate([entry.reshape(imgs, -1) for entry in flat], 1)
        joined = lax.dynamic_index_in_dim(lax.psum(joined, ("img", "band")), img, 0, False)
        shares, at = [], 0
        for entry in flat:
            size = entry.shape[0] // imgs
            shares.append(joined[at : at + size])
            at += size
    (s_qb, s_vb, s_bo, s_g1, s_c1, s_g2, s_c2, s_bu, s_bd, s_sa, s_sm) = shares
    return (
        output, input_grad, grad_w_qkv, s_qb, s_vb, grad_w_out, s_bo, s_g1, s_c1, s_g2, s_c2, grad_w_up, s_bu,
        grad_w_down, s_bd, s_sa, s_sm,
    )


def with_small(segments):
    columns = by_columns(segments)
    at = sum(high - low for _, low, high in segments)

    def body(place, refs, outs):
        columns(place, refs, outs)
        lanes = 128
        values = total(*(ref[x, :16, at : at + lanes] for ref in refs for x in range(2)))
        row = 0
        for out in outs[2:]:
            for start in range(0, out.shape[1], lanes):
                n = min(lanes, out.shape[1] - start)
                out[:, start : start + n] = values[row : row + 1, :n]
                row += 1

    return body


def solution(mesh):
    cut = P("img", "band", None)
    in_specs = (cut, cut, P("img"), P("img", None)) + (P(),) * 15
    row, vec = P("img", None), P("img")
    out_specs = (cut, cut, row, vec, vec, row, vec, vec, vec, vec, vec, row, vec, row, vec, vec, vec)
    return jax.shard_map(shards, mesh=mesh, in_specs=in_specs, out_specs=out_specs, check_vma=False)
```
